32 devices in a mesh: seq: 4 (over y, core), batch: 8 (over z, x).
Axes of the slice: x: 2, y: 2, z: 4, core: 2. Of those that a mesh axis runs over, the one named last changes fastest.
Arguments:
- layer_input: bfloat16 [8, 2048, 1024], P('batch', 'seq'), may hold values from -6 to 6
- lengths: int32 [8], P('batch'), may hold values from 1537 to 2048, as said below
- first_gain: bfloat16 [1024], P('batch'), may hold values from 0.5 to 1.5
- first_shift: bfloat16 [1024], P('batch'), may hold values from -1.25 to 1.25
- joined_weight: bfloat16 [1024, 3072], P('batch'), may hold values from -1 to 1
- joined_bias: bfloat16 [2048], P('batch'), may hold values from -4 to 4
- output_weight: bfloat16 [1024, 1024], P('batch'), may hold values from -0.375 to 0.375
- output_bias: bfloat16 [1024], P('batch'), may hold values from -1.25 to 1.25
- second_gain: bfloat16 [1024], P('batch'), may hold values from 0.5 to 1.5
- second_shift: bfloat16 [1024], P('batch'), may hold values from -1.25 to 1.25
- expand_weight: bfloat16 [1024, 4096], P('batch'), may hold values from -0.1875 to 0.1875
- expand_bias: bfloat16 [4096], P('batch'), may hold values from -1.75 to 1.75
- shrink_weight: bfloat16 [4096, 1024], P('batch'), may hold values from -0.1875 to 0.1875
- shrink_bias: bfloat16 [1024], P('batch'), may hold values from -1.25 to 1.25
- out_grad: bfloat16 [8, 2048, 1024], P('batch', 'seq'), may hold values from -6 to 6
Outputs:
- layer_output: bfloat16 [8, 2048, 1024], P('batch', 'seq')
- input_grad: float32 [8, 2048, 1024], P('batch', 'seq')
- first_gain_grad: float32 [1024], P('batch')
- first_shift_grad: float32 [1024], P('batch')
- joined_weight_grad: float32 [1024, 3072], P('batch')
- joined_bias_grad: float32 [2048], P('batch')
- output_weight_grad: float32 [1024, 1024], P('batch')
- output_bias_grad: float32 [1024], P('batch')
- second_gain_grad: float32 [1024], P('batch')
- second_shift_grad: float32 [1024], P('batch')
- expand_weight_grad: float32 [1024, 4096], P('batch')
- expand_bias_grad: float32 [4096], P('batch')
- shrink_weight_grad: float32 [4096, 1024], P('batch')
- shrink_bias_grad: float32 [1024], P('batch')
The draws below stay inside these ranges and needn't reach their ends.
Inputs may be any that keep to these rules, and one draw needn't show every extreme that they name: `lengths`: among the 1 row of each index of batch, one row drawn from the seed reaches the last index of seq (its length exceeds 2048 - 512); exactly one row in all has length 2048; with more than one row to an index of batch, one row has length 200.
All inputs are finite; a program needn't handle non-finite values.
Results may differ from the reference program's by a relative error of at most 0.018.
Values may be sent and summed in bfloat16 or wider, within the bound.
No kernel may reach another device: no remote copies, remote signals or barrier semaphores. Data moves between devices by JAX's collectives and lax.ppermute only.
A program may use at most 256 MiB of HBM per device.

```python
import math
import jax
import jax.numpy as jnp
from jax import lax

D = 1024
H = 16
HD = 64
FF = 4096
SEQ_LEN = 2048
SHORTEST = 200
ROWS_DEV = 1
ROWS = 8
TOK_DEV = 512


def sink_signs(key):
    key = jax.random.fold_in(key, 901)
    picks = jax.random.randint(key, (D,), 0, 2, dtype=jnp.int32)
    return (2 * picks - 1).astype(jnp.float32)


def normal_directions(key):
    key = jax.random.fold_in(key, 902)
    return jnp.clip(jax.random.normal(key, (H, HD), jnp.float32), -4.0, 4.0)


def draw_layer_input(key, part):
    signs = sink_signs(key)
    key = jax.random.fold_in(key, 21)
    main_key, scale_key = jax.random.split(key)
    values = jnp.clip(jax.random.normal(main_key, (ROWS, SEQ_LEN, D), jnp.float32), -6.0, 6.0)
    sink_count = SEQ_LEN // 32
    scales = jnp.exp(jax.random.uniform(scale_key, (ROWS, SEQ_LEN, 1), jnp.float32, math.log(0.5), math.log(2.0)))
    position = jnp.arange(SEQ_LEN, dtype=jnp.int32)[None, :, None]
    values = jnp.where(position < sink_count, scales * signs[None, None, :], values)
    return values.astype(jnp.bfloat16)


def draw_joined_weight(key, part):
    signs = sink_signs(key)
    directions = normal_directions(key)
    key = jax.random.fold_in(key, 22)
    random_part = jnp.clip(jax.random.normal(key, (D, H, 3, HD), jnp.float32), -6.0, 6.0)
    random_part = random_part / math.sqrt(D)
    planted = 64.0 / (D * HD) * signs[:, None, None] * directions[None, :, :]
    kind_index = jnp.arange(3, dtype=jnp.int32)[None, None, :, None]
    weight = random_part + jnp.where(kind_index == 1, planted[:, :, None, :], 0.0)
    weight = jnp.clip(weight.reshape(D, 3 * D), -1.0, 1.0)
    return weight.astype(jnp.bfloat16)


def draw_joined_bias(key, part):
    directions = normal_directions(key)
    key = jax.random.fold_in(key, 23)
    value_part = 0.3 * jnp.clip(jax.random.normal(key, (H, HD), jnp.float32), -4.0, 4.0)
    bias = jnp.stack([directions, value_part], axis=1).reshape(2 * D)
    return bias.astype(jnp.bfloat16)


def draw_lengths(key, part):
    key = jax.random.fold_in(key, 11)
    length_key, pick_key, long_key, full_key = jax.random.split(key, 4)
    group_count = ROWS // ROWS_DEV
    last_start = SEQ_LEN - TOK_DEV // ROWS_DEV + 1
    row_index = jnp.arange(ROWS, dtype=jnp.int32)
    slot_index = row_index % ROWS_DEV
    group_index = row_index // ROWS_DEV
    drawn_len = jax.random.randint(length_key, (ROWS,), SHORTEST, SEQ_LEN + 1, dtype=jnp.int32)
    picked = jax.random.randint(pick_key, (group_count,), 0, ROWS_DEV, dtype=jnp.int32)
    picked_rows = jnp.repeat(picked, ROWS_DEV)
    long_row = slot_index == picked_rows
    long_len = jax.random.randint(long_key, (ROWS,), last_start, SEQ_LEN + 1, dtype=jnp.int32)
    result = jnp.where(long_row, long_len, drawn_len)
    full_group = jax.random.randint(full_key, (), 0, group_count, dtype=jnp.int32)
    full_row = long_row & (group_index == full_group)
    result = jnp.where(full_row, SEQ_LEN, result)
    if ROWS_DEV > 1:
        short_group = (full_group + 1) % group_count
        short_row = (slot_index == (picked_rows + 1) % ROWS_DEV) & (group_index == short_group)
        result = jnp.where(short_row, SHORTEST, result)
    return result.astype(jnp.int32)


def level_of(own_key, extent, cuts, smallest, high):
    factor_of = 1.0
    for axis_at, blocks in cuts:
        heights = jax.random.uniform(jax.random.fold_in(jax.random.fold_in(own_key, 6), axis_at), (blocks,), jnp.float32, smallest / len(cuts), high / len(cuts))
        factor_of = factor_of * jnp.repeat(jnp.exp(heights), extent[axis_at] // blocks).reshape((-1,) + (1,) * (len(extent) - 1 - axis_at))
    return factor_of


def scatter_about(own_key, shape, width, most, shards=(), kind=jnp.bfloat16):
    values = width * jax.random.normal(own_key, shape, jnp.float32)
    if shards:
        values = values * level_of(own_key, shape, shards, -0.22, 0.18)
    return jnp.clip(values, -most, most).astype(kind)


def setup_inputs(seed: int = 0) -> dict:
    key_list = jax.random.split(jax.random.key(seed), 16)
    layer_input = draw_layer_input(jax.random.fold_in(key_list[15], 71), 0)
    lengths = draw_lengths(jax.random.fold_in(key_list[15], 71), 0)
    first_gain = jnp.clip(1.0 + 0.1 * jax.random.normal(key_list[2], (D,), jnp.float32), 0.5, 1.5).astype(jnp.bfloat16)
    first_shift = scatter_about(key_list[3], (D,), 0.2, 1.25, ((0, 8),))
    joined_weight = draw_joined_weight(jax.random.fold_in(key_list[15], 71), 0)
    joined_bias = draw_joined_bias(jax.random.fold_in(key_list[15], 71), 0)
    output_weight = scatter_about(key_list[6], (D, D), (D // 4) ** -0.5, 0.375, ((0, 8),))
    output_bias = scatter_about(key_list[7], (D,), 0.2, 1.25, ((0, 8),))
    second_gain = jnp.clip(1.0 + 0.1 * jax.random.normal(key_list[8], (D,), jnp.float32), 0.5, 1.5).astype(jnp.bfloat16)
    second_shift = scatter_about(key_list[9], (D,), 0.2, 1.25, ((0, 8),))
    expand_weight = scatter_about(key_list[10], (D, FF), D ** -0.5, 0.1875, ((0, 8),))
    expand_bias = scatter_about(key_list[11], (FF,), 0.3, 1.75, ((0, 8),))
    shrink_weight = scatter_about(key_list[12], (FF, D), (FF // 4) ** -0.5, 0.1875, ((0, 8),))
    shrink_bias = scatter_about(key_list[13], (D,), 0.2, 1.25, ((0, 8),))
    out_grad = scatter_about(key_list[14], (ROWS, SEQ_LEN, D), 1.0, 6.0, ((0, 8), (1, 4)))
    return {"layer_input": layer_input, "lengths": lengths, "first_gain": first_gain, "first_shift": first_shift, "joined_weight": joined_weight, "joined_bias": joined_bias, "output_weight": output_weight, "output_bias": output_bias, "second_gain": second_gain, "second_shift": second_shift, "expand_weight": expand_weight, "expand_bias": expand_bias, "shrink_weight": shrink_weight, "shrink_bias": shrink_bias, "out_grad": out_grad}


HIGHEST = lax.Precision.HIGHEST
EPSILON = 1e-05

@jax.custom_vjp
def low(v):
    return lax.optimization_barrier(v.astype(jnp.bfloat16)).astype(jnp.float32)

@jax.custom_vjp
def low_back(v):
    return v

def low_keep(v):
    return (low(v), None)

def low_pass(kept, grad):
    return (grad,)

def back_keep(v):
    return (v, None)

def back_low(kept, grad):
    return (low(grad),)
low.defvjp(low_keep, low_pass)
low_back.defvjp(back_keep, back_low)

def layer_norm(values, norm_gain, norm_shift):
    mean_val = lax.optimization_barrier(jnp.mean(values, axis=-1, keepdims=True))
    centered = values - mean_val
    variance = lax.optimization_barrier(jnp.mean(centered * centered, axis=-1, keepdims=True))
    return centered * lax.rsqrt(variance + EPSILON) * norm_gain + norm_shift

def attention(queries, key_rows, value_rows, lengths):
    group_rows, seq_len, head_count, head_size = queries.shape
    block_size = min(512, seq_len)
    block_count = seq_len // block_size
    float_type = queries.dtype
    slopes = (2.0 ** (-8.0 * (jnp.arange(head_count) + 1) / head_count)).astype(float_type)
    key_pos = jnp.arange(seq_len, dtype=jnp.int32)
    key_live = key_pos[None, :] < lengths[:, None]

    def one_block(block_item):
        query_block, block_start = block_item
        query_pos = block_start + jnp.arange(block_size, dtype=jnp.int32)
        scores = jnp.einsum('gqhd,gkhd->ghqk', query_block, key_rows, precision=HIGHEST) * 0.125
        offset = (key_pos[None, :] - query_pos[:, None]).astype(float_type)
        scores = scores + slopes[None, :, None, None] * offset[None, None]
        live_mask = (key_pos[None, :] <= query_pos[:, None])[None, None] & key_live[:, None, None, :]
        scores = low_back(jnp.where(live_mask, scores, -1e+30))
        row_max = lax.optimization_barrier(jnp.max(scores, axis=-1, keepdims=True))
        exp_scores = jnp.exp(scores - row_max)
        attn_probs = exp_scores / lax.optimization_barrier(jnp.sum(exp_scores, axis=-1, keepdims=True))
        return jnp.einsum('ghqk,gkhd->gqhd', low(attn_probs), value_rows, precision=HIGHEST)
    query_blocks = jnp.moveaxis(queries.reshape(group_rows, block_count, block_size, head_count, head_size), 1, 0)
    block_starts = jnp.arange(block_count, dtype=jnp.int32) * block_size
    block_outs = lax.map(jax.checkpoint(one_block), (query_blocks, block_starts))
    return jnp.moveaxis(block_outs, 0, 1).reshape(group_rows, seq_len, head_count * head_size)

def forward(layer_in, lengths, first_gain, first_shift, joined_weight, joined_bias, output_weight, output_bias, second_gain, second_shift, expand_weight, expand_bias, shrink_weight, shrink_bias):
    group_rows, seq_len, feat_count = layer_in.shape
    normed = low(layer_norm(layer_in, first_gain, first_shift))
    joined = jnp.dot(normed, joined_weight, precision=HIGHEST).reshape(group_rows, seq_len, H, 3, HD)
    bias_grid = joined_bias.reshape(H, 2, HD)
    queries = low(low_back(joined[:, :, :, 0] + bias_grid[:, 0]))
    key_rows = low(low_back(joined[:, :, :, 1]))
    value_rows = low(low_back(joined[:, :, :, 2] + bias_grid[:, 1]))
    mixed = low(low_back(attention(queries, key_rows, value_rows, lengths)))
    branch = low_back(jnp.dot(mixed, output_weight, precision=HIGHEST) + output_bias)
    resid = layer_in + branch
    second = low(layer_norm(resid, second_gain, second_shift))
    pre_act = low_back(jnp.dot(second, expand_weight, precision=HIGHEST) + expand_bias)
    activ = low(jax.nn.gelu(pre_act, approximate=True))
    return resid + jnp.dot(activ, shrink_weight, precision=HIGHEST) + shrink_bias

def reference(layer_input, lengths, first_gain, first_shift, joined_weight, joined_bias, output_weight, output_bias, second_gain, second_shift, expand_weight, expand_bias, shrink_weight, shrink_bias, out_grad):
    weights = tuple((param.astype(jnp.float32) for param in (first_gain, first_shift, joined_weight, joined_bias, output_weight, output_bias, second_gain, second_shift, expand_weight, expand_bias, shrink_weight, shrink_bias)))
    row_total = layer_input.shape[0]
    group_rows = math.gcd(row_total, max(1, 4096 // SEQ_LEN))
    group_count = row_total // group_rows
    inputs = layer_input.astype(jnp.float32).reshape(group_count, group_rows, SEQ_LEN, D)
    cotans = out_grad.astype(jnp.float32).reshape(group_count, group_rows, SEQ_LEN, D)
    group_lens = lengths.astype(jnp.int32).reshape(group_count, group_rows)

    def scan_step(totals, scan_item):
        layer_in, cotan, lens_group = scan_item

        def run_layer(values, *params):
            return forward(values, lens_group, *params)
        outputs, pullback = jax.vjp(run_layer, layer_in, *weights)
        grads = pullback(cotan)
        totals = tuple((left + right for left, right in zip(totals, grads[1:])))
        return (totals, (outputs, grads[0]))
    zero_grads = tuple((jnp.zeros_like(param) for param in weights))
    totals, (outputs, input_grads) = lax.scan(scan_step, zero_grads, (inputs, cotans, group_lens))
    return (outputs.reshape(row_total, SEQ_LEN, D).astype(jnp.bfloat16), input_grads.reshape(row_total, SEQ_LEN, D), totals[0], totals[1], totals[2], totals[3], totals[4], totals[5], totals[6], totals[7], totals[8], totals[9], totals[10], totals[11])
```

```python
import functools

import jax
import jax.numpy as jnp
from jax import lax
from jax.experimental import pallas as pl
from jax.experimental.pallas import tpu as pltpu
from jax.sharding import PartitionSpec as P

H = 16
HD = 64
EPSILON = 1e-05
F32 = jnp.float32
BF = jnp.bfloat16
NT = (((1,), (1,)), ((), ()))
NN = (((1,), (0,)), ((), ()))
TN = (((0,), (0,)), ((), ()))
MIB = 2**20


def dg(left, right, dims):
    return lax.dot_general(left, right, dims, preferred_element_type=F32)


def params(limit=56):
    return pltpu.CompilerParams(vmem_limit_bytes=limit * MIB)


def cost(flops, moved, exps=0):
    return pl.CostEstimate(flops=flops, bytes_accessed=moved, transcendentals=exps)


def norm_parts(values):
    mean = jnp.mean(values, axis=-1, keepdims=True)
    centered = values - mean
    scale = lax.rsqrt(jnp.mean(centered * centered, axis=-1, keepdims=True) + EPSILON)
    return centered * scale, scale


def norm_back(grad, unit, scale, gain):
    scaled = grad * gain
    return scale * (
        scaled
        - jnp.mean(scaled, axis=-1, keepdims=True)
        - unit * jnp.mean(scaled * unit, axis=-1, keepdims=True)
    )


def pairs(size, bit):
    return [(i, i ^ bit) for i in range(size)]


def bits_low_last(size):
    bits = []
    bit = 2
    while bit < size:
        bits.append(bit)
        bit *= 2
    if size > 1:
        bits.append(1)
    return bits


def place_of(rel, size):
    place = 0
    for at, bit in enumerate(bits_low_last(size)):
        place |= (1 << at) if rel & bit else 0
    return place


def place_table(me, size):
    index = jnp.arange(size, dtype=jnp.int32) ^ me
    place = jnp.zeros_like(index)
    for at, bit in enumerate(bits_low_last(size)):
        place = place | jnp.where(index & bit, 1 << at, 0)
    return place


def gather_stack(block, axis, size):
    out = block[None]
    for bit in bits_low_last(size):
        out = jnp.concatenate([out, lax.ppermute(out, axis, pairs(size, bit))], 0)
    return out


def add16(left, right):
    return (left.astype(F32) + right.astype(F32)).astype(BF)


def scatter_stack(stack, axis, size):
    for bit in bits_low_last(size)[::-1]:
        half = stack.shape[0] // 2
        stack = add16(stack[:half], lax.ppermute(stack[half:], axis, pairs(size, bit)))
    return stack[0]


def gather_rel(block, axis, size):
    out = {0: block}
    for bit in bits_low_last(size):
        for rel in list(out):
            out[rel | bit] = lax.ppermute(out[rel], axis, pairs(size, bit))
    return out


def scatter_rel(parts, axis, size, last=True):
    parts = dict(parts)
    order = bits_low_last(size)[::-1]
    for bit in order:
        for rel in sorted(parts, reverse=True):
            if rel & bit:
                other = lax.ppermute(parts.pop(rel), axis, pairs(size, bit))
                if bit == order[-1] and not last:
                    return parts[0], other
                parts[rel ^ bit] = add16(parts[rel ^ bit], other)
    return parts[0]


def first_kernel(nt, nb, rows, info, xa, xb, weight, vecs, jbias, *rest):
    normed, joined, full = rest[-3:]
    step = pl.program_id(0)

    @pl.when(step == 0)
    def _():
        for k in range(nb):
            full[k * rows : (k + 1) * rows] = weight[info[2 + k], :rows]

    gain = vecs[0:1]
    shift = vecs[1:2]

    def work(x):
        unit, _ = norm_parts(x[...].astype(F32))
        value = (unit * gain + shift).astype(BF)
        normed[...] = value
        joined[...] = (dg(value, full[...], NN) + jbias[...]).astype(BF)

    @pl.when(step < nt)
    def _():
        work(xa)

    @pl.when(step >= nt)
    def _():
        work(xb)


def first_call(rel, xa, xb, info, weight, vecs, jbias, before, ns):
    tok, dim = xa.shape
    nb, padded, cols = weight.shape
    rows = dim // nb
    tile = min(256, tok)
    nt = tok // tile
    whole = lambda shape: pl.BlockSpec(shape, lambda i, info: (0,) * len(shape), pipeline_mode=pl.Buffered(1))
    place = lambda i, info: ((info[0] ^ (rel + lax.div(i, nt))) * nt + lax.rem(i, nt), 0)
    outs = [jax.ShapeDtypeStruct((ns * tok, dim), BF), jax.ShapeDtypeStruct((ns * tok, cols), BF)]
    extra = [] if before is None else list(before)
    return pl.pallas_call(
        functools.partial(first_kernel, nt, nb, rows),
        grid_spec=pltpu.PrefetchScalarGridSpec(
            num_scalar_prefetch=1,
            grid=(2 * nt,),
            in_specs=[
                pl.BlockSpec((tile, dim), lambda i, info: (jnp.minimum(i, nt - 1), 0)),
                pl.BlockSpec((tile, dim), lambda i, info: (jnp.maximum(i - nt, 0), 0)),
                whole(weight.shape),
                whole(vecs.shape),
                whole(jbias.shape),
            ]
            + [pl.BlockSpec(memory_space=pl.ANY)] * len(extra),
            out_specs=[pl.BlockSpec((tile, dim), place), pl.BlockSpec((tile, cols), place)],
            scratch_shapes=[pltpu.VMEM((dim, cols), BF)],
        ),
        out_shape=outs,
        input_output_aliases={6: 0, 7: 1} if extra else {},
        compiler_params=params(40),
        cost_estimate=cost(4 * tok * dim * cols, 4 * tok * (2 * dim + cols)),
        name="first",
    )(info, xa, xb, weight, vecs, jbias, *extra)


def three(value):
    high = value.astype(BF)
    rest = value - high.astype(F32)
    mid = rest.astype(BF)
    return high, mid, (rest - mid.astype(F32)).astype(BF)


def spread(lane, base, columns):
    for at, column in columns:
        base = jnp.where(lane == at, column.astype(F32), base)
    return base.astype(BF)


def key_extra(count, slope, length):
    lane = lax.broadcasted_iota(jnp.int32, (count, HD), 1)
    pos = lax.broadcasted_iota(jnp.int32, (count, HD), 0)
    high, mid, low = three(slope * pos.astype(F32))
    dead = jnp.where(pos < length, 0.0, -1e30)
    return spread(lane, jnp.where(lane < 7, 1.0, 0.0), [(0, high), (1, mid), (2, low), (3, dead)])


def attend_kernel(count, size, info, slopes, joined, mixed, sums, keys):
    pair = pl.program_id(0)
    lane = lax.broadcasted_iota(jnp.int32, (size, HD), 1)
    ones = jnp.where(lane < 4, 1.0, 0.0).astype(BF)
    for hh in range(2):
        base = 3 * HD * hh
        extra = key_extra(count, slopes[2 * pair + hh], info[1])
        keys[hh] = jnp.concatenate([joined[:, base + HD : base + 2 * HD], extra], 1)
    query_at = lax.broadcasted_iota(jnp.int32, (size, size), 0)
    key_at = lax.broadcasted_iota(jnp.int32, (size, size), 1)
    for block in range(count // size):
        low = block * size
        high = low + size
        outs = []
        logs = []
        for hh in range(2):
            base = 3 * HD * hh
            query = (joined[low:high, base : base + HD].astype(F32) * 0.125).astype(BF)
            query = jnp.concatenate([query, ones], 1)
            near = jnp.where(key_at <= query_at, dg(query, keys[hh, low:high], NT), -1e30)
            top = jnp.max(near, axis=1, keepdims=True)
            if block:
                far = dg(query, keys[hh, 0:low], NT)
                top = jnp.maximum(top, jnp.max(far, axis=1, keepdims=True))
            near = jnp.exp(near - top)
            total = jnp.sum(near, axis=1, keepdims=True)
            acc = dg(near.astype(BF), joined[low:high, base + 2 * HD : base + 3 * HD], NN)
            if block:
                far = jnp.exp(far - top)
                total += jnp.sum(far, axis=1, keepdims=True)
                acc += dg(far.astype(BF), joined[0:low, base + 2 * HD : base + 3 * HD], NN)
            outs.append(acc / total)
            logs.append(jnp.broadcast_to(top + jnp.log(total), (size, HD)))
        mixed[low:high] = jnp.concatenate(outs, 1).astype(BF)
        sums[low:high] = jnp.concatenate(logs, 1)


def attend(joined, info, slopes):
    count, width = joined.shape
    groups = width // (6 * HD)
    smem = pl.BlockSpec(memory_space=pltpu.SMEM)
    area = count * count * groups
    return pl.pallas_call(
        functools.partial(attend_kernel, count, min(512, count)),
        grid=(groups,),
        in_specs=[smem, smem, pl.BlockSpec((count, 6 * HD), lambda p: (0, p))],
        out_specs=[pl.BlockSpec((count, 2 * HD), lambda p: (0, p))] * 2,
        out_shape=[
            jax.ShapeDtypeStruct((count, groups * 2 * HD), BF),
            jax.ShapeDtypeStruct((count, groups * 2 * HD), F32),
        ],
        scratch_shapes=[pltpu.VMEM((2, count, 2 * HD), BF)],
        compiler_params=params(),
        cost_estimate=cost(area * 1024, 4 * joined.size, area),
        name="attend",
    )(info, slopes, joined)


def attend_back_kernel(
    count, size, info, slopes, joined, grad, mixed, sums, out, keys, queries, values, grads, query_grad
):
    pair = pl.program_id(0)
    lane = lax.broadcasted_iota(jnp.int32, (count, HD), 1)
    for hh in range(2):
        base = 3 * HD * hh
        half = slice(hh * HD, (hh + 1) * HD)
        extra = key_extra(count, slopes[2 * pair + hh], info[1])
        keys[hh] = jnp.concatenate([joined[:, base + HD : base + 2 * HD], extra], 1)
        query = (joined[:, base : base + HD].astype(F32) * 0.125).astype(BF)
        high, mid, low = three(-sums[:, half])
        extra = spread(lane, jnp.where(lane < 4, 1.0, 0.0), [(4, high), (5, mid), (6, low)])
        queries[hh] = jnp.concatenate([query, extra], 1)
        part = grad[:, half]
        inner = jnp.sum(part.astype(F32) * mixed[:, half].astype(F32), axis=1, keepdims=True)
        high, mid, low = three(jnp.broadcast_to(-inner, (count, HD)))
        extra = spread(lane, jnp.zeros((count, HD), F32), [(0, high), (1, mid), (2, low)])
        grads[hh] = jnp.concatenate([part, extra], 1)
        ones = jnp.where(lane < 3, 1.0, 0.0).astype(BF)
        values[hh] = jnp.concatenate([joined[:, base + 2 * HD : base + 3 * HD], ones], 1)
    key_at = lax.broadcasted_iota(jnp.int32, (size, size), 0)
    query_at = lax.broadcasted_iota(jnp.int32, (size, size), 1)
    blocks = count // size
    for j in range(blocks):
        ks = slice(j * size, (j + 1) * size)
        pieces = []
        for hh in range(2):
            key_sum = None
            for i in range(j, blocks):
                qs = slice(i * size, (i + 1) * size)
                probs = jnp.exp(dg(keys[hh, ks], queries[hh, qs], NT))
                if i == j:
                    probs = jnp.where(key_at <= query_at, probs, 0.0)
                slope = (probs * dg(values[hh, ks], grads[hh, qs], NT)).astype(BF)
                value_part = dg(probs.astype(BF), grads[hh, qs], NN)
                key_part = dg(slope, queries[hh, qs], NN)
                query_part = dg(keys[hh, ks], slope, TN)
                value_sum = value_part if key_sum is None else value_sum + value_part
                key_sum = key_part if key_sum is None else key_sum + key_part
                query_grad[hh, :, qs] = query_part if j == 0 else query_grad[hh, :, qs] + query_part
            pieces += [jnp.zeros((size, HD), F32), key_sum[:, :HD], value_sum[:, :HD]]
        out[ks] = jnp.concatenate(pieces, 1).astype(BF)
    for hh in range(2):
        base = 3 * HD * hh
        out[:, base : base + HD] = (query_grad[hh].T[:, :HD] * 0.125).astype(BF)


def attend_back(joined, grad, mixed, sums, info, slopes):
    count, width = joined.shape
    groups = width // (6 * HD)
    smem = pl.BlockSpec(memory_space=pltpu.SMEM)
    wide = pl.BlockSpec((count, 6 * HD), lambda p: (0, p))
    narrow = pl.BlockSpec((count, 2 * HD), lambda p: (0, p))
    area = count * count * groups
    return pl.pallas_call(
        functools.partial(attend_back_kernel, count, min(512, count)),
        grid=(groups,),
        in_specs=[smem, smem, wide, narrow, narrow, narrow],
        out_specs=wide,
        out_shape=jax.ShapeDtypeStruct((count, width), BF),
        scratch_shapes=[pltpu.VMEM((2, count, 2 * HD), BF)] * 4 + [pltpu.VMEM((2, 2 * HD, count), F32)],
        compiler_params=params(),
        cost_estimate=cost(area * 2560, 8 * joined.size, area),
        name="attend_back",
    )(info, slopes, joined, grad, mixed, sums)


def middle_kernel(ns, nb, rows, cw, info, x, vecs, *refs):
    mixed = refs[:ns]
    weights = refs[ns : 2 * ns]
    merged, resid, second, full = refs[2 * ns :]

    @pl.when(pl.program_id(0) == 0)
    def _():
        for rel in range(ns):
            col = pl.ds(pl.multiple_of((info[0] ^ rel) * cw, cw), cw)
            for k in range(nb):
                full[k * rows : (k + 1) * rows, col] = weights[rel][info[2 + k]]

    for rel in range(ns):
        col = pl.ds(pl.multiple_of((info[0] ^ rel) * cw, cw), cw)
        merged[:, col] = mixed[rel][...]
    value = x[...].astype(F32) + dg(merged[...], full[...], NN) + vecs[4:5]
    resid[...] = value
    unit, _ = norm_parts(value)
    second[...] = (unit * vecs[5:6] + vecs[6:7]).astype(BF)


def middle_call(info, x, vecs, mixed, weights):
    tok, dim = x.shape
    ns = len(mixed)
    nb, rows, cw = weights[0].shape
    tile = min(256, tok)
    whole = lambda shape: pl.BlockSpec(shape, lambda i, info: (0,) * len(shape), pipeline_mode=pl.Buffered(1))
    part = lambda width: pl.BlockSpec((tile, width), lambda i, info: (i, 0))
    return pl.pallas_call(
        functools.partial(middle_kernel, ns, nb, rows, cw),
        grid_spec=pltpu.PrefetchScalarGridSpec(
            num_scalar_prefetch=1,
            grid=(tok // tile,),
            in_specs=[part(dim), whole(vecs.shape)] + [part(cw)] * ns + [whole((nb, rows, cw))] * ns,
            out_specs=[part(dim), part(dim), part(dim), whole((dim, dim))],
        ),
        out_shape=[
            jax.ShapeDtypeStruct((tok, dim), BF),
            jax.ShapeDtypeStruct((tok, dim), F32),
            jax.ShapeDtypeStruct((tok, dim), BF),
            jax.ShapeDtypeStruct((dim, dim), BF),
        ],
        compiler_params=params(40),
        cost_estimate=cost(2 * tok * dim * dim, 12 * tok * dim + 4 * dim * dim),
        name="middle",
    )(info, x, vecs, *mixed, *weights)


def feed_kernel(nt, nb, rows, units, info, sa, sb, ca, cb, expand, shrink, ebias, activ, pre_grad, out, back, bgrad, wide, tall):
    step = pl.program_id(0)

    @pl.when(step == 0)
    def _():
        for k in range(nb):
            wide[k * rows : (k + 1) * rows] = expand[info[2 + k]]
            tall[k * units : (k + 1) * units] = shrink[info[2 + k]]
        bgrad[...] = jnp.zeros_like(bgrad)

    def work(second, cot):
        pre = dg(second[...], wide[...], NN) + ebias[...]
        square = pre * pre
        bend = jnp.tanh(0.7978845608028654 * pre * (1.0 + 0.044715 * square))
        half = 0.5 + 0.5 * bend
        act = (pre * half).astype(BF)
        activ[...] = act
        out[0] = dg(act, tall[...], NN).astype(BF)
        steep = half + pre * (0.5 - 0.5 * bend * bend) * (0.7978845608028654 + 0.10703222440890037 * square)
        grad = (dg(cot[...], tall[...], NT) * steep).astype(BF)
        pre_grad[...] = grad
        bgrad[...] += jnp.sum(grad.astype(F32), axis=0, keepdims=True)
        back[0] = dg(grad, wide[...], NT).astype(BF)

    @pl.when(step < nt)
    def _():
        work(sa, ca)

    @pl.when(step >= nt)
    def _():
        work(sb, cb)


def feed_call(info, sa, sb, ca, cb, expand, shrink, ebias):
    tok, dim = sa.shape
    nb, rows, ff = expand.shape
    units = shrink.shape[1]
    tile = min(256, tok)
    nt = tok // tile
    whole = lambda shape: pl.BlockSpec(shape, lambda i, info: (0,) * len(shape), pipeline_mode=pl.Buffered(1))
    left = pl.BlockSpec((tile, dim), lambda i, info: (jnp.minimum(i, nt - 1), 0))
    right = pl.BlockSpec((tile, dim), lambda i, info: (jnp.maximum(i - nt, 0), 0))
    flat = pl.BlockSpec((tile, ff), lambda i, info: (i, 0))
    part = pl.BlockSpec((1, tile, dim), lambda i, info: (lax.div(i, nt), lax.rem(i, nt), 0))

    return pl.pallas_call(
        functools.partial(feed_kernel, nt, nb, rows, units),
        grid_spec=pltpu.PrefetchScalarGridSpec(
            num_scalar_prefetch=1,
            grid=(2 * nt,),
            in_specs=[left, right, left, right, whole(expand.shape), whole(shrink.shape), whole(ebias.shape)],
            out_specs=[flat, flat, part, part, pl.BlockSpec((1, ff), lambda i, info: (0, 0))],
            scratch_shapes=[pltpu.VMEM((dim, ff), BF), pltpu.VMEM((ff, dim), BF)],
        ),
        out_shape=[
            jax.ShapeDtypeStruct((2 * tok, ff), BF),
            jax.ShapeDtypeStruct((2 * tok, ff), BF),
            jax.ShapeDtypeStruct((2, tok, dim), BF),
            jax.ShapeDtypeStruct((2, tok, dim), BF),
            jax.ShapeDtypeStruct((1, ff), F32),
        ],
        compiler_params=params(),
        cost_estimate=cost(16 * tok * dim * ff, 16 * tok * dim + 8 * dim * ff, 2 * tok * ff),
        name="feed",
    )(info, sa, sb, ca, cb, expand, shrink, ebias)


def wgrad_kernel(count, nb, rows, tile, split, info, *refs):
    lefts = refs[:count]
    rights = refs[count : 2 * count]
    out = refs[2 * count]
    total = dg(lefts[0][...], rights[0][...], TN)
    for at in range(1, count):
        total += dg(lefts[at][...], rights[at][...], TN)
    first = pl.program_id(0) * (tile // rows)
    if split == 1:
        total = total.astype(BF)
        for k in range(tile // rows):
            out[info[2 + first + k]] = total[k * rows : (k + 1) * rows]
    else:
        held = refs[2 * count + 1]
        held[...] = total
        cw = total.shape[1] // split
        for rel in range(split):
            col = pl.ds(pl.multiple_of((info[0] ^ rel) * cw, cw), cw)
            value = held[:, col].astype(BF)
            for k in range(tile // rows):
                out[rel, info[2 + first + k]] = value[k * rows : (k + 1) * rows]


def wgrad_call(info, lefts, rights, nb, split=1):
    dim = lefts[0].shape[1]
    width = rights[0].shape[1]
    rows = dim // nb
    tile = 256
    tok = sum(a.shape[0] for a in lefts)
    shape = (nb, rows, width) if split == 1 else (split, nb, rows, width // split)
    whole = lambda shape: pl.BlockSpec(shape, lambda i, info: (0,) * len(shape), pipeline_mode=pl.Buffered(1))
    return pl.pallas_call(
        functools.partial(wgrad_kernel, len(lefts), nb, rows, tile, split),
        grid_spec=pltpu.PrefetchScalarGridSpec(
            num_scalar_prefetch=1,
            grid=(dim // tile,),
            in_specs=[pl.BlockSpec((a.shape[0], tile), lambda i, info: (0, i)) for a in lefts]
            + [whole(b.shape) for b in rights],
            out_specs=pl.BlockSpec(shape, lambda i, info: (0,) * len(shape)),
            scratch_shapes=[] if split == 1 else [pltpu.VMEM((tile, width), F32)],
        ),
        out_shape=jax.ShapeDtypeStruct(shape, BF),
        compiler_params=params(),
        cost_estimate=cost(2 * tok * dim * width, 2 * tok * (dim + width) + 2 * dim * width),
        name="weight_grad",
    )(info, *lefts, *rights)


def turn_kernel(ns, cw, info, ga, gb, resid, cot, vecs, full, resid_grad, branch, mixed_grad, sums, held):
    @pl.when(pl.program_id(0) == 0)
    def _():
        sums[...] = jnp.zeros_like(sums)

    grad = ga[...].astype(F32) + gb[...].astype(F32)
    unit, scale = norm_parts(resid[...])
    outer = cot[...].astype(F32)
    value = outer + norm_back(grad, unit, scale, vecs[5:6])
    resid_grad[...] = value
    low = value.astype(BF)
    branch[...] = low
    held[...] = dg(low, full[...], NT).astype(BF)
    for rel in range(ns):
        col = pl.ds(pl.multiple_of((info[0] ^ rel) * cw, cw), cw)
        mixed_grad[rel] = held[:, col]
    for at, term in enumerate((grad * unit, grad, low.astype(F32), outer)):
        sums[at : at + 1] += jnp.sum(term, axis=0, keepdims=True)


def turn_call(info, ga, gb, resid, cot, vecs, full, ns):
    tok, dim = resid.shape
    cw = dim // ns
    tile = min(256, tok)
    whole = lambda shape: pl.BlockSpec(shape, lambda i, info: (0,) * len(shape), pipeline_mode=pl.Buffered(1))
    part = pl.BlockSpec((tile, dim), lambda i, info: (i, 0))
    return pl.pallas_call(
        functools.partial(turn_kernel, ns, cw),
        grid_spec=pltpu.PrefetchScalarGridSpec(
            num_scalar_prefetch=1,
            grid=(tok // tile,),
            in_specs=[part, part, part, part, whole(vecs.shape), whole(full.shape)],
            out_specs=[
                part,
                part,
                pl.BlockSpec((ns, tile, cw), lambda i, info: (0, i, 0)),
                pl.BlockSpec((8, dim), lambda i, info: (0, 0)),
            ],
            scratch_shapes=[pltpu.VMEM((tile, dim), BF)],
        ),
        out_shape=[
            jax.ShapeDtypeStruct((tok, dim), F32),
            jax.ShapeDtypeStruct((tok, dim), BF),
            jax.ShapeDtypeStruct((ns, tok, cw), BF),
            jax.ShapeDtypeStruct((8, dim), F32),
        ],
        compiler_params=params(40),
        cost_estimate=cost(2 * tok * dim * dim, 16 * tok * dim + 2 * dim * dim),
        name="turn",
    )(info, ga, gb, resid, cot, vecs, full)


def last_kernel(nb, rows, tok_tiles, info, joined_grad, normed, weight, out, sums, sides, full):
    @pl.when(pl.program_id(0) == 0)
    def _():
        for k in range(nb):
            full[k * rows : (k + 1) * rows] = weight[info[2 + k], :rows]
        sums[...] = jnp.zeros_like(sums)
        sides[...] = jnp.zeros_like(sides)

    grad = dg(joined_grad[...], full[...], NT)
    out[0] = grad.astype(BF)
    sums[0:1] += jnp.sum(grad * normed[...].astype(F32), axis=0, keepdims=True)
    sums[1:2] += jnp.sum(grad, axis=0, keepdims=True)
    sides[...] += jnp.sum(joined_grad[...].astype(F32), axis=0, keepdims=True)


def last_call(info, joined_grad, normed, weight, ns):
    count, cols = joined_grad.shape
    dim = normed.shape[1]
    nb = weight.shape[0]
    rows = dim // nb
    tok = count // ns
    tile = min(256, tok)
    nt = tok // tile
    whole = lambda shape: pl.BlockSpec(shape, lambda i, info: (0,) * len(shape), pipeline_mode=pl.Buffered(1))
    return pl.pallas_call(
        functools.partial(last_kernel, nb, rows, nt),
        grid_spec=pltpu.PrefetchScalarGridSpec(
            num_scalar_prefetch=1,
            grid=(ns * nt,),
            in_specs=[
                pl.BlockSpec((tile, cols), lambda i, info: (i, 0)),
                pl.BlockSpec((tile, dim), lambda i, info: (i, 0)),
                whole(weight.shape),
            ],
            out_specs=[
                pl.BlockSpec((1, tile, dim), lambda i, info: (info[0] ^ lax.div(i, nt), lax.rem(i, nt), 0)),
                pl.BlockSpec((8, dim), lambda i, info: (0, 0)),
                pl.BlockSpec((1, cols), lambda i, info: (0, 0)),
            ],
            scratch_shapes=[pltpu.VMEM((dim, cols), BF)],
        ),
        out_shape=[
            jax.ShapeDtypeStruct((ns, tok, dim), BF),
            jax.ShapeDtypeStruct((8, dim), F32),
            jax.ShapeDtypeStruct((1, cols), F32),
        ],
        compiler_params=params(40),
        cost_estimate=cost(2 * count * dim * cols, 2 * count * (2 * dim + cols)),
        name="last",
    )(info, joined_grad, normed, weight)


def end_kernel(ga, gb, x, resid_grad, vecs, out):
    grad = ga[...].astype(F32) + gb[...].astype(F32)
    unit, scale = norm_parts(x[...].astype(F32))
    out[...] = resid_grad[...] + norm_back(grad, unit, scale, vecs[0:1])


def end_call(ga, gb, x, resid_grad, vecs):
    tok, dim = x.shape
    tile = min(128, tok)
    part = pl.BlockSpec((tile, dim), lambda i: (i, 0))
    return pl.pallas_call(
        end_kernel,
        grid=(tok // tile,),
        in_specs=[part, part, part, part, pl.BlockSpec(vecs.shape, lambda i: (0, 0))],
        out_specs=part,
        out_shape=jax.ShapeDtypeStruct((tok, dim), F32),
        compiler_params=params(40),
        cost_estimate=cost(20 * tok * dim, 14 * tok * dim),
        name="end",
    )(ga, gb, x, resid_grad, vecs)


def body(
    layer_input,
    lengths,
    first_gain,
    first_shift,
    joined_weight,
    joined_bias,
    output_weight,
    output_bias,
    second_gain,
    second_shift,
    expand_weight,
    expand_bias,
    shrink_weight,
    shrink_bias,
    out_grad,
):
    ns = lax.axis_size("seq")
    nb = lax.axis_size("batch")
    si = lax.axis_index("seq")
    bi = lax.axis_index("batch")
    tok = layer_input.shape[1]
    dim = layer_input.shape[2]
    count = ns * tok
    heads = H // ns
    cols = 3 * HD * heads
    cw = HD * heads
    rows = dim // nb
    ff = expand_weight.shape[1] // ns
    units = ff // nb
    x = layer_input[0]
    cot = out_grad[0]
    info = jnp.concatenate([jnp.stack([si, lengths[0]]), place_table(bi, nb)]).astype(jnp.int32)
    head_ids = si * heads + jnp.arange(heads, dtype=jnp.int32) + 1
    slopes = 2.0 ** (-8.0 * head_ids.astype(F32) / H)

    smalls = jnp.concatenate(
        [first_gain, first_shift, joined_bias, output_bias, second_gain, second_shift, expand_bias, shrink_bias]
    )
    wide = -(-smalls.shape[0] // cols)
    pad = -(-wide // 16) * 16
    small_rows = jnp.pad(smalls, (0, pad * cols - smalls.shape[0])).reshape(pad, cols)
    joined_part = lax.dynamic_slice(joined_weight, (0, si * cols), (rows, cols))
    group_one = gather_stack(jnp.concatenate([joined_part, small_rows], 0), "batch", nb)
    xs = gather_rel(x, "seq", ns)
    cots = gather_rel(cot, "seq", ns)
    expand_part = lax.dynamic_slice(
        expand_weight.reshape(rows, nb, ns, units), (0, 0, si, 0), (rows, nb, 1, units)
    ).reshape(rows, ff)
    shrink_part = lax.dynamic_slice(shrink_weight, (si * units, 0), (units, dim))
    outw_part = lax.dynamic_slice(output_weight, (0, si * cw), (rows, cw))
    expand_all = gather_stack(expand_part, "batch", nb)
    shrink_all = gather_stack(shrink_part, "batch", nb)
    outw_all = gather_rel(gather_stack(outw_part, "batch", nb), "seq", ns)

    places = place_table(bi, nb)
    flat = group_one[:, rows : rows + wide].reshape(nb, wide * cols)[:, : smalls.shape[0]]
    flat = jnp.take(flat, places, axis=0).astype(F32)
    vecs = flat.reshape(nb, 12, rows).transpose(1, 0, 2).reshape(12, dim)
    low = vecs[2:4].reshape(2, nb, rows).transpose(1, 0, 2).reshape(2 * dim)
    low = lax.dynamic_slice(low, (si * 2 * cw,), (2 * cw,)).reshape(heads, 2, HD)
    jbias = jnp.stack([low[:, 0], jnp.zeros_like(low[:, 0]), low[:, 1]], 1).reshape(1, cols)
    ebias = vecs[7:11].reshape(4, nb, rows).transpose(1, 0, 2).reshape(nb, ns, units)
    ebias = lax.dynamic_slice(ebias, (0, si, 0), (nb, 1, units)).reshape(1, ff)
    held = None
    for rel in range(0, ns, 2):
        held = first_call(rel, xs[rel], xs[rel + 1], info, group_one, vecs, jbias, held, ns)
    normed, joined = held
    mixed, log_sums = attend(joined, info, slopes)

    def to_tokens(values):
        out = []
        for rel in range(ns):
            block = lax.dynamic_slice(values, ((si ^ rel) * tok, 0), (tok, values.shape[1]))
            out.append(lax.ppermute(block, "seq", pairs(ns, rel)) if rel else block)
        return out

    merged, resid, second, outw_full = middle_call(
        info, x, vecs, to_tokens(mixed), [outw_all[rel] for rel in range(ns)]
    )
    seconds = gather_rel(second, "seq", ns)
    out_parts = {}
    back_parts = {}
    activs = []
    pre_grads = []
    bias_sum = 0.0
    for rel in range(0, ns, 2):
        activ, pre_grad, out, back, bgrad = feed_call(
            info, seconds[rel], seconds[rel + 1], cots[rel], cots[rel + 1], expand_all, shrink_all, ebias
        )
        activs.append(activ)
        pre_grads.append(pre_grad)
        bias_sum = bias_sum + bgrad
        for at in range(2):
            out_parts[rel + at] = out[at]
            back_parts[rel + at] = back[at]
    back_a, back_b = scatter_rel(back_parts, "seq", ns, last=False)
    resid_grad, branch, mixed_grad, turn_sums = turn_call(info, back_a, back_b, resid, cot, vecs, outw_full, ns)
    out_a, out_b = scatter_rel(out_parts, "seq", ns, last=False)
    layer_output = (resid + out_a.astype(F32) + out_b.astype(F32) + vecs[11:12]).astype(BF)

    pair_of = lambda values: [jnp.concatenate([values[r], values[r + 1]], 0) for r in range(0, ns, 2)]
    shrink_stack = wgrad_call(info, activs, pair_of(cots), nb)
    expand_stack = wgrad_call(info, pair_of(seconds), pre_grads, nb)
    outw_stack = wgrad_call(info, [merged], [branch], nb, split=ns)

    heads_grad = jnp.zeros((count, cw), BF)
    for rel in range(ns):
        block = mixed_grad[rel]
        block = lax.ppermute(block, "seq", pairs(ns, rel)) if rel else block
        heads_grad = lax.dynamic_update_slice(heads_grad, block, ((si ^ rel) * tok, 0))
    joined_grad = attend_back(joined, heads_grad, mixed, log_sums, info, slopes)
    normed_parts, last_sums, sides = last_call(info, joined_grad, normed, group_one, ns)
    norm_a, norm_b = scatter_rel({rel: normed_parts[rel] for rel in range(ns)}, "seq", ns, last=False)
    joined_stack = wgrad_call(info, [normed], [joined_grad], nb)
    input_grad = end_call(norm_a, norm_b, x, resid_grad, vecs)

    shift_one = last_sums[1]
    gain_one = (last_sums[0] - vecs[1] * shift_one) / vecs[0]
    side = sides.reshape(heads, 3, HD)
    side = jnp.stack([side[:, 0], side[:, 2]], 1).reshape(2 * cw)
    side = lax.dynamic_update_slice(jnp.zeros((2 * dim,), F32), side, (si * 2 * cw,))
    spread_bias = lax.dynamic_update_slice(
        jnp.zeros((nb, ns, units), F32), bias_sum.reshape(nb, 1, units), (0, si, 0)
    )
    pieces = [gain_one, shift_one, side, turn_sums[2], turn_sums[0], turn_sums[1], spread_bias, turn_sums[3]]
    shares = jnp.concatenate([piece.reshape(nb, -1) for piece in pieces], 1).astype(BF)
    owners = bi ^ jnp.array(sorted(range(nb), key=lambda rel: place_of(rel, nb)), jnp.int32)
    shares = scatter_stack(jnp.take(shares, owners, axis=0), "batch", nb)
    for bit in bits_low_last(ns)[::-1]:
        shares = add16(shares, lax.ppermute(shares, "seq", pairs(ns, bit)))
    shares = shares.astype(F32)

    def collect(block):
        parts = gather_rel(block, "seq", ns)
        stack = jnp.stack([parts[rel] for rel in range(ns)])
        return jnp.take(stack, jnp.arange(ns, dtype=jnp.int32) ^ si, axis=0).astype(F32)

    shrink_grad = collect(scatter_stack(shrink_stack, "batch", nb)).reshape(ns * units, dim)
    expand_grad = collect(scatter_stack(expand_stack, "batch", nb).reshape(rows, nb, units))
    expand_grad = expand_grad.transpose(1, 2, 0, 3).reshape(rows, ns * ff)
    outw_share = scatter_rel({rel: outw_stack[rel] for rel in range(ns)}, "seq", ns)
    outw_grad = collect(scatter_stack(outw_share, "batch", nb)).transpose(1, 0, 2).reshape(rows, dim)
    joined_wgrad = collect(scatter_stack(joined_stack, "batch", nb)).transpose(1, 0, 2).reshape(rows, ns * cols)
    small = []
    at = 0
    for size in (1, 1, 2, 1, 1, 1, 4, 1):
        small.append(shares[at * rows : (at + size) * rows])
        at += size
    return (
        layer_output[None],
        input_grad[None],
        small[0],
        small[1],
        joined_wgrad,
        small[2],
        outw_grad,
        small[3],
        small[4],
        small[5],
        expand_grad,
        small[6],
        shrink_grad,
        small[7],
    )


def solution(mesh):
    row = P("batch")
    mat = P("batch", None)
    act = P("batch", "seq", None)
    return jax.shard_map(
        body,
        mesh=mesh,
        in_specs=(act, row, row, row, mat, row, mat, row, row, row, mat, row, mat, row, act),
        out_specs=(act, act, row, row, mat, row, mat, row, row, row, mat, row, mat, row),
        check_vma=False,
    )
```

```python
import functools

import jax
import jax.numpy as jnp
from jax import lax
from jax.experimental import pallas as pl
from jax.experimental.pallas import tpu as pltpu
from jax.sharding import PartitionSpec as P

H = 16
HD = 64
EPSILON = 1e-05
F32 = jnp.float32
BF = jnp.bfloat16
NT = (((1,), (1,)), ((), ()))
NN = (((1,), (0,)), ((), ()))
TN = (((0,), (0,)), ((), ()))
MIB = 2**20
SHRINK = 1000


def dg(left, right, dims):
    return lax.dot_general(left, right, dims, preferred_element_type=F32)


def params(limit=56):
    return pltpu.CompilerParams(vmem_limit_bytes=limit * MIB)


def cost(flops, moved, exps=0):
    return pl.CostEstimate(flops=flops // SHRINK, bytes_accessed=moved // SHRINK, transcendentals=exps // SHRINK)


def norm_parts(values):
    mean = jnp.mean(values, axis=-1, keepdims=True)
    centered = values - mean
    scale = lax.rsqrt(jnp.mean(centered * centered, axis=-1, keepdims=True) + EPSILON)
    return centered * scale, scale


def norm_back(grad, unit, scale, gain):
    scaled = grad * gain
    return scale * (
        scaled
        - jnp.mean(scaled, axis=-1, keepdims=True)
        - unit * jnp.mean(scaled * unit, axis=-1, keepdims=True)
    )


def pairs(size, bit):
    return [(i, i ^ bit) for i in range(size)]


def bits_low_last(size):
    bits = []
    bit = 2
    while bit < size:
        bits.append(bit)
        bit *= 2
    if size > 1:
        bits.append(1)
    return bits


def add16(left, right):
    return (left.astype(F32) + right.astype(F32)).astype(BF)


def gather_rel(block, axis, size):
    out = {0: block}
    for bit in bits_low_last(size):
        for rel in list(out):
            out[rel | bit] = lax.ppermute(out[rel], axis, pairs(size, bit))
    return out


def scatter_rel(parts, axis, size, last=True):
    parts = dict(parts)
    order = bits_low_last(size)[::-1]
    for bit in order:
        for rel in sorted(parts, reverse=True):
            if rel & bit:
                other = lax.ppermute(parts.pop(rel), axis, pairs(size, bit))
                if bit == order[-1] and not last:
                    return parts[0], other
                parts[rel ^ bit] = add16(parts[rel ^ bit], other)
    return parts[0]


def tie(*values):
    return lax.optimization_barrier(values)


def place_table(me, size):
    index = jnp.arange(size, dtype=jnp.int32) ^ me
    place = jnp.zeros_like(index)
    for at, bit in enumerate(bits_low_last(size)):
        place = place | jnp.where(index & bit, 1 << at, 0)
    return place


def owner_table(me, size):
    place = jnp.arange(size, dtype=jnp.int32)
    rel = jnp.zeros_like(place)
    for at, bit in enumerate(bits_low_last(size)):
        rel = rel | jnp.where(place & (1 << at), bit, 0)
    return rel ^ me


def gather_all(block, axis, size, me):
    order = bits_low_last(size)
    out = block[None]
    for bit in order:
        out = jnp.concatenate([out, lax.ppermute(out, axis, pairs(size, bit))], 0)
    return jnp.take(out, place_table(me, size), axis=0)


def scatter_all(blocks, axis, size, me):
    stack = jnp.take(blocks, owner_table(me, size), axis=0)
    for bit in bits_low_last(size)[::-1]:
        half = stack.shape[0] // 2
        stack = add16(stack[:half], lax.ppermute(stack[half:], axis, pairs(size, bit)))
    return stack[0]


class Ring:
    def __init__(self, size, index, live):
        self.size = size
        self.live = live
        order = list(range(0, size, 2)) + list(range(size - 1, 0, -2))
        self.forward = [(order[i], order[(i + 1) % size]) for i in range(size)]
        self.backward = [(b, a) for a, b in self.forward]
        count = jnp.arange(size, dtype=jnp.int32)
        place = lambda k: jnp.where(k % 2 == 0, k // 2, size - (k + 1) // 2)
        if self.live:
            self.slots = (place(count) - place(index) + size) % size
            seat = (place(index) + count) % size
            self.owners = jnp.where(seat < size // 2, 2 * seat, 2 * (size - seat) - 1)
        else:
            self.slots = count
            self.owners = count
        self.half = size // 2

    def table(self):
        return jnp.concatenate([self.slots, self.owners])

    def ahead(self, value):
        return lax.ppermute(value, "batch", self.forward)

    def back(self, value):
        return lax.ppermute(value, "batch", self.backward)


def owner_at(info, live, nb, slot):
    return info[2 + nb + slot] if live else slot


def put(outs, slot, value):
    if len(outs) == 1:
        outs[0][slot] = value
        return
    for at, out in enumerate(outs):

        @pl.when(slot == at)
        def _():
            out[0] = value


def blocks_of(refs):
    out = []
    for ref in refs:
        out += [(ref, at) for at in range(ref.shape[0])]
    return out


def once(shape):
    return pl.BlockSpec(shape, lambda i, *_: (0,) * len(shape), pipeline_mode=pl.Buffered(1))


def first_pack_kernel(info, joined, outw, out):
    cols = joined.shape[1]
    out[:, :cols] = joined[...]
    out[:, cols:] = outw[...]


def first_pack(info, joined, outw, cols, cw):
    rows = joined.shape[0]
    return pl.pallas_call(
        first_pack_kernel,
        grid_spec=pltpu.PrefetchScalarGridSpec(
            num_scalar_prefetch=1,
            grid=(1,),
            in_specs=[
                pl.BlockSpec((rows, cols), lambda i, info: (0, info[0])),
                pl.BlockSpec((rows, cw), lambda i, info: (0, info[0])),
            ],
            out_specs=pl.BlockSpec((rows, cols + cw), lambda i, info: (0, 0)),
        ),
        out_shape=jax.ShapeDtypeStruct((rows, cols + cw), BF),
        compiler_params=params(40),
        name="first_pack",
    )(info, joined, outw)


def second_pack_kernel(nb, ns, units, info, expand, shrink, out):
    rows = expand.shape[0]
    for k in range(nb):
        col = pl.ds(pl.multiple_of((k * ns + info[0]) * units, units), units)
        out[:rows, k * units : (k + 1) * units] = expand[:, col]
    out[rows:] = shrink[...]


def second_pack(info, expand, shrink, nb, ns):
    rows, wide = expand.shape
    dim = shrink.shape[1]
    units = shrink.shape[0] // ns
    return pl.pallas_call(
        functools.partial(second_pack_kernel, nb, ns, units),
        grid_spec=pltpu.PrefetchScalarGridSpec(
            num_scalar_prefetch=1,
            grid=(1,),
            in_specs=[
                pl.BlockSpec((rows, wide), lambda i, info: (0, 0)),
                pl.BlockSpec((units, dim), lambda i, info: (info[0], 0)),
            ],
            out_specs=pl.BlockSpec((rows + units, dim), lambda i, info: (0, 0)),
        ),
        out_shape=jax.ShapeDtypeStruct((rows + units, dim), BF),
        compiler_params=params(40),
        name="second_pack",
    )(info, expand, shrink)


def first_kernel(ns, nt, nb, rows, cols, live, info, vecs, jbias, *refs):
    xs, weights = refs[:ns], refs[ns:-4]
    normed, joined, full, outw = refs[-4:]
    step = pl.program_id(0)

    @pl.when(step == 0)
    def _():
        for slot, (ref, at) in enumerate(blocks_of(weights)):
            high = owner_at(info, live, nb, slot) * rows
            high = pl.multiple_of(high, rows) if live else high
            full[pl.ds(high, rows)] = ref[at, :, :cols]
            outw[pl.ds(high, rows)] = ref[at, :, cols:]

    for rel in range(ns):

        @pl.when(lax.div(step, nt) == rel)
        def _():
            unit, _ = norm_parts(xs[rel][...].astype(F32))
            value = (unit * vecs[0:1] + vecs[1:2]).astype(BF)
            normed[...] = value
            joined[...] = (dg(value, full[...], NN) + jbias[...]).astype(BF)


def first_call(info, vecs, jbias, xs, weights, live):
    ns = len(xs)
    tok, dim = xs[0].shape
    nb = sum(weight.shape[0] for weight in weights)
    rows = dim // nb
    cols = jbias.shape[1]
    cw = weights[0].shape[2] - cols
    tile = min(256, tok)
    nt = tok // tile
    place = lambda i, info: ((info[0] ^ lax.div(i, nt)) * nt + lax.rem(i, nt), 0)

    def source(rel):
        return pl.BlockSpec((tile, dim), lambda i, info: (jnp.clip(i - rel * nt, 0, nt - 1), 0))

    return pl.pallas_call(
        functools.partial(first_kernel, ns, nt, nb, rows, cols, live),
        grid_spec=pltpu.PrefetchScalarGridSpec(
            num_scalar_prefetch=1,
            grid=(ns * nt,),
            in_specs=[once(vecs.shape), once(jbias.shape)]
            + [source(rel) for rel in range(ns)]
            + [once(weight.shape) for weight in weights],
            out_specs=[
                pl.BlockSpec((tile, dim), place),
                pl.BlockSpec((tile, cols), place),
                once((dim, cols)),
                once((dim, cw)),
            ],
        ),
        out_shape=[
            jax.ShapeDtypeStruct((ns * tok, dim), BF),
            jax.ShapeDtypeStruct((ns * tok, cols), BF),
            jax.ShapeDtypeStruct((dim, cols), BF),
            jax.ShapeDtypeStruct((dim, cw), BF),
        ],
        compiler_params=params(40),
        cost_estimate=cost(2 * ns * tok * dim * cols, 2 * ns * tok * (2 * dim + cols)),
        name="first",
    )(info, vecs, jbias, *xs, *weights)


def three(value):
    high = value.astype(BF)
    rest = value - high.astype(F32)
    mid = rest.astype(BF)
    return high, mid, (rest - mid.astype(F32)).astype(BF)


def spread(lane, base, columns):
    for at, column in columns:
        base = jnp.where(lane == at, column.astype(F32), base)
    return base.astype(BF)


def key_extra(count, slope, length):
    lane = lax.broadcasted_iota(jnp.int32, (count, HD), 1)
    pos = lax.broadcasted_iota(jnp.int32, (count, HD), 0)
    high, mid, low = three(slope * pos.astype(F32))
    dead = jnp.where(pos < length, 0.0, -1e30)
    return spread(lane, jnp.where(lane < 7, 1.0, 0.0), [(0, high), (1, mid), (2, low), (3, dead)])


def attend_kernel(count, size, pair, info, slopes, joined, mixed, sums, keys):
    lane = lax.broadcasted_iota(jnp.int32, (size, HD), 1)
    ones = jnp.where(lane < 4, 1.0, 0.0).astype(BF)
    for hh in range(2):
        base = 3 * HD * hh
        extra = key_extra(count, slopes[2 * pair + hh], info[1])
        keys[hh] = jnp.concatenate([joined[:, base + HD : base + 2 * HD], extra], 1)
    query_at = lax.broadcasted_iota(jnp.int32, (size, size), 0)
    key_at = lax.broadcasted_iota(jnp.int32, (size, size), 1)
    for block in range(count // size):
        low = block * size
        high = low + size
        outs = []
        logs = []
        for hh in range(2):
            base = 3 * HD * hh
            query = (joined[low:high, base : base + HD].astype(F32) * 0.125).astype(BF)
            query = jnp.concatenate([query, ones], 1)
            near = jnp.where(key_at <= query_at, dg(query, keys[hh, low:high], NT), -1e30)
            top = jnp.max(near, axis=1, keepdims=True)
            if block:
                far = dg(query, keys[hh, 0:low], NT)
                top = jnp.maximum(top, jnp.max(far, axis=1, keepdims=True))
            near = jnp.exp(near - top)
            total = jnp.sum(near, axis=1, keepdims=True)
            acc = dg(near.astype(BF), joined[low:high, base + 2 * HD : base + 3 * HD], NN)
            if block:
                far = jnp.exp(far - top)
                total += jnp.sum(far, axis=1, keepdims=True)
                acc += dg(far.astype(BF), joined[0:low, base + 2 * HD : base + 3 * HD], NN)
            outs.append(acc / total)
            logs.append(jnp.broadcast_to(top + jnp.log(total), (size, HD)))
        mixed[low:high] = jnp.concatenate(outs, 1).astype(BF)
        sums[low:high] = jnp.concatenate(logs, 1)


def attend(joined, info, slopes, pair):
    count = joined.shape[0]
    smem = pl.BlockSpec(memory_space=pltpu.SMEM)
    area = count * count
    return pl.pallas_call(
        functools.partial(attend_kernel, count, min(512, count), pair),
        grid=(1,),
        in_specs=[smem, smem, pl.BlockSpec((count, 6 * HD), lambda i: (0, pair))],
        out_specs=[pl.BlockSpec((count, 2 * HD), lambda i: (0, 0))] * 2,
        out_shape=[
            jax.ShapeDtypeStruct((count, 2 * HD), BF),
            jax.ShapeDtypeStruct((count, 2 * HD), F32),
        ],
        scratch_shapes=[pltpu.VMEM((2, count, 2 * HD), BF)],
        compiler_params=params(),
        cost_estimate=cost(area * 1024, 20 * count * HD, area),
        name="attend",
    )(info, slopes, joined)


def attend_back_kernel(count, size, ns, pair, info, slopes, joined, mixed, sums, *refs):
    pieces_in = refs[:ns]
    out, sides, keys, queries, values, grads, query_grad = refs[ns:]
    tok = count // ns
    lane = lax.broadcasted_iota(jnp.int32, (count, HD), 1)
    near_lane = lax.broadcasted_iota(jnp.int32, (tok, HD), 1)
    for hh in range(2):
        base = 3 * HD * hh
        half = slice(hh * HD, (hh + 1) * HD)
        extra = key_extra(count, slopes[2 * pair + hh], info[1])
        keys[hh] = jnp.concatenate([joined[:, base + HD : base + 2 * HD], extra], 1)
        query = (joined[:, base : base + HD].astype(F32) * 0.125).astype(BF)
        high, mid, low = three(-sums[:, half])
        extra = spread(lane, jnp.where(lane < 4, 1.0, 0.0), [(4, high), (5, mid), (6, low)])
        queries[hh] = jnp.concatenate([query, extra], 1)
        ones = jnp.where(lane < 3, 1.0, 0.0).astype(BF)
        values[hh] = jnp.concatenate([joined[:, base + 2 * HD : base + 3 * HD], ones], 1)
        for rel in range(ns):
            at = pl.ds(pl.multiple_of((info[0] ^ rel) * tok, tok), tok)
            part = pieces_in[rel][:, half]
            inner = jnp.sum(part.astype(F32) * mixed[at, half].astype(F32), axis=1, keepdims=True)
            high, mid, low = three(jnp.broadcast_to(-inner, (tok, HD)))
            extra = spread(near_lane, jnp.zeros((tok, HD), F32), [(0, high), (1, mid), (2, low)])
            grads[hh, at] = jnp.concatenate([part, extra], 1)
    key_at = lax.broadcasted_iota(jnp.int32, (size, size), 0)
    query_at = lax.broadcasted_iota(jnp.int32, (size, size), 1)
    blocks = count // size
    for j in range(blocks):
        ks = slice(j * size, (j + 1) * size)
        pieces = []
        for hh in range(2):
            key_sum = None
            for i in range(j, blocks):
                qs = slice(i * size, (i + 1) * size)
                probs = jnp.exp(dg(keys[hh, ks], queries[hh, qs], NT))
                if i == j:
                    probs = jnp.where(key_at <= query_at, probs, 0.0)
                slope = (probs * dg(values[hh, ks], grads[hh, qs], NT)).astype(BF)
                value_part = dg(probs.astype(BF), grads[hh, qs], NN)
                key_part = dg(slope, queries[hh, qs], NN)
                query_part = dg(keys[hh, ks], slope, TN)
                value_sum = value_part if key_sum is None else value_sum + value_part
                key_sum = key_part if key_sum is None else key_sum + key_part
                query_grad[hh, :, qs] = query_part if j == 0 else query_grad[hh, :, qs] + query_part
            pieces += [jnp.zeros((size, HD), F32), key_sum[:, :HD], value_sum[:, :HD]]
        out[ks] = jnp.concatenate(pieces, 1).astype(BF)
    for hh in range(2):
        base = 3 * HD * hh
        out[:, base : base + HD] = (query_grad[hh].T[:, :HD] * 0.125).astype(BF)
    sides[...] = jnp.sum(out[...].astype(F32), axis=0, keepdims=True)


def attend_back(joined, grads, mixed, sums, info, slopes, pair):
    count = joined.shape[0]
    ns = len(grads)
    smem = pl.BlockSpec(memory_space=pltpu.SMEM)
    wide = pl.BlockSpec((count, 6 * HD), lambda i: (0, pair))
    narrow = pl.BlockSpec((count, 2 * HD), lambda i: (0, 0))
    piece = pl.BlockSpec((count // ns, 2 * HD), lambda i: (0, 0))
    area = count * count
    return pl.pallas_call(
        functools.partial(attend_back_kernel, count, min(512, count), ns, pair),
        grid=(1,),
        in_specs=[smem, smem, wide, narrow, narrow] + [piece] * ns,
        out_specs=[pl.BlockSpec((count, 6 * HD), lambda i: (0, 0)), pl.BlockSpec((1, 6 * HD), lambda i: (0, 0))],
        out_shape=[jax.ShapeDtypeStruct((count, 6 * HD), BF), jax.ShapeDtypeStruct((1, 6 * HD), F32)],
        scratch_shapes=[pltpu.VMEM((2, count, 2 * HD), BF)] * 4 + [pltpu.VMEM((2, 2 * HD, count), F32)],
        compiler_params=params(),
        cost_estimate=cost(area * 2560, 40 * count * HD, area),
        name="attend_back",
    )(info, slopes, joined, mixed, sums, *grads)


def middle_kernel(ns, np, info, x, vecs, *refs):
    mixed, weights = refs[: ns * np], refs[ns * np : ns * np + ns]
    merged, resid, second, full = refs[ns * np + ns :]
    cw = weights[0].shape[1]
    pw = cw // np

    @pl.when(pl.program_id(0) == 0)
    def _():
        for rel in range(ns):
            full[:, pl.ds(pl.multiple_of((info[0] ^ rel) * cw, cw), cw)] = weights[rel][...]

    for pair in range(np):
        for rel in range(ns):
            col = pl.ds(pl.multiple_of((info[0] ^ rel) * cw + pair * pw, pw), pw)
            merged[:, col] = mixed[pair * ns + rel][...]
    value = x[...].astype(F32) + dg(merged[...], full[...], NN) + vecs[4:5]
    resid[...] = value
    unit, _ = norm_parts(value)
    second[...] = (unit * vecs[5:6] + vecs[6:7]).astype(BF)


def middle_call(info, x, vecs, mixed, weights):
    tok, dim = x.shape
    ns = len(weights)
    np = len(mixed) // ns
    tile = min(256, tok)
    part = lambda width: pl.BlockSpec((tile, width), lambda i, info: (i, 0))
    return pl.pallas_call(
        functools.partial(middle_kernel, ns, np),
        grid_spec=pltpu.PrefetchScalarGridSpec(
            num_scalar_prefetch=1,
            grid=(tok // tile,),
            in_specs=[part(dim), once(vecs.shape)]
            + [part(block.shape[1]) for block in mixed]
            + [once(weight.shape) for weight in weights],
            out_specs=[part(dim), part(dim), part(dim), once((dim, dim))],
        ),
        out_shape=[
            jax.ShapeDtypeStruct((tok, dim), BF),
            jax.ShapeDtypeStruct((tok, dim), F32),
            jax.ShapeDtypeStruct((tok, dim), BF),
            jax.ShapeDtypeStruct((dim, dim), BF),
        ],
        compiler_params=params(40),
        cost_estimate=cost(2 * tok * dim * dim, 12 * tok * dim + 4 * dim * dim),
        name="middle",
    )(info, x, vecs, *mixed, *weights)


def feed_kernel(nt, nb, rows, units, live, info, sa, sb, ca, cb, ebias, *refs):
    weights = refs[:-9]
    activ, pre_grad, oa, ob, ba, bb, bgrad, wide, tall = refs[-9:]
    step = pl.program_id(0)

    @pl.when(step == 0)
    def _():
        blocks = blocks_of(weights)
        for slot in range(nb):
            owner = owner_at(info, live, nb, slot)
            high = pl.multiple_of(owner * rows, rows) if live else owner * rows
            deep = pl.multiple_of(owner * units, units) if live else owner * units
            if len(blocks) == nb:
                ref, at = blocks[slot]
                wide[pl.ds(high, rows)] = ref[at, :rows]
                tall[pl.ds(deep, units)] = ref[at, rows:]
            else:
                wide[pl.ds(high, rows)] = weights[0][slot]
                tall[pl.ds(deep, units)] = weights[1][slot]
        bgrad[...] = jnp.zeros_like(bgrad)

    def work(second, cot, out, back):
        pre = dg(second[...], wide[...], NN) + ebias[...]
        square = pre * pre
        bend = jnp.tanh(0.7978845608028654 * pre * (1.0 + 0.044715 * square))
        half = 0.5 + 0.5 * bend
        act = (pre * half).astype(BF)
        activ[...] = act
        out[...] = dg(act, tall[...], NN).astype(BF)
        steep = half + pre * (0.5 - 0.5 * bend * bend) * (0.7978845608028654 + 0.10703222440890037 * square)
        grad = (dg(cot[...], tall[...], NT) * steep).astype(BF)
        pre_grad[...] = grad
        bgrad[...] += jnp.sum(grad.astype(F32), axis=0, keepdims=True)
        back[...] = dg(grad, wide[...], NT).astype(BF)

    @pl.when(step < nt)
    def _():
        work(sa, ca, oa, ba)

    @pl.when(step >= nt)
    def _():
        work(sb, cb, ob, bb)


def feed_call(info, sa, sb, ca, cb, ebias, weights, rows, units, nb, live):
    tok, dim = sa.shape
    ff = ebias.shape[1]
    tile = min(256, tok)
    nt = tok // tile
    left = pl.BlockSpec((tile, dim), lambda i, info: (jnp.minimum(i, nt - 1), 0))
    right = pl.BlockSpec((tile, dim), lambda i, info: (jnp.maximum(i - nt, 0), 0))
    flat = pl.BlockSpec((tile, ff), lambda i, info: (i, 0))
    shape = jax.ShapeDtypeStruct((tok, dim), BF)
    return pl.pallas_call(
        functools.partial(feed_kernel, nt, nb, rows, units, live),
        grid_spec=pltpu.PrefetchScalarGridSpec(
            num_scalar_prefetch=1,
            grid=(2 * nt,),
            in_specs=[left, right, left, right, once(ebias.shape)] + [once(weight.shape) for weight in weights],
            out_specs=[flat, flat, left, right, left, right, pl.BlockSpec((1, ff), lambda i, info: (0, 0))],
            scratch_shapes=[pltpu.VMEM((dim, ff), BF), pltpu.VMEM((ff, dim), BF)],
        ),
        out_shape=[jax.ShapeDtypeStruct((2 * tok, ff), BF)] * 2
        + [shape] * 4
        + [jax.ShapeDtypeStruct((1, ff), F32)],
        compiler_params=params(),
        cost_estimate=cost(16 * tok * dim * ff, 16 * tok * dim + 8 * dim * ff, 2 * tok * ff),
        name="feed",
    )(info, sa, sb, ca, cb, ebias, *weights)


def feed_grad_kernel(ns, nb, rows, units, steps, info, *refs):
    half = ns // 2
    activs, cots, seconds, grads = refs[:half], refs[half : half + ns], refs[half + ns : half + 2 * ns], refs[half + 2 * ns : 2 * half + 2 * ns]
    outs = refs[2 * half + 2 * ns :]
    step = pl.program_id(0)

    def total(wides, thins, wide_left):
        out = None
        for rel in range(ns):
            thin = thins[rel]
            tok = thin.shape[0]
            wide = wides[rel // 2][(rel % 2) * tok : (rel % 2 + 1) * tok]
            term = dg(wide, thin[...], TN) if wide_left else dg(thin[...], wide, TN)
            out = term if out is None else out + term
        return out.astype(BF)

    def store(value, high, count, at, low):
        for k in range(value.shape[0] // count):
            slot = info[2 + at * (value.shape[0] // count) + k]
            piece = value[k * count : (k + 1) * count]
            if len(outs) == nb:
                for mine, out in enumerate(outs):

                    @pl.when(slot == mine)
                    def _():
                        out[0, low : low + count] = piece

            else:
                outs[0 if high else 1][slot] = piece

    @pl.when(step < steps)
    def _():
        store(total(activs, cots, True), False, units, step, rows)

    @pl.when(step >= steps)
    def _():
        store(total(grads, seconds, False), True, rows, step - steps, 0)


def feed_grad_call(info, activs, cots, seconds, grads, nb, live):
    ns = len(cots)
    dim = cots[0].shape[1]
    ff = activs[0].shape[1]
    rows, units = dim // nb, ff // nb
    tile = 256
    steps = ff // tile
    tok = ns * cots[0].shape[0]
    left = lambda a: pl.BlockSpec((a.shape[0], tile), lambda i, info: (0, jnp.minimum(i, steps - 1)))
    right = lambda a: pl.BlockSpec((a.shape[0], tile), lambda i, info: (0, jnp.maximum(i - steps, 0)))
    fixed = lambda a: once(a.shape)
    shapes = [(1, rows + units, dim)] * nb if live else [(nb, rows, ff), (nb, units, dim)]
    return pl.pallas_call(
        functools.partial(feed_grad_kernel, ns, nb, rows, units, steps),
        grid_spec=pltpu.PrefetchScalarGridSpec(
            num_scalar_prefetch=1,
            grid=(steps + dim // tile,),
            in_specs=[left(a) for a in activs]
            + [fixed(a) for a in cots]
            + [right(a) for a in seconds]
            + [fixed(a) for a in grads],
            out_specs=[once(shape) for shape in shapes],
        ),
        out_shape=[jax.ShapeDtypeStruct(shape, BF) for shape in shapes],
        compiler_params=params(),
        cost_estimate=cost(4 * tok * dim * ff, 4 * tok * (dim + ff) + 4 * dim * ff),
        name="feed_grad",
    )(info, *activs, *cots, *seconds, *grads)


def split_grad_kernel(ns, info, left, right, *refs):
    outs, held = refs[:ns], refs[ns]
    held[...] = dg(left[...], right[...], TN)
    cw = held.shape[1] // ns
    for rel in range(ns):
        col = pl.ds(pl.multiple_of((info[0] ^ rel) * cw, cw), cw)
        outs[rel][...] = held[:, col].astype(BF)


def split_grad(info, left, right, ns):
    tok, dim = left.shape
    tile = 256
    cw = dim // ns
    return pl.pallas_call(
        functools.partial(split_grad_kernel, ns),
        grid_spec=pltpu.PrefetchScalarGridSpec(
            num_scalar_prefetch=1,
            grid=(dim // tile,),
            in_specs=[pl.BlockSpec((tok, tile), lambda i, info: (0, i)), once((tok, dim))],
            out_specs=[pl.BlockSpec((tile, cw), lambda i, info: (i, 0))] * ns,
            scratch_shapes=[pltpu.VMEM((tile, dim), F32)],
        ),
        out_shape=[jax.ShapeDtypeStruct((dim, cw), BF)] * ns,
        compiler_params=params(40),
        cost_estimate=cost(2 * tok * dim * dim, 6 * dim * dim),
        name="split_grad",
    )(info, left, right)


def joined_grad_kernel(nb, rows, np, info, left, other, *refs):
    rights, outs = refs[:np], refs[np:]
    totals = [dg(left[...], right[...], TN).astype(BF) for right in rights]
    value = jnp.concatenate(totals + [other[...]], 1)
    tile = value.shape[0]
    first = pl.program_id(0) * (tile // rows)
    for k in range(tile // rows):
        put(outs, info[2 + first + k], value[k * rows : (k + 1) * rows])


def joined_grad_call(info, left, rights, other, nb, live):
    count, dim = left.shape
    cols = sum(right.shape[1] for right in rights)
    cw = other.shape[1]
    rows = dim // nb
    tile = 256
    shapes = [(1, rows, cols + cw)] * nb if live else [(nb, rows, cols + cw)]
    return pl.pallas_call(
        functools.partial(joined_grad_kernel, nb, rows, len(rights)),
        grid_spec=pltpu.PrefetchScalarGridSpec(
            num_scalar_prefetch=1,
            grid=(dim // tile,),
            in_specs=[
                pl.BlockSpec((count, tile), lambda i, info: (0, i)),
                pl.BlockSpec((tile, cw), lambda i, info: (i, 0)),
            ]
            + [once(right.shape) for right in rights],
            out_specs=[once(shape) for shape in shapes],
        ),
        out_shape=[jax.ShapeDtypeStruct(shape, BF) for shape in shapes],
        compiler_params=params(),
        cost_estimate=cost(2 * count * dim * cols, 2 * count * (dim + cols) + 4 * dim * dim),
        name="joined_grad",
    )(info, left, other, *rights)


def turn_kernel(ns, np, cw, info, ga, gb, resid, cot, vecs, full, resid_grad, branch, *refs):
    mixed_grads, sums, held = refs[: ns * np], refs[ns * np], refs[ns * np + 1]

    @pl.when(pl.program_id(0) == 0)
    def _():
        sums[...] = jnp.zeros_like(sums)

    grad = ga[...].astype(F32) + gb[...].astype(F32)
    unit, scale = norm_parts(resid[...])
    outer = cot[...].astype(F32)
    value = outer + norm_back(grad, unit, scale, vecs[5:6])
    resid_grad[...] = value
    low = value.astype(BF)
    branch[...] = low
    held[...] = dg(low, full[...], NT).astype(BF)
    pw = cw // np
    for pair in range(np):
        for rel in range(ns):
            col = pl.ds(pl.multiple_of((info[0] ^ rel) * cw + pair * pw, pw), pw)
            mixed_grads[pair * ns + rel][...] = held[:, col]
    for at, term in enumerate((grad * unit, grad, low.astype(F32), outer)):
        sums[at : at + 1] += jnp.sum(term, axis=0, keepdims=True)


def turn_call(info, ga, gb, resid, cot, vecs, full, ns, np):
    tok, dim = resid.shape
    cw = dim // ns
    tile = min(256, tok)
    part = pl.BlockSpec((tile, dim), lambda i, info: (i, 0))
    return pl.pallas_call(
        functools.partial(turn_kernel, ns, np, cw),
        grid_spec=pltpu.PrefetchScalarGridSpec(
            num_scalar_prefetch=1,
            grid=(tok // tile,),
            in_specs=[part, part, part, part, once(vecs.shape), once(full.shape)],
            out_specs=[part, part]
            + [pl.BlockSpec((tile, cw // np), lambda i, info: (i, 0))] * (ns * np)
            + [pl.BlockSpec((8, dim), lambda i, info: (0, 0))],
            scratch_shapes=[pltpu.VMEM((tile, dim), BF)],
        ),
        out_shape=[
            jax.ShapeDtypeStruct((tok, dim), F32),
            jax.ShapeDtypeStruct((tok, dim), BF),
        ]
        + [jax.ShapeDtypeStruct((tok, cw // np), BF)] * (ns * np)
        + [jax.ShapeDtypeStruct((8, dim), F32)],
        compiler_params=params(40),
        cost_estimate=cost(2 * tok * dim * dim, 16 * tok * dim + 2 * dim * dim),
        name="turn",
    )(info, ga, gb, resid, cot, vecs, full)


def last_kernel(ns, nt, np, info, normed, weight, *refs):
    rights, outs, sums = refs[:np], refs[np:-1], refs[-1]
    step = pl.program_id(0)

    @pl.when(step == 0)
    def _():
        sums[...] = jnp.zeros_like(sums)

    grad = None
    at = 0
    for right in rights:
        width = right.shape[1]
        term = dg(right[...], weight[:, at : at + width], NT)
        grad = term if grad is None else grad + term
        at += width
    low = grad.astype(BF)
    rel = ns - 1 - lax.div(step, nt)
    tile = low.shape[0]
    row = pl.multiple_of(lax.rem(step, nt) * tile, tile)
    for mine in range(ns):

        @pl.when(rel == mine)
        def _():
            if ns == 4 and mine % 2:
                outs[2][mine // 2, pl.ds(row, tile)] = low
            elif ns == 4:
                outs[mine // 2][pl.ds(row, tile)] = low
            else:
                outs[mine][pl.ds(row, tile)] = low

    sums[0:1] += jnp.sum(grad * normed[...].astype(F32), axis=0, keepdims=True)
    sums[1:2] += jnp.sum(grad, axis=0, keepdims=True)


def last_call(info, rights, normed, weight, ns):
    count, dim = normed.shape
    cols = weight.shape[1]
    tok = count // ns
    tile = min(256, tok)
    nt = tok // tile
    source = lambda i, info: ((info[0] ^ (ns - 1 - lax.div(i, nt))) * nt + lax.rem(i, nt), 0)
    shapes = [(tok, dim)] * 2 + [(2, tok, dim)] if ns == 4 else [(tok, dim)] * ns
    return pl.pallas_call(
        functools.partial(last_kernel, ns, nt, len(rights)),
        grid_spec=pltpu.PrefetchScalarGridSpec(
            num_scalar_prefetch=1,
            grid=(ns * nt,),
            in_specs=[pl.BlockSpec((tile, dim), source), once(weight.shape)]
            + [pl.BlockSpec((tile, right.shape[1]), source) for right in rights],
            out_specs=[once(shape) for shape in shapes] + [pl.BlockSpec((8, dim), lambda i, info: (0, 0))],
        ),
        out_shape=[jax.ShapeDtypeStruct(shape, BF) for shape in shapes] + [jax.ShapeDtypeStruct((8, dim), F32)],
        compiler_params=params(40),
        cost_estimate=cost(2 * count * dim * cols, 2 * count * (2 * dim + cols)),
        name="last",
    )(info, normed, weight, *rights)


def end_kernel(ga, gb, x, resid_grad, vecs, out):
    grad = ga[...].astype(F32) + gb[...].astype(F32)
    unit, scale = norm_parts(x[...].astype(F32))
    out[...] = resid_grad[...] + norm_back(grad, unit, scale, vecs[0:1])


def end_call(ga, gb, x, resid_grad, vecs):
    tok, dim = x.shape
    tile = min(128, tok)
    part = pl.BlockSpec((tile, dim), lambda i: (i, 0))
    return pl.pallas_call(
        end_kernel,
        grid=(tok // tile,),
        in_specs=[part, part, part, part, pl.BlockSpec(vecs.shape, lambda i: (0, 0))],
        out_specs=part,
        out_shape=jax.ShapeDtypeStruct((tok, dim), F32),
        compiler_params=params(40),
        cost_estimate=cost(20 * tok * dim, 14 * tok * dim),
        name="end",
    )(ga, gb, x, resid_grad, vecs)


def joined_out_kernel(ns, cols, info, *refs):
    parts, joined, outw = refs[:ns], refs[ns], refs[ns + 1]
    cw = parts[0].shape[1] - cols
    for rel in range(ns):
        joined[:, pl.ds(pl.multiple_of((info[0] ^ rel) * cols, cols), cols)] = parts[rel][:, :cols].astype(F32)
        outw[:, pl.ds(pl.multiple_of((info[0] ^ rel) * cw, cw), cw)] = parts[rel][:, cols:].astype(F32)


def joined_out(info, parts, cols):
    ns = len(parts)
    rows, wide = parts[0].shape
    shapes = [(rows, ns * cols), (rows, ns * (wide - cols))]
    return pl.pallas_call(
        functools.partial(joined_out_kernel, ns, cols),
        grid_spec=pltpu.PrefetchScalarGridSpec(
            num_scalar_prefetch=1,
            grid=(1,),
            in_specs=[once(part.shape) for part in parts],
            out_specs=[once(shape) for shape in shapes],
        ),
        out_shape=[jax.ShapeDtypeStruct(shape, F32) for shape in shapes],
        compiler_params=params(40),
        cost_estimate=cost(0, 6 * ns * rows * wide),
        name="joined_out",
    )(info, *parts)


def feed_out_kernel(ns, nb, rows, units, info, *refs):
    parts, expand, shrink = refs[:ns], refs[ns], refs[ns + 1]
    for rel in range(ns):
        seat = info[0] ^ rel
        shrink[pl.ds(pl.multiple_of(seat * units, units), units)] = parts[rel][rows:].astype(F32)
        for k in range(nb):
            col = pl.ds(pl.multiple_of((k * ns + seat) * units, units), units)
            expand[:, col] = parts[rel][:rows, k * units : (k + 1) * units].astype(F32)


def feed_out(info, parts, nb, rows):
    ns = len(parts)
    high, dim = parts[0].shape
    units = high - rows
    shapes = [(rows, ns * units * nb), (ns * units, dim)]
    return pl.pallas_call(
        functools.partial(feed_out_kernel, ns, nb, rows, units),
        grid_spec=pltpu.PrefetchScalarGridSpec(
            num_scalar_prefetch=1,
            grid=(1,),
            in_specs=[once(part.shape) for part in parts],
            out_specs=[once(shape) for shape in shapes],
        ),
        out_shape=[jax.ShapeDtypeStruct(shape, F32) for shape in shapes],
        compiler_params=params(40),
        cost_estimate=cost(0, 6 * ns * high * dim),
        name="feed_out",
    )(info, *parts)


def body(
    layer_input,
    lengths,
    first_gain,
    first_shift,
    joined_weight,
    joined_bias,
    output_weight,
    output_bias,
    second_gain,
    second_shift,
    expand_weight,
    expand_bias,
    shrink_weight,
    shrink_bias,
    out_grad,
):
    ns = lax.axis_size("seq")
    nb = lax.axis_size("batch")
    si = lax.axis_index("seq")
    bi = lax.axis_index("batch")
    tok = layer_input.shape[1]
    dim = layer_input.shape[2]
    heads = H // ns
    np = heads // 2
    cols = 3 * HD * heads
    cw = HD * heads
    rows = dim // nb
    ff = expand_weight.shape[1] // ns
    units = ff // nb
    x = layer_input[0]
    cot = out_grad[0]
    live = ns == 4 and nb == 8
    ring = Ring(nb, bi, live)
    info = jnp.concatenate([jnp.stack([si, lengths[0]]), ring.table()]).astype(jnp.int32)
    head_ids = si * heads + jnp.arange(heads, dtype=jnp.int32) + 1
    slopes = 2.0 ** (-8.0 * head_ids.astype(F32) / H)

    smalls = (first_gain, first_shift, joined_bias, output_bias, second_gain, second_shift, expand_bias, shrink_bias)
    smalls = jnp.concatenate([small.reshape(-1, rows) for small in smalls], 0)
    seat = si.reshape(1).astype(jnp.int32)
    one = first_pack(seat, joined_weight, output_weight, cols, cw)

    def step(held, t):
        if t < ring.half:
            held[t] = ring.back(held[t - 1])
        held[nb - t] = ring.ahead(held[(nb - t + 1) % nb])

    if live:
        x, one = tie(x, one)
        ones = {0: one}
        step(ones, 1)
        xs = gather_rel(x, "seq", ns)
        expand_weight, shrink_weight, _ = tie(expand_weight, shrink_weight, one)
        two = second_pack(seat, expand_weight, shrink_weight, nb, ns)
        smalls, _ = tie(smalls, one)
        smalls = smalls[None]
        for t in range(2, ring.half + 1):
            bit = bits_low_last(nb)[t - 2]
            smalls = jnp.concatenate([smalls, lax.ppermute(smalls, "batch", pairs(nb, bit))], 0)
            if t == 2:
                smalls, ones[1], ones[7], two, xs[1], cot = tie(smalls, ones[1], ones[7], two, xs[1], cot)
                cots = {0: cot, 1: lax.ppermute(cot, "seq", pairs(ns, 1))}
            elif t == 3:
                smalls, ones[2], ones[6], cots[1] = tie(smalls, ones[2], ones[6], cots[1])
            else:
                smalls, ones[3], ones[5], xs[2], two = tie(smalls, ones[3], ones[5], xs[2], two)
                twos = {0: two}
                step(twos, 1)
                cot, _ = tie(cot, two)
                cots[2] = lax.ppermute(cot, "seq", pairs(ns, 2))
            step(ones, t)
        smalls = jnp.take(smalls, place_table(bi, nb), axis=0)
        ones[4], twos[1], twos[7] = tie(ones[4], twos[1], twos[7])
        one_parts = [ones[slot][None] for slot in range(nb)]
    else:
        xs = gather_rel(x, "seq", ns)
        cots = gather_rel(cot, "seq", ns)
        smalls = gather_all(smalls, "batch", nb, bi)
        one_parts = [lax.all_gather(one, "batch")]

    vecs = smalls.astype(F32).transpose(1, 0, 2).reshape(12, dim)
    low = vecs[2:4].reshape(2, nb, rows).transpose(1, 0, 2).reshape(2 * dim)
    low = lax.dynamic_slice(low, (si * 2 * cw,), (2 * cw,)).reshape(heads, 2, HD)
    jbias = jnp.stack([low[:, 0], jnp.zeros_like(low[:, 0]), low[:, 1]], 1).reshape(1, cols)
    ebias = vecs[7:11].reshape(4, nb, rows).transpose(1, 0, 2).reshape(nb, ns, units)
    ebias = lax.dynamic_slice(ebias, (0, si, 0), (nb, 1, units)).reshape(1, ff)
    normed, joined, joined_full, outw_own = first_call(
        info, vecs, jbias, [xs[rel] for rel in range(ns)], one_parts, live
    )
    if live:
        step(twos, 2)
        joined, twos[2], twos[6], cots[2] = tie(joined, twos[2], twos[6], cots[2])
        step(twos, 3)
        cots[3] = lax.ppermute(cots[2], "seq", pairs(ns, 1))
    outw_all = gather_rel(outw_own, "seq", ns)
    mixed = []
    log_sums = []
    merged_parts = []

    def to_tokens(out):
        parts = []
        for rel in range(ns):
            block = lax.dynamic_slice(out, ((si ^ rel) * tok, 0), (tok, 2 * HD))
            parts.append(lax.ppermute(block, "seq", pairs(ns, rel)) if rel else block)
        return parts

    for pair in range(np):
        out, logs = attend(joined, info, slopes, pair)
        if live and pair == 0:
            out, joined, twos[3], twos[5], cots[3], outw_all[2], outw_all[1] = tie(
                out, joined, twos[3], twos[5], cots[3], outw_all[2], outw_all[1]
            )
            step(twos, 4)
            outw_all[3] = lax.ppermute(outw_all[2], "seq", pairs(ns, 1))
        mixed.append(out)
        log_sums.append(logs)
        merged_parts.append(to_tokens(out))
        if live and pair == 1:
            out, twos[4], outw_all[3], *merged_parts[0] = tie(out, twos[4], outw_all[3], *merged_parts[0])
            mixed[1] = out
            merged_parts[1] = to_tokens(out)
    merged_parts = [block for parts in merged_parts for block in parts]
    merged, resid, second, outw_full = middle_call(
        info, x, vecs, merged_parts, [outw_all[rel] for rel in range(ns)]
    )
    if live:
        two_parts = [twos[slot][None] for slot in range(nb)]
    else:
        expand_part = expand_weight.reshape(rows, nb, ns, units)
        expand_part = lax.dynamic_slice(expand_part, (0, 0, si, 0), (rows, nb, 1, units)).reshape(rows, ff)
        shrink_part = lax.dynamic_slice(shrink_weight, (si * units, 0), (units, dim))
        two_parts = [lax.all_gather(expand_part, "batch"), lax.all_gather(shrink_part, "batch")]
    out_parts = {}
    back_parts = {}
    activs = []
    pre_grads = []
    bias_sum = 0.0
    if live:
        seconds = {0: second, 2: lax.ppermute(second, "seq", pairs(ns, 2)), 1: lax.ppermute(second, "seq", pairs(ns, 1))}
    else:
        seconds = gather_rel(second, "seq", ns)
    for rel in range(0, ns, 2):
        activ, pre_grad, oa, ob, ba, bb, bgrad = feed_call(
            info, seconds[rel], seconds[rel + 1], cots[rel], cots[rel + 1], ebias, two_parts, rows, units, nb, live
        )
        if live and rel == 0:
            activ, ob, bb, seconds[2] = tie(activ, ob, bb, seconds[2])
            seconds[3] = lax.ppermute(seconds[2], "seq", pairs(ns, 1))
            seconds[2], seconds[3] = tie(seconds[2], seconds[3])
            near_back = lax.ppermute(bb, "seq", pairs(ns, 1))
            near_out = lax.ppermute(ob, "seq", pairs(ns, 1))
        activs.append(activ)
        pre_grads.append(pre_grad)
        bias_sum = bias_sum + bgrad
        out_parts.update({rel: oa, rel + 1: ob})
        back_parts.update({rel: ba, rel + 1: bb})
    if live:
        back_parts[3], near_back, near_out = tie(back_parts[3], near_back, near_out)
        back_a = add16(back_parts[0], near_back)
        out_a = add16(out_parts[0], near_out)
        far_back = lax.ppermute(back_parts[3], "seq", pairs(ns, 1))
        far_back, out_far = tie(far_back, out_parts[3])
        back_b = lax.ppermute(add16(back_parts[2], far_back), "seq", pairs(ns, 2))
        far_out = lax.ppermute(out_far, "seq", pairs(ns, 1))
    else:
        back_a, back_b = scatter_rel(back_parts, "seq", ns, last=False)
        out_a, out_b = scatter_rel(out_parts, "seq", ns, last=False)
    feed_stack = feed_grad_call(
        info,
        activs,
        [cots[rel] for rel in range(ns)],
        [seconds[rel] for rel in range(ns)],
        pre_grads,
        nb,
        live,
    )

    class Scatter:
        def __init__(self, parts):
            self.parts = [part[0] for part in parts]
            self.t = 0
            self.ahead = self.parts[ring.half]
            self.back = self.parts[ring.half + 1]

        def send(self):
            self.t += 1
            self.got_ahead = ring.ahead(self.ahead)
            self.got_back = ring.back(self.back) if self.t > 1 else None

        def take(self, *after):
            if after:
                self.got_ahead, *_ = tie(self.got_ahead, *after)
            if self.t == ring.half:
                total = self.parts[0].astype(F32) + self.got_ahead.astype(F32) + self.got_back.astype(F32)
                return total.astype(BF)
            self.ahead = add16(self.parts[ring.half - self.t], self.got_ahead)
            if self.t > 1:
                self.back = add16(self.parts[nb - ring.half + self.t], self.got_back)

    if live:
        feed_ring = Scatter(feed_stack)
        feed_ring.send()
        back_b, back_a, out_a, far_out, _ = tie(back_b, back_a, out_a, far_out, feed_stack[0])
        out_b = add16(out_parts[2], far_out)
    resid_grad, branch, *mixed_grads, turn_sums = turn_call(
        info, back_a, back_b, resid, cot, vecs, outw_full, ns, np
    )
    outw_stack = split_grad(info, merged, branch, ns)
    joined_grads = []
    sides = []

    def to_heads(pair):
        blocks = mixed_grads[pair * ns : (pair + 1) * ns]
        return [lax.ppermute(block, "seq", pairs(ns, rel)) if rel else block for rel, block in enumerate(blocks)]

    grads = to_heads(0)
    if live:
        feed_ring.take(*grads, *outw_stack)
        grads[0], *rest = tie(grads[0], feed_ring.ahead, *grads[1:], *outw_stack, *mixed_grads[ns:])
        feed_ring.ahead, grads[1:], outw_stack = rest[0], rest[1:ns], rest[ns : 2 * ns]
        mixed_grads[ns:] = rest[2 * ns :]
        feed_ring.send()
    for pair in range(np):
        if pair:
            grads = after
        out, side = attend_back(joined, grads, mixed[pair], log_sums[pair], info, slopes, pair)
        if pair + 1 < np:
            after = to_heads(pair + 1)
        if live and pair == 0:
            feed_ring.take(out, *after)
            after[0], feed_ring.ahead, feed_ring.back, out, *outw_stack = tie(
                after[0], feed_ring.ahead, feed_ring.back, out, *outw_stack
            )
            feed_ring.send()
        elif live:
            feed_ring.take(out)
        joined_grads.append(out)
        sides.append(side)
    outw_share = scatter_rel(dict(enumerate(outw_stack)), "seq", ns)
    if live:
        joined_grads[1], outw_share, feed_ring.ahead, feed_ring.back = tie(
            joined_grads[1], outw_share, feed_ring.ahead, feed_ring.back
        )
        feed_ring.send()
        out_b, _ = tie(out_b, outw_share)
        out_b = lax.ppermute(out_b, "seq", pairs(ns, 2))
    joined_stack = joined_grad_call(info, normed, joined_grads, outw_share, nb, live)
    if live:
        feed_share = feed_ring.take(joined_stack[0])
        feed_share, *joined_stack = tie(feed_share, *joined_stack)
        joined_ring = Scatter(joined_stack)
        joined_ring.send()
        joined_grads[0], _ = tie(joined_grads[0], joined_stack[0])
    *normed_parts, last_sums = last_call(info, joined_grads, normed, joined_full, ns)
    if live:
        joined_ring.take(last_sums, out_b)
        joined_ring.ahead, out_b, feed_share, sent, last_sums = tie(
            joined_ring.ahead, out_b, feed_share, normed_parts[2], last_sums
        )
        joined_ring.send()
        got = lax.ppermute(sent, "seq", pairs(ns, 1))
        feed_parts = {0: feed_share, 2: lax.ppermute(feed_share, "seq", pairs(ns, 2))}
        norm_a = add16(normed_parts[0], got[0])
        far = add16(normed_parts[1], got[1])
    else:
        norm_a, norm_b = scatter_rel(dict(enumerate(normed_parts)), "seq", ns, last=False)
    layer_output = (resid + out_a.astype(F32) + out_b.astype(F32) + vecs[11:12]).astype(BF)

    shift_one = last_sums[1:2]
    gain_one = (last_sums[0:1] - vecs[1:2] * shift_one) / vecs[0:1]
    side = jnp.concatenate(sides, 1).reshape(heads, 3, HD)
    side = jnp.stack([side[:, 0], side[:, 2]], 1).reshape(2 * cw)
    side = lax.dynamic_update_slice(jnp.zeros((2 * dim,), F32), side, (si * 2 * cw,))
    side = side.reshape(nb, 2, rows).transpose(1, 0, 2).reshape(2, dim)
    spread_bias = lax.dynamic_update_slice(
        jnp.zeros((nb, ns, units), F32), bias_sum.reshape(nb, 1, units), (0, si, 0)
    )
    spread_bias = spread_bias.reshape(nb, 4, rows).transpose(1, 0, 2).reshape(4, dim)
    shares = jnp.concatenate(
        [gain_one, shift_one, side, turn_sums[2:3], turn_sums[0:2], spread_bias, turn_sums[3:4]], 0
    )
    shares = shares.astype(BF).reshape(12, nb, rows).transpose(1, 0, 2)

    def ordered(block):
        parts = gather_rel(block, "seq", ns)
        return [parts[rel] for rel in range(ns)]

    if live:
        shares = jnp.take(shares, owner_table(bi, nb), axis=0)

        def fold(stack, bit):
            half = stack.shape[0] // 2
            return add16(stack[:half], lax.ppermute(stack[half:], "batch", pairs(nb, bit)))

        shares = fold(shares, 1)
        joined_ring.take(shares, far, feed_parts[2])
        joined_ring.ahead, joined_ring.back, shares, far, feed_parts[0], feed_parts[2] = tie(
            joined_ring.ahead, joined_ring.back, shares, far, feed_parts[0], feed_parts[2]
        )
        joined_ring.send()
        norm_b = lax.ppermute(far, "seq", pairs(ns, 2))
        feed_parts[1] = lax.ppermute(feed_parts[0], "seq", pairs(ns, 1))
        shares = fold(shares, 4)
        joined_ring.take(shares, feed_parts[1])
        joined_ring.ahead, joined_ring.back, shares, feed_parts[1], feed_parts[2] = tie(
            joined_ring.ahead, joined_ring.back, shares, feed_parts[1], feed_parts[2]
        )
        joined_ring.send()
        feed_parts[3] = lax.ppermute(feed_parts[2], "seq", pairs(ns, 1))
        shares = fold(shares, 2)[0]
        expand_grad, shrink_grad = feed_out(info, [feed_parts[rel] for rel in range(ns)], nb, rows)
        joined_share = joined_ring.take(norm_b, shares, expand_grad)
        joined_share, norm_b, shares = tie(joined_share, norm_b, shares)
        joined_parts = {0: joined_share, 2: lax.ppermute(joined_share, "seq", pairs(ns, 2))}
        joined_parts[1] = lax.ppermute(joined_share, "seq", pairs(ns, 1))
        shares = add16(shares, lax.ppermute(shares, "seq", pairs(ns, 1)))
        input_grad = end_call(norm_a, norm_b, x, resid_grad, vecs)
        joined_parts[2], joined_parts[1], shares, _ = tie(joined_parts[2], joined_parts[1], shares, input_grad)
        joined_parts[3] = lax.ppermute(joined_parts[2], "seq", pairs(ns, 1))
        shares = add16(shares, lax.ppermute(shares, "seq", pairs(ns, 2)))
        joined_parts = [joined_parts[rel] for rel in range(ns)]
    else:
        input_grad = end_call(norm_a, norm_b, x, resid_grad, vecs)
        shares = scatter_all(shares, "batch", nb, bi)
        for bit in bits_low_last(ns)[::-1]:
            shares = add16(shares, lax.ppermute(shares, "seq", pairs(ns, bit)))
        joined_share = lax.psum_scatter(joined_stack[0], "batch", scatter_dimension=0)
        expand_share = lax.psum_scatter(feed_stack[0], "batch", scatter_dimension=0)
        shrink_share = lax.psum_scatter(feed_stack[1], "batch", scatter_dimension=0)
        seats = jnp.arange(ns, dtype=jnp.int32) ^ si
        shrink_grad = jnp.take(jnp.stack(ordered(shrink_share)), seats, axis=0).astype(F32).reshape(ns * units, dim)
        expand_grad = jnp.take(jnp.stack(ordered(expand_share)), seats, axis=0).astype(F32)
        expand_grad = expand_grad.reshape(ns, rows, nb, units).transpose(1, 2, 0, 3).reshape(rows, ns * ff)
        joined_parts = ordered(joined_share)
    shares = shares.astype(F32)
    joined_wgrad, outw_grad = joined_out(info, joined_parts, cols)
    small = []
    at = 0
    for size in (1, 1, 2, 1, 1, 1, 4, 1):
        small.append(shares[at : at + size].reshape(size * rows))
        at += size
    return (
        layer_output[None],
        input_grad[None],
        small[0],
        small[1],
        joined_wgrad,
        small[2],
        outw_grad,
        small[3],
        small[4],
        small[5],
        expand_grad,
        small[6],
        shrink_grad,
        small[7],
    )


def solution(mesh):
    row = P("batch")
    mat = P("batch", None)
    act = P("batch", "seq", None)
    return jax.shard_map(
        body,
        mesh=mesh,
        in_specs=(act, row, row, row, mat, row, mat, row, row, row, mat, row, mat, row, act),
        out_specs=(act, act, row, row, mat, row, mat, row, row, row, mat, row, mat, row),
        check_vma=False,
    )
```

```python
import functools

import jax
import jax.numpy as jnp
from jax import lax
from jax.experimental import pallas as pl
from jax.experimental.pallas import tpu as pltpu
from jax.sharding import PartitionSpec as P

H = 16
HD = 64
EPSILON = 1e-05
F32 = jnp.float32
BF = jnp.bfloat16
NT = (((1,), (1,)), ((), ()))
NN = (((1,), (0,)), ((), ()))
TN = (((0,), (0,)), ((), ()))
MIB = 2**20
SHRINK = 1000


def dg(left, right, dims):
    return lax.dot_general(left, right, dims, preferred_element_type=F32)


def params(limit=56):
    return pltpu.CompilerParams(vmem_limit_bytes=limit * MIB)


def cost(flops, moved, exps=0):
    return pl.CostEstimate(flops=flops // SHRINK, bytes_accessed=moved // SHRINK, transcendentals=exps // SHRINK)


def norm_parts(values):
    mean = jnp.mean(values, axis=-1, keepdims=True)
    centered = values - mean
    scale = lax.rsqrt(jnp.mean(centered * centered, axis=-1, keepdims=True) + EPSILON)
    return centered * scale, scale


def norm_back(grad, unit, scale, gain):
    scaled = grad * gain
    return scale * (
        scaled
        - jnp.mean(scaled, axis=-1, keepdims=True)
        - unit * jnp.mean(scaled * unit, axis=-1, keepdims=True)
    )


def pairs(size, bit):
    return [(i, i ^ bit) for i in range(size)]


def bits_low_last(size):
    bits = []
    bit = 2
    while bit < size:
        bits.append(bit)
        bit *= 2
    if size > 1:
        bits.append(1)
    return bits


def add16(left, right):
    return (left.astype(F32) + right.astype(F32)).astype(BF)


def gather_rel(block, axis, size):
    out = {0: block}
    for bit in bits_low_last(size):
        for rel in list(out):
            out[rel | bit] = lax.ppermute(out[rel], axis, pairs(size, bit))
    return out


def scatter_rel(parts, axis, size, last=True):
    parts = dict(parts)
    order = bits_low_last(size)[::-1]
    for bit in order:
        for rel in sorted(parts, reverse=True):
            if rel & bit:
                other = lax.ppermute(parts.pop(rel), axis, pairs(size, bit))
                if bit == order[-1] and not last:
                    return parts[0], other
                parts[rel ^ bit] = add16(parts[rel ^ bit], other)
    return parts[0]


def tie(*values):
    return lax.optimization_barrier(values)


class Ring:
    def __init__(self, size, index, live):
        self.size = size
        self.live = live
        order = list(range(0, size, 2)) + list(range(size - 1, 0, -2))
        self.forward = [(order[i], order[(i + 1) % size]) for i in range(size)]
        self.backward = [(b, a) for a, b in self.forward]
        count = jnp.arange(size, dtype=jnp.int32)
        place = lambda k: jnp.where(k % 2 == 0, k // 2, size - (k + 1) // 2)
        if self.live:
            self.slots = (place(count) - place(index) + size) % size
            seat = (place(index) + count) % size
            self.owners = jnp.where(seat < size // 2, 2 * seat, 2 * (size - seat) - 1)
        else:
            self.slots = count
            self.owners = count
        self.half = size // 2

    def table(self):
        return jnp.concatenate([self.slots, self.owners])

    def ahead(self, value):
        return lax.ppermute(value, "batch", self.forward)

    def back(self, value):
        return lax.ppermute(value, "batch", self.backward)


def owner_at(info, live, nb, slot):
    return info[2 + nb + slot] if live else slot


def put(outs, slot, value, rows, cols):
    if len(outs) == 1:
        outs[0][slot, rows, cols] = value
        return
    for at, out in enumerate(outs):

        @pl.when(slot == at)
        def _():
            out[0, rows, cols] = value


def blocks_of(refs):
    out = []
    for ref in refs:
        out += [(ref, at) for at in range(ref.shape[0])]
    return out


def once(shape):
    return pl.BlockSpec(shape, lambda i, *_: (0,) * len(shape), pipeline_mode=pl.Buffered(1))


def first_pack_kernel(info, joined, outw, *refs):
    smalls, out = refs[:-1], refs[-1]
    rows, cols = joined.shape
    out[:rows, :cols] = joined[...]
    out[:rows, cols:] = outw[...]
    pieces = [small[...].astype(F32) for small in smalls]
    count = sum(piece.shape[0] for piece in pieces)
    pieces.append(jnp.zeros((16 - count, rows), F32))
    out[rows:, :rows] = jnp.concatenate(pieces, 0).astype(BF)
    out[rows:, rows:] = jnp.zeros((16, out.shape[1] - rows), BF)


def first_pack(info, joined, outw, smalls, cols, cw):
    rows = joined.shape[0]
    shape = (rows + 16, cols + cw)
    return pl.pallas_call(
        first_pack_kernel,
        grid_spec=pltpu.PrefetchScalarGridSpec(
            num_scalar_prefetch=1,
            grid=(1,),
            in_specs=[
                pl.BlockSpec((rows, cols), lambda i, info: (0, info[0])),
                pl.BlockSpec((rows, cw), lambda i, info: (0, info[0])),
            ]
            + [once(small.shape) for small in smalls],
            out_specs=pl.BlockSpec(shape, lambda i, info: (0, 0)),
        ),
        out_shape=jax.ShapeDtypeStruct(shape, BF),
        compiler_params=params(60),
        name="first_pack",
    )(info, joined, outw, *smalls)


def second_pack_kernel(nb, ns, units, info, expand, shrink, out):
    rows = expand.shape[0]
    for k in range(nb):
        col = pl.ds(pl.multiple_of((k * ns + info[0]) * units, units), units)
        out[:rows, k * units : (k + 1) * units] = expand[:, col]
    out[rows:] = shrink[...]


def second_pack(info, expand, shrink, nb, ns):
    rows, wide = expand.shape
    dim = shrink.shape[1]
    units = shrink.shape[0] // ns
    return pl.pallas_call(
        functools.partial(second_pack_kernel, nb, ns, units),
        grid_spec=pltpu.PrefetchScalarGridSpec(
            num_scalar_prefetch=1,
            grid=(1,),
            in_specs=[
                pl.BlockSpec((rows, wide), lambda i, info: (0, 0)),
                pl.BlockSpec((units, dim), lambda i, info: (info[0], 0)),
            ],
            out_specs=pl.BlockSpec((rows + units, dim), lambda i, info: (0, 0)),
        ),
        out_shape=jax.ShapeDtypeStruct((rows + units, dim), BF),
        compiler_params=params(60),
        name="second_pack",
    )(info, expand, shrink)


def first_kernel(ns, nt, nb, rows, cols, live, info, *refs):
    jbias_in, refs = (None, refs) if live else (refs[0], refs[1:])
    xs, weights = refs[:ns], refs[ns:-6]
    normed, joined, full, outw, vecs, jbias = refs[-6:]
    step = pl.program_id(0)

    @pl.when(step == 0)
    def _():
        for slot, (ref, at) in enumerate(blocks_of(weights)):
            high = owner_at(info, live, nb, slot) * rows
            high = pl.multiple_of(high, rows) if live else high
            full[pl.ds(high, rows)] = ref[at, :rows, :cols]
            outw[pl.ds(high, rows)] = ref[at, :rows, cols:]
            vecs[:, pl.ds(high, rows)] = ref[at, rows:, :rows].astype(F32)
        if live:
            heads = cols // (3 * HD)
            for head in range(heads):
                at = info[0] * heads + head
                col = pl.ds(pl.multiple_of(lax.div(at, 2) * rows, rows), rows)
                row = vecs[0:8, col][2 + head % 2 : 3 + head % 2]
                pieces = [row[:, :HD], jnp.zeros((1, HD), F32), row[:, HD:]]
                jbias[:, head * 3 * HD : (head + 1) * 3 * HD] = jnp.concatenate(pieces, 1)
        else:
            jbias[...] = jbias_in[...]

    for rel in range(ns):

        @pl.when(lax.div(step, nt) == rel)
        def _():
            unit, _ = norm_parts(xs[rel][...].astype(F32))
            value = (unit * vecs[0:1] + vecs[1:2]).astype(BF)
            normed[...] = value
            joined[...] = (dg(value, full[...], NN) + jbias[...]).astype(BF)


def first_call(info, jbias, xs, weights, cols, live):
    ns = len(xs)
    tok, dim = xs[0].shape
    nb = sum(weight.shape[0] for weight in weights)
    rows = dim // nb
    cw = weights[0].shape[2] - cols
    tile = min(256, tok)
    nt = tok // tile
    extra = [] if live else [jbias]
    place = lambda i, info: ((info[0] ^ lax.div(i, nt)) * nt + lax.rem(i, nt), 0)

    def source(rel):
        return pl.BlockSpec((tile, dim), lambda i, info: (jnp.clip(i - rel * nt, 0, nt - 1), 0))

    return pl.pallas_call(
        functools.partial(first_kernel, ns, nt, nb, rows, cols, live),
        grid_spec=pltpu.PrefetchScalarGridSpec(
            num_scalar_prefetch=1,
            grid=(ns * nt,),
            in_specs=[once(value.shape) for value in extra]
            + [source(rel) for rel in range(ns)]
            + [once(weight.shape) for weight in weights],
            out_specs=[
                pl.BlockSpec((tile, dim), place),
                pl.BlockSpec((tile, cols), place),
                once((dim, cols)),
                once((dim, cw)),
                once((16, dim)),
            ],
            scratch_shapes=[pltpu.VMEM((1, cols), F32)],
        ),
        out_shape=[
            jax.ShapeDtypeStruct((ns * tok, dim), BF),
            jax.ShapeDtypeStruct((ns * tok, cols), BF),
            jax.ShapeDtypeStruct((dim, cols), BF),
            jax.ShapeDtypeStruct((dim, cw), BF),
            jax.ShapeDtypeStruct((16, dim), F32),
        ],
        compiler_params=params(60),
        cost_estimate=cost(2 * ns * tok * dim * cols, 2 * ns * tok * (2 * dim + cols)),
        name="first",
    )(info, *extra, *xs, *weights)


def three(value):
    high = value.astype(BF)
    rest = value - high.astype(F32)
    mid = rest.astype(BF)
    return high, mid, (rest - mid.astype(F32)).astype(BF)


def spread(lane, base, columns):
    for at, column in columns:
        base = jnp.where(lane == at, column.astype(F32), base)
    return base.astype(BF)


def key_extra(count, slope, length):
    lane = lax.broadcasted_iota(jnp.int32, (count, HD), 1)
    pos = lax.broadcasted_iota(jnp.int32, (count, HD), 0)
    high, mid, low = three(slope * pos.astype(F32))
    dead = jnp.where(pos < length, 0.0, -1e30)
    return spread(lane, jnp.where(lane < 7, 1.0, 0.0), [(0, high), (1, mid), (2, low), (3, dead)])


def attend_kernel(count, size, pair, info, slopes, joined, mixed, sums, keys):
    lane = lax.broadcasted_iota(jnp.int32, (size, HD), 1)
    ones = jnp.where(lane < 4, 1.0, 0.0).astype(BF)
    for hh in range(2):
        base = 3 * HD * hh
        extra = key_extra(count, slopes[2 * pair + hh], info[1])
        keys[hh] = jnp.concatenate([joined[:, base + HD : base + 2 * HD], extra], 1)
    query_at = lax.broadcasted_iota(jnp.int32, (size, size), 0)
    key_at = lax.broadcasted_iota(jnp.int32, (size, size), 1)
    for block in range(count // size):
        low = block * size
        high = low + size
        outs = []
        logs = []
        for hh in range(2):
            base = 3 * HD * hh
            query = (joined[low:high, base : base + HD].astype(F32) * 0.125).astype(BF)
            query = jnp.concatenate([query, ones], 1)
            near = jnp.where(key_at <= query_at, dg(query, keys[hh, low:high], NT), -1e30)
            top = jnp.max(near, axis=1, keepdims=True)
            if block:
                far = dg(query, keys[hh, 0:low], NT)
                top = jnp.maximum(top, jnp.max(far, axis=1, keepdims=True))
            near = jnp.exp(near - top)
            total = jnp.sum(near, axis=1, keepdims=True)
            acc = dg(near.astype(BF), joined[low:high, base + 2 * HD : base + 3 * HD], NN)
            if block:
                far = jnp.exp(far - top)
                total += jnp.sum(far, axis=1, keepdims=True)
                acc += dg(far.astype(BF), joined[0:low, base + 2 * HD : base + 3 * HD], NN)
            outs.append(acc / total)
            logs.append(jnp.broadcast_to(top + jnp.log(total), (size, HD)))
        mixed[low:high] = jnp.concatenate(outs, 1).astype(BF)
        sums[low:high] = jnp.concatenate(logs, 1)


def attend(joined, info, slopes, pair):
    count = joined.shape[0]
    smem = pl.BlockSpec(memory_space=pltpu.SMEM)
    area = count * count
    return pl.pallas_call(
        functools.partial(attend_kernel, count, min(512, count), pair),
        grid=(1,),
        in_specs=[smem, smem, pl.BlockSpec((count, 6 * HD), lambda i: (0, pair))],
        out_specs=[pl.BlockSpec((count, 2 * HD), lambda i: (0, 0))] * 2,
        out_shape=[
            jax.ShapeDtypeStruct((count, 2 * HD), BF),
            jax.ShapeDtypeStruct((count, 2 * HD), F32),
        ],
        scratch_shapes=[pltpu.VMEM((2, count, 2 * HD), BF)],
        compiler_params=params(60),
        cost_estimate=cost(area * 1024, 20 * count * HD, area),
        name="attend",
    )(info, slopes, joined)


def attend_back_kernel(count, size, ns, pair, info, slopes, joined, mixed, sums, *refs):
    pieces_in = refs[:ns]
    out, sides, keys, queries, values, grads, query_grad = refs[ns:]
    tok = count // ns
    lane = lax.broadcasted_iota(jnp.int32, (count, HD), 1)
    near_lane = lax.broadcasted_iota(jnp.int32, (tok, HD), 1)
    for hh in range(2):
        base = 3 * HD * hh
        half = slice(hh * HD, (hh + 1) * HD)
        extra = key_extra(count, slopes[2 * pair + hh], info[1])
        keys[hh] = jnp.concatenate([joined[:, base + HD : base + 2 * HD], extra], 1)
        query = (joined[:, base : base + HD].astype(F32) * 0.125).astype(BF)
        high, mid, low = three(-sums[:, half])
        extra = spread(lane, jnp.where(lane < 4, 1.0, 0.0), [(4, high), (5, mid), (6, low)])
        queries[hh] = jnp.concatenate([query, extra], 1)
        ones = jnp.where(lane < 3, 1.0, 0.0).astype(BF)
        values[hh] = jnp.concatenate([joined[:, base + 2 * HD : base + 3 * HD], ones], 1)
        for rel in range(ns):
            at = pl.ds(pl.multiple_of((info[0] ^ rel) * tok, tok), tok)
            part = pieces_in[rel][:, half]
            inner = jnp.sum(part.astype(F32) * mixed[at, half].astype(F32), axis=1, keepdims=True)
            high, mid, low = three(jnp.broadcast_to(-inner, (tok, HD)))
            extra = spread(near_lane, jnp.zeros((tok, HD), F32), [(0, high), (1, mid), (2, low)])
            grads[hh, at] = jnp.concatenate([part, extra], 1)
    key_at = lax.broadcasted_iota(jnp.int32, (size, size), 0)
    query_at = lax.broadcasted_iota(jnp.int32, (size, size), 1)
    blocks = count // size
    for j in range(blocks):
        ks = slice(j * size, (j + 1) * size)
        pieces = []
        for hh in range(2):
            key_sum = None
            for i in range(j, blocks):
                qs = slice(i * size, (i + 1) * size)
                probs = jnp.exp(dg(keys[hh, ks], queries[hh, qs], NT))
                if i == j:
                    probs = jnp.where(key_at <= query_at, probs, 0.0)
                slope = (probs * dg(values[hh, ks], grads[hh, qs], NT)).astype(BF)
                value_part = dg(probs.astype(BF), grads[hh, qs], NN)
                key_part = dg(slope, queries[hh, qs], NN)
                query_part = dg(keys[hh, ks], slope, TN)
                value_sum = value_part if key_sum is None else value_sum + value_part
                key_sum = key_part if key_sum is None else key_sum + key_part
                query_grad[hh, :, qs] = query_part if j == 0 else query_grad[hh, :, qs] + query_part
            pieces += [jnp.zeros((size, HD), F32), key_sum[:, :HD], value_sum[:, :HD]]
        out[ks] = jnp.concatenate(pieces, 1).astype(BF)
    for hh in range(2):
        base = 3 * HD * hh
        out[:, base : base + HD] = (query_grad[hh].T[:, :HD] * 0.125).astype(BF)
    sides[...] = jnp.sum(out[...].astype(F32), axis=0, keepdims=True)


def attend_back(joined, grads, mixed, sums, info, slopes, pair):
    count = joined.shape[0]
    ns = len(grads)
    smem = pl.BlockSpec(memory_space=pltpu.SMEM)
    wide = pl.BlockSpec((count, 6 * HD), lambda i: (0, pair))
    narrow = pl.BlockSpec((count, 2 * HD), lambda i: (0, 0))
    piece = pl.BlockSpec((count // ns, 2 * HD), lambda i: (0, pair))
    area = count * count
    return pl.pallas_call(
        functools.partial(attend_back_kernel, count, min(512, count), ns, pair),
        grid=(1,),
        in_specs=[smem, smem, wide, narrow, narrow] + [piece] * ns,
        out_specs=[pl.BlockSpec((count, 6 * HD), lambda i: (0, 0)), pl.BlockSpec((1, 6 * HD), lambda i: (0, 0))],
        out_shape=[jax.ShapeDtypeStruct((count, 6 * HD), BF), jax.ShapeDtypeStruct((1, 6 * HD), F32)],
        scratch_shapes=[pltpu.VMEM((2, count, 2 * HD), BF)] * 4 + [pltpu.VMEM((2, 2 * HD, count), F32)],
        compiler_params=params(60),
        cost_estimate=cost(area * 2560, 40 * count * HD, area),
        name="attend_back",
    )(info, slopes, joined, mixed, sums, *grads)


def middle_kernel(ns, np, info, x, vecs, *refs):
    mixed, weights = refs[: ns * np], refs[ns * np : ns * np + ns]
    merged, resid, second, full = refs[ns * np + ns :]
    cw = weights[0].shape[1]
    pw = cw // np

    @pl.when(pl.program_id(0) == 0)
    def _():
        for rel in range(ns):
            full[:, pl.ds(pl.multiple_of((info[0] ^ rel) * cw, cw), cw)] = weights[rel][...]

    for pair in range(np):
        for rel in range(ns):
            col = pl.ds(pl.multiple_of((info[0] ^ rel) * cw + pair * pw, pw), pw)
            merged[:, col] = mixed[pair * ns + rel][...]
    value = x[...].astype(F32) + dg(merged[...], full[...], NN) + vecs[4:5]
    resid[...] = value
    unit, _ = norm_parts(value)
    second[...] = (unit * vecs[5:6] + vecs[6:7]).astype(BF)


def middle_call(info, x, vecs, mixed, weights):
    tok, dim = x.shape
    ns = len(weights)
    np = len(mixed) // ns
    tile = min(256, tok)
    part = lambda width: pl.BlockSpec((tile, width), lambda i, info: (i, 0))
    return pl.pallas_call(
        functools.partial(middle_kernel, ns, np),
        grid_spec=pltpu.PrefetchScalarGridSpec(
            num_scalar_prefetch=1,
            grid=(tok // tile,),
            in_specs=[part(dim), once(vecs.shape)]
            + [part(block.shape[1]) for block in mixed]
            + [once(weight.shape) for weight in weights],
            out_specs=[part(dim), part(dim), part(dim), once((dim, dim))],
        ),
        out_shape=[
            jax.ShapeDtypeStruct((tok, dim), BF),
            jax.ShapeDtypeStruct((tok, dim), F32),
            jax.ShapeDtypeStruct((tok, dim), BF),
            jax.ShapeDtypeStruct((dim, dim), BF),
        ],
        compiler_params=params(60),
        cost_estimate=cost(2 * tok * dim * dim, 12 * tok * dim + 4 * dim * dim),
        name="middle",
    )(info, x, vecs, *mixed, *weights)


def feed_kernel(nt, nb, rows, units, live, info, sa, sb, ca, cb, ebias, *refs):
    weights = refs[:-9]
    activ, pre_grad, oa, ob, ba, bb, bgrad, wide, tall = refs[-9:]
    step = pl.program_id(0)

    @pl.when(step == 0)
    def _():
        blocks = blocks_of(weights)
        for slot in range(nb):
            owner = owner_at(info, live, nb, slot)
            high = pl.multiple_of(owner * rows, rows) if live else owner * rows
            deep = pl.multiple_of(owner * units, units) if live else owner * units
            if len(blocks) == nb:
                ref, at = blocks[slot]
                wide[pl.ds(high, rows)] = ref[at, :rows]
                tall[pl.ds(deep, units)] = ref[at, rows:]
            else:
                wide[pl.ds(high, rows)] = weights[0][slot]
                tall[pl.ds(deep, units)] = weights[1][slot]
        bgrad[...] = jnp.zeros_like(bgrad)

    def work(second, cot, out, back):
        pre = dg(second[...], wide[...], NN) + ebias[...]
        square = pre * pre
        bend = jnp.tanh(0.7978845608028654 * pre * (1.0 + 0.044715 * square))
        half = 0.5 + 0.5 * bend
        act = (pre * half).astype(BF)
        activ[...] = act
        out[...] = dg(act, tall[...], NN).astype(BF)
        steep = half + pre * (0.5 - 0.5 * bend * bend) * (0.7978845608028654 + 0.10703222440890037 * square)
        grad = (dg(cot[...], tall[...], NT) * steep).astype(BF)
        pre_grad[...] = grad
        bgrad[...] += jnp.sum(grad.astype(F32), axis=0, keepdims=True)
        back[...] = dg(grad, wide[...], NT).astype(BF)

    @pl.when(step < nt)
    def _():
        work(sa, ca, oa, ba)

    @pl.when(step >= nt)
    def _():
        work(sb, cb, ob, bb)


def feed_call(info, sa, sb, ca, cb, ebias, weights, rows, units, nb, live):
    tok, dim = sa.shape
    ff = ebias.shape[1]
    tile = min(256, tok)
    nt = tok // tile
    left = pl.BlockSpec((tile, dim), lambda i, info: (jnp.minimum(i, nt - 1), 0))
    right = pl.BlockSpec((tile, dim), lambda i, info: (jnp.maximum(i - nt, 0), 0))
    flat = pl.BlockSpec((tile, ff), lambda i, info: (i, 0))
    shape = jax.ShapeDtypeStruct((tok, dim), BF)
    return pl.pallas_call(
        functools.partial(feed_kernel, nt, nb, rows, units, live),
        grid_spec=pltpu.PrefetchScalarGridSpec(
            num_scalar_prefetch=1,
            grid=(2 * nt,),
            in_specs=[left, right, left, right, once(ebias.shape)] + [once(weight.shape) for weight in weights],
            out_specs=[flat, flat, left, right, left, right, pl.BlockSpec((1, ff), lambda i, info: (0, 0))],
            scratch_shapes=[pltpu.VMEM((dim, ff), BF), pltpu.VMEM((ff, dim), BF)],
        ),
        out_shape=[jax.ShapeDtypeStruct((2 * tok, ff), BF)] * 2
        + [shape] * 4
        + [jax.ShapeDtypeStruct((1, ff), F32)],
        compiler_params=params(60),
        cost_estimate=cost(16 * tok * dim * ff, 16 * tok * dim + 8 * dim * ff, 2 * tok * ff),
        name="feed",
    )(info, sa, sb, ca, cb, ebias, *weights)


def feed_grad_kernel(ns, nb, rows, units, steps, info, *refs):
    half = ns // 2
    activs, cots, seconds, grads = refs[:half], refs[half : half + ns], refs[half + ns : half + 2 * ns], refs[half + 2 * ns : 2 * half + 2 * ns]
    outs = refs[2 * half + 2 * ns :]
    step = pl.program_id(0)

    def total(wides, thins, wide_left):
        out = None
        for rel in range(ns):
            thin = thins[rel]
            tok = thin.shape[0]
            wide = wides[rel // 2][(rel % 2) * tok : (rel % 2 + 1) * tok]
            term = dg(wide, thin[...], TN) if wide_left else dg(thin[...], wide, TN)
            out = term if out is None else out + term
        return out.astype(BF)

    def store(value, high, count, at, low):
        for k in range(value.shape[0] // count):
            slot = info[2 + at * (value.shape[0] // count) + k]
            piece = value[k * count : (k + 1) * count]
            if len(outs) == nb:
                for mine, out in enumerate(outs):

                    @pl.when(slot == mine)
                    def _():
                        out[0, low : low + count] = piece

            else:
                outs[0 if high else 1][slot] = piece

    @pl.when(step < steps)
    def _():
        store(total(activs, cots, True), False, units, step, rows)

    @pl.when(step >= steps)
    def _():
        store(total(grads, seconds, False), True, rows, step - steps, 0)


def feed_grad_call(info, activs, cots, seconds, grads, nb, live):
    ns = len(cots)
    dim = cots[0].shape[1]
    ff = activs[0].shape[1]
    rows, units = dim // nb, ff // nb
    tile = 256
    steps = ff // tile
    tok = ns * cots[0].shape[0]
    left = lambda a: pl.BlockSpec((a.shape[0], tile), lambda i, info: (0, jnp.minimum(i, steps - 1)))
    right = lambda a: pl.BlockSpec((a.shape[0], tile), lambda i, info: (0, jnp.maximum(i - steps, 0)))
    fixed = lambda a: once(a.shape)
    shapes = [(1, rows + units, dim)] * nb if live else [(nb, rows, ff), (nb, units, dim)]
    return pl.pallas_call(
        functools.partial(feed_grad_kernel, ns, nb, rows, units, steps),
        grid_spec=pltpu.PrefetchScalarGridSpec(
            num_scalar_prefetch=1,
            grid=(steps + dim // tile,),
            in_specs=[left(a) for a in activs]
            + [fixed(a) for a in cots]
            + [right(a) for a in seconds]
            + [fixed(a) for a in grads],
            out_specs=[once(shape) for shape in shapes],
        ),
        out_shape=[jax.ShapeDtypeStruct(shape, BF) for shape in shapes],
        compiler_params=params(60),
        cost_estimate=cost(4 * tok * dim * ff, 4 * tok * (dim + ff) + 4 * dim * ff),
        name="feed_grad",
    )(info, *activs, *cots, *seconds, *grads)


def pair_shapes(shape, ns):
    return [shape, shape, (2, *shape)] if ns == 4 else [shape] * ns


def pair_put(outs, ns, rel, rows, value):
    if ns == 4 and rel % 2:
        outs[2][rel // 2, rows] = value
    elif ns == 4:
        outs[rel // 2][rows] = value
    else:
        outs[rel][rows] = value


def split_grad_kernel(ns, info, left, right, *refs):
    outs, held = refs[:-1], refs[-1]
    held[...] = dg(left[...], right[...], TN)
    tile = held.shape[0]
    cw = held.shape[1] // ns
    rows = pl.ds(pl.multiple_of(pl.program_id(0) * tile, tile), tile)
    for rel in range(ns):
        col = pl.ds(pl.multiple_of((info[0] ^ rel) * cw, cw), cw)
        pair_put(outs, ns, rel, rows, held[:, col].astype(BF))


def split_grad(info, left, right, ns):
    tok, dim = left.shape
    tile = 256
    shapes = pair_shapes((dim, dim // ns), ns)
    return pl.pallas_call(
        functools.partial(split_grad_kernel, ns),
        grid_spec=pltpu.PrefetchScalarGridSpec(
            num_scalar_prefetch=1,
            grid=(dim // tile,),
            in_specs=[pl.BlockSpec((tok, tile), lambda i, info: (0, i)), once((tok, dim))],
            out_specs=[once(shape) for shape in shapes],
            scratch_shapes=[pltpu.VMEM((tile, dim), F32)],
        ),
        out_shape=[jax.ShapeDtypeStruct(shape, BF) for shape in shapes],
        compiler_params=params(60),
        cost_estimate=cost(2 * tok * dim * dim, 6 * dim * dim),
        name="split_grad",
    )(info, left, right)


def joined_grad_kernel(nb, rows, np, live, info, left, other, weight, vecs, *refs):
    smalls, refs = (refs[:3], refs[3:]) if live else (refs[:1], refs[1:])
    rights, sides, outs = refs[:np], refs[np : 2 * np], refs[2 * np :]
    totals = [dg(left[...], right[...], TN) for right in rights]
    tile, cw = other.shape
    cols = weight.shape[1]
    first = pl.program_id(0) * (tile // rows)
    low = jnp.concatenate(totals, 1).astype(BF)
    weights = weight[...].astype(F32)
    moment = jnp.sum(jnp.concatenate(totals, 1) * weights, axis=1, keepdims=True)
    shift = jnp.sum(jnp.concatenate([side[...] for side in sides], 1) * weights, axis=1, keepdims=True)
    moment = jnp.broadcast_to(moment, (tile, 128)).T[:1]
    shift = jnp.broadcast_to(shift, (tile, 128)).T[:1]
    gain = (moment - vecs[1:2] * shift) / vecs[0:1]
    row = lax.broadcasted_iota(jnp.int32, (16, tile), 0)
    held = jnp.zeros((16, tile), F32) if live else smalls[0][...]
    held = jnp.where(row == 0, gain, jnp.where(row == 1, shift, held))
    if live:
        turned = smalls[0][...]
        for at, source in ((4, 2), (5, 0), (6, 1), (11, 3)):
            held = jnp.where(row == at, turned[source : source + 1], held)
        held = jnp.where(row == 7 + info[0], smalls[1][...] + smalls[2][...], held)
        for part in range(2):
            pieces = []
            for side in sides:
                base = part * 3 * HD
                pieces += [side[:, base : base + HD], side[:, base + 2 * HD : base + 3 * HD]]
            bias = jnp.where(pl.program_id(0) == info[0], jnp.concatenate(pieces, 1), 0.0)
            held = jnp.where(row == 2 + part, bias, held)
    held = held.astype(BF)
    for k in range(tile // rows):
        slot = info[2 + first + k]
        high = slice(k * rows, (k + 1) * rows)
        put(outs, slot, low[high], slice(0, rows), slice(0, cols))
        put(outs, slot, other[high], slice(0, rows), slice(cols, cols + cw))
        put(outs, slot, held[:, high], slice(rows, rows + 16), slice(0, rows))


def joined_grad_call(info, left, rights, sides, other, weight, vecs, shares, turned, biases, nb, live):
    count, dim = left.shape
    cols = weight.shape[1]
    cw = other.shape[1]
    rows = dim // nb
    tile = 256
    wide = (rows + 16, cols + cw)
    shapes = [(1, *wide)] * nb if live else [(nb, *wide)]
    flat = lambda width: pl.BlockSpec((tile, width), lambda i, info: (i, 0))
    tall = lambda value: pl.BlockSpec((value.shape[0], tile), lambda i, info: (0, i))
    smalls = (turned, *biases) if live else (shares,)
    return pl.pallas_call(
        functools.partial(joined_grad_kernel, nb, rows, len(rights), live),
        grid_spec=pltpu.PrefetchScalarGridSpec(
            num_scalar_prefetch=1,
            grid=(dim // tile,),
            in_specs=[pl.BlockSpec((count, tile), lambda i, info: (0, i)), flat(cw), flat(cols), tall(vecs)]
            + [tall(value) for value in smalls]
            + [once(value.shape) for value in (*rights, *sides)],
            out_specs=[once(shape) for shape in shapes],
        ),
        out_shape=[jax.ShapeDtypeStruct(shape, BF) for shape in shapes],
        compiler_params=params(60),
        cost_estimate=cost(2 * count * dim * cols, 2 * count * (dim + cols) + 4 * dim * dim),
        name="joined_grad",
    )(info, left, other, weight, vecs, *smalls, *rights, *sides)


def turn_kernel(ns, np, cw, info, ga, gb, gc, resid, cot, vecs, full, resid_grad, branch, *refs):
    mixed_grads, sums, held = refs[: ns * np], refs[ns * np], refs[ns * np + 1]

    @pl.when(pl.program_id(0) == 0)
    def _():
        sums[...] = jnp.zeros_like(sums)

    grad = ga[...].astype(F32) + gb[...].astype(F32) + gc[...].astype(F32)
    unit, scale = norm_parts(resid[...])
    outer = cot[...].astype(F32)
    value = outer + norm_back(grad, unit, scale, vecs[5:6])
    resid_grad[...] = value
    low = value.astype(BF)
    branch[...] = low
    held[...] = dg(low, full[...], NT).astype(BF)
    pw = cw // np
    for pair in range(np):
        for rel in range(ns):
            col = pl.ds(pl.multiple_of((info[0] ^ rel) * cw + pair * pw, pw), pw)
            mixed_grads[pair * ns + rel][...] = held[:, col]
    for at, term in enumerate((grad * unit, grad, low.astype(F32), outer)):
        sums[at : at + 1] += jnp.sum(term, axis=0, keepdims=True)


def turn_call(info, terms, resid, cot, vecs, full, ns, np):
    tok, dim = resid.shape
    cw = dim // ns
    tile = min(256, tok)
    part = pl.BlockSpec((tile, dim), lambda i, info: (i, 0))
    return pl.pallas_call(
        functools.partial(turn_kernel, ns, np, cw),
        grid_spec=pltpu.PrefetchScalarGridSpec(
            num_scalar_prefetch=1,
            grid=(tok // tile,),
            in_specs=[part, part, part, part, part, once(vecs.shape), once(full.shape)],
            out_specs=[part, part]
            + [pl.BlockSpec((tile, cw // np), lambda i, info: (i, 0))] * (ns * np)
            + [pl.BlockSpec((8, dim), lambda i, info: (0, 0))],
            scratch_shapes=[pltpu.VMEM((tile, dim), BF)],
        ),
        out_shape=[
            jax.ShapeDtypeStruct((tok, dim), F32),
            jax.ShapeDtypeStruct((tok, dim), BF),
        ]
        + [jax.ShapeDtypeStruct((tok, cw // np), BF)] * (ns * np)
        + [jax.ShapeDtypeStruct((8, dim), F32)],
        compiler_params=params(60),
        cost_estimate=cost(2 * tok * dim * dim, 16 * tok * dim + 2 * dim * dim),
        name="turn",
    )(info, *terms, resid, cot, vecs, full)


def last_kernel(ns, nt, np, info, weight, *refs):
    rights, outs = refs[:np], refs[np:]
    step = pl.program_id(0)
    grad = None
    at = 0
    for right in rights:
        width = right.shape[1]
        term = dg(right[...], weight[:, at : at + width], NT)
        grad = term if grad is None else grad + term
        at += width
    low = grad.astype(BF)
    tile = low.shape[0]
    rows = pl.ds(pl.multiple_of(lax.rem(step, nt) * tile, tile), tile)
    for rel in range(ns):

        @pl.when(ns - 1 - lax.div(step, nt) == rel)
        def _():
            pair_put(outs, ns, rel, rows, low)


def last_call(info, rights, weight, ns):
    count = rights[0].shape[0]
    dim, cols = weight.shape
    tok = count // ns
    tile = min(256, tok)
    nt = tok // tile
    source = lambda i, info: ((info[0] ^ (ns - 1 - lax.div(i, nt))) * nt + lax.rem(i, nt), 0)
    shapes = pair_shapes((tok, dim), ns)
    return pl.pallas_call(
        functools.partial(last_kernel, ns, nt, len(rights)),
        grid_spec=pltpu.PrefetchScalarGridSpec(
            num_scalar_prefetch=1,
            grid=(ns * nt,),
            in_specs=[once(weight.shape)] + [pl.BlockSpec((tile, right.shape[1]), source) for right in rights],
            out_specs=[once(shape) for shape in shapes],
        ),
        out_shape=[jax.ShapeDtypeStruct(shape, BF) for shape in shapes],
        compiler_params=params(60),
        cost_estimate=cost(2 * count * dim * cols, 2 * count * (2 * dim + cols)),
        name="last",
    )(info, weight, *rights)


def end_kernel(ga, gb, gc, x, resid_grad, vecs, out):
    grad = ga[...].astype(F32) + gb[...].astype(F32) + gc[...].astype(F32)
    unit, scale = norm_parts(x[...].astype(F32))
    out[...] = resid_grad[...] + norm_back(grad, unit, scale, vecs[0:1])


def end_call(terms, x, resid_grad, vecs):
    tok, dim = x.shape
    tile = min(128, tok)
    part = pl.BlockSpec((tile, dim), lambda i: (i, 0))
    head = pl.BlockSpec((None, tile, dim), lambda i: (0, i, 0))
    return pl.pallas_call(
        end_kernel,
        grid=(tok // tile,),
        in_specs=[head if term.ndim == 3 else part for term in terms]
        + [part, part, pl.BlockSpec(vecs.shape, lambda i: (0, 0))],
        out_specs=part,
        out_shape=jax.ShapeDtypeStruct((tok, dim), F32),
        compiler_params=params(40),
        cost_estimate=cost(20 * tok * dim, 14 * tok * dim),
        name="end",
    )(*terms, x, resid_grad, vecs)


def add_pairs_kernel(count, *refs):
    for at in range(count):
        left, right, out = refs[at], refs[count + at], refs[2 * count + at]
        out[...] = (left[...].astype(F32) + right[...].astype(F32)).astype(BF)


def add_pairs(lefts, rights):
    count = len(lefts)
    return pl.pallas_call(
        functools.partial(add_pairs_kernel, count),
        in_specs=[pl.BlockSpec(memory_space=pltpu.VMEM)] * (2 * count),
        out_specs=[pl.BlockSpec(memory_space=pltpu.VMEM)] * count,
        out_shape=[jax.ShapeDtypeStruct(left.shape, BF) for left in lefts],
        compiler_params=params(20),
        cost_estimate=cost(1, 1),
        name="add_pairs",
    )(*lefts, *rights)


def joined_out_kernel(ns, cols, info, *refs):
    parts, joined, outw, smalls = refs[:ns], refs[ns], refs[ns + 1], refs[ns + 2 :]
    rows = joined.shape[0]
    cw = parts[0].shape[1] - cols
    total = None
    for rel in range(ns):
        part = parts[rel]
        joined[:, pl.ds(pl.multiple_of((info[0] ^ rel) * cols, cols), cols)] = part[:rows, :cols].astype(F32)
        outw[:, pl.ds(pl.multiple_of((info[0] ^ rel) * cw, cw), cw)] = part[:rows, cols:].astype(F32)
        term = part[rows:, :rows].astype(F32)
        total = term if total is None else total + term
    at = 0
    for small in smalls:
        for row in range(small.shape[0]):
            small[row : row + 1] = total[at + row : at + row + 1]
        at += small.shape[0]


def joined_out(info, parts, cols):
    ns = len(parts)
    high, wide = parts[0].shape
    rows = high - 16
    shapes = [(rows, ns * cols), (rows, ns * (wide - cols))]
    shapes += [(count, rows) for count in (1, 1, 2, 1, 1, 1, 4, 1)]
    return pl.pallas_call(
        functools.partial(joined_out_kernel, ns, cols),
        grid_spec=pltpu.PrefetchScalarGridSpec(
            num_scalar_prefetch=1,
            grid=(1,),
            in_specs=[once(part.shape) for part in parts],
            out_specs=[once(shape) for shape in shapes],
        ),
        out_shape=[jax.ShapeDtypeStruct(shape, F32) for shape in shapes],
        compiler_params=params(60),
        cost_estimate=cost(0, 6 * ns * rows * wide),
        name="joined_out",
    )(info, *parts)


def feed_out_kernel(ns, nb, rows, units, info, *refs):
    parts, expand, shrink = refs[:ns], refs[ns], refs[ns + 1]
    for rel in range(ns):
        seat = info[0] ^ rel
        shrink[pl.ds(pl.multiple_of(seat * units, units), units)] = parts[rel][rows:].astype(F32)
        for k in range(nb):
            col = pl.ds(pl.multiple_of((k * ns + seat) * units, units), units)
            expand[:, col] = parts[rel][:rows, k * units : (k + 1) * units].astype(F32)


def feed_out(info, parts, nb, rows):
    ns = len(parts)
    high, dim = parts[0].shape
    units = high - rows
    shapes = [(rows, ns * units * nb), (ns * units, dim)]
    return pl.pallas_call(
        functools.partial(feed_out_kernel, ns, nb, rows, units),
        grid_spec=pltpu.PrefetchScalarGridSpec(
            num_scalar_prefetch=1,
            grid=(1,),
            in_specs=[once(part.shape) for part in parts],
            out_specs=[once(shape) for shape in shapes],
        ),
        out_shape=[jax.ShapeDtypeStruct(shape, F32) for shape in shapes],
        compiler_params=params(60),
        cost_estimate=cost(0, 6 * ns * high * dim),
        name="feed_out",
    )(info, *parts)


def body(
    layer_input,
    lengths,
    first_gain,
    first_shift,
    joined_weight,
    joined_bias,
    output_weight,
    output_bias,
    second_gain,
    second_shift,
    expand_weight,
    expand_bias,
    shrink_weight,
    shrink_bias,
    out_grad,
):
    ns = lax.axis_size("seq")
    nb = lax.axis_size("batch")
    si = lax.axis_index("seq")
    bi = lax.axis_index("batch")
    tok = layer_input.shape[1]
    dim = layer_input.shape[2]
    heads = H // ns
    np = heads // 2
    cols = 3 * HD * heads
    cw = HD * heads
    rows = dim // nb
    ff = expand_weight.shape[1] // ns
    units = ff // nb
    x = layer_input[0]
    cot = out_grad[0]
    live = ns == 4 and nb == 8
    ring = Ring(nb, bi, live)
    info = jnp.concatenate([jnp.stack([si, lengths[0]]), ring.table()]).astype(jnp.int32)
    head_ids = si * heads + jnp.arange(heads, dtype=jnp.int32) + 1
    slopes = 2.0 ** (-8.0 * head_ids.astype(F32) / H)

    smalls = (first_gain, first_shift, joined_bias, output_bias, second_gain, second_shift, expand_bias, shrink_bias)
    smalls = [small.reshape(-1, rows) for small in smalls]
    seat = si.reshape(1).astype(jnp.int32)
    one = first_pack(seat, joined_weight, output_weight, smalls, cols, cw)
    jbias = None

    def step(held, t):
        if t < ring.half:
            held[t] = ring.back(held[t - 1])
        held[nb - t] = ring.ahead(held[(nb - t + 1) % nb])

    if live:
        x, cot, one = tie(x, cot, one)
        ones = {0: one}
        step(ones, 1)
        xs = {0: x, 1: lax.ppermute(x, "seq", pairs(ns, 1)), 2: lax.ppermute(x, "seq", pairs(ns, 2))}
        expand_weight, shrink_weight, _ = tie(expand_weight, shrink_weight, one)
        two = second_pack(seat, expand_weight, shrink_weight, nb, ns)
        ones[1], ones[7], two, xs[1], cot = tie(ones[1], ones[7], two, xs[1], cot)
        step(ones, 2)
        cots = {0: cot, 1: lax.ppermute(cot, "seq", pairs(ns, 1))}
        ones[2], ones[6], cots[1], xs[2], cot = tie(ones[2], ones[6], cots[1], xs[2], cot)
        step(ones, 3)
        xs[3] = lax.ppermute(xs[2], "seq", pairs(ns, 1))
        cots[2] = lax.ppermute(cot, "seq", pairs(ns, 2))
        ones[3], ones[5], xs[3] = tie(ones[3], ones[5], xs[3])
        step(ones, 4)
        ones[4], two = tie(ones[4], two)
        twos = {0: two}
        step(twos, 1)
        one_parts = [ones[slot][None] for slot in range(nb)]
    else:
        xs = gather_rel(x, "seq", ns)
        cots = gather_rel(cot, "seq", ns)
        one_parts = [lax.all_gather(one, "batch")]
        low = one_parts[0][:, rows + 2 : rows + 4, :rows].astype(F32).reshape(2 * dim)
        low = lax.dynamic_slice(low, (si * 2 * cw,), (2 * cw,)).reshape(heads, 2, HD)
        jbias = jnp.stack([low[:, 0], jnp.zeros_like(low[:, 0]), low[:, 1]], 1).reshape(1, cols)

    normed, joined, joined_full, outw_own, vecs = first_call(
        info, jbias, [xs[rel] for rel in range(ns)], one_parts, cols, live
    )
    if live:
        joined, twos[1], twos[7], cots[2] = tie(joined, twos[1], twos[7], cots[2])
        step(twos, 2)
        cots[3] = lax.ppermute(cots[2], "seq", pairs(ns, 1))
    if units == rows:
        ebias = lax.dynamic_slice(vecs, (7 + si, 0), (1, dim))
    else:
        ebias = vecs[7:11].reshape(4, nb, rows).transpose(1, 0, 2).reshape(nb, ns, units)
        ebias = lax.dynamic_slice(ebias, (0, si, 0), (nb, 1, units)).reshape(1, ff)
    outw_all = gather_rel(outw_own, "seq", ns)
    mixed = []
    log_sums = []
    merged_parts = []

    def to_tokens(out):
        parts = []
        for rel in range(ns):
            block = lax.dynamic_slice(out, ((si ^ rel) * tok, 0), (tok, 2 * HD))
            parts.append(lax.ppermute(block, "seq", pairs(ns, rel)) if rel else block)
        return parts

    for pair in range(np):
        out, logs = attend(joined, info, slopes, pair)
        if live and pair == 0:
            out, joined, twos[2], twos[6], cots[3], outw_all[2], outw_all[1] = tie(
                out, joined, twos[2], twos[6], cots[3], outw_all[2], outw_all[1]
            )
            step(twos, 3)
            outw_all[3] = lax.ppermute(outw_all[2], "seq", pairs(ns, 1))
        mixed.append(out)
        log_sums.append(logs)
        merged_parts.append(to_tokens(out))
        if live and pair == 1:
            out, twos[3], twos[5], outw_all[3], *merged_parts[0] = tie(
                out, twos[3], twos[5], outw_all[3], *merged_parts[0]
            )
            step(twos, 4)
            mixed[1] = out
            merged_parts[1] = to_tokens(out)
    merged_parts = [block for parts in merged_parts for block in parts]
    merged, resid, second, outw_full = middle_call(
        info, x, vecs, merged_parts, [outw_all[rel] for rel in range(ns)]
    )
    if not live:
        expand_part = expand_weight.reshape(rows, nb, ns, units)
        expand_part = lax.dynamic_slice(expand_part, (0, 0, si, 0), (rows, nb, 1, units)).reshape(rows, ff)
        shrink_part = lax.dynamic_slice(shrink_weight, (si * units, 0), (units, dim))
        two_parts = [lax.all_gather(expand_part, "batch"), lax.all_gather(shrink_part, "batch")]
    out_parts = {}
    back_parts = {}
    activs = []
    pre_grads = []
    bias_sums = []
    if live:
        second, twos[4] = tie(second, twos[4])
        two_parts = [twos[slot][None] for slot in range(nb)]
        seconds = {0: second, 2: lax.ppermute(second, "seq", pairs(ns, 2)), 1: lax.ppermute(second, "seq", pairs(ns, 1))}
    else:
        seconds = gather_rel(second, "seq", ns)
    for rel in range(0, ns, 2):
        activ, pre_grad, oa, ob, ba, bb, bgrad = feed_call(
            info, seconds[rel], seconds[rel + 1], cots[rel], cots[rel + 1], ebias, two_parts, rows, units, nb, live
        )
        if live and rel == 0:
            activ, ob, bb, seconds[2] = tie(activ, ob, bb, seconds[2])
            seconds[3] = lax.ppermute(seconds[2], "seq", pairs(ns, 1))
            seconds[2], seconds[3] = tie(seconds[2], seconds[3])
            near_back = lax.ppermute(bb, "seq", pairs(ns, 1))
            near_out = lax.ppermute(ob, "seq", pairs(ns, 1))
        activs.append(activ)
        pre_grads.append(pre_grad)
        bias_sums.append(bgrad)
        out_parts.update({rel: oa, rel + 1: ob})
        back_parts.update({rel: ba, rel + 1: bb})
    if live:
        back_parts[3], near_back, near_out = tie(back_parts[3], near_back, near_out)
        far_back = lax.ppermute(back_parts[3], "seq", pairs(ns, 1))
        far_back, out_far = tie(far_back, out_parts[3])
        back_b = lax.ppermute(add16(back_parts[2], far_back), "seq", pairs(ns, 2))
        far_out = lax.ppermute(out_far, "seq", pairs(ns, 1))
    else:
        back_terms = (*scatter_rel(back_parts, "seq", ns, last=False), jnp.zeros((tok, dim), BF))
        out_a, out_b = scatter_rel(out_parts, "seq", ns, last=False)
    feed_stack = feed_grad_call(
        info,
        activs,
        [cots[rel] for rel in range(ns)],
        [seconds[rel] for rel in range(ns)],
        pre_grads,
        nb,
        live,
    )

    class Scatter:
        def __init__(self, parts):
            self.parts = [part[0] for part in parts]
            self.t = 0
            self.ahead = self.parts[ring.half]
            self.back = self.parts[ring.half + 1]

        def send(self):
            self.t += 1
            self.got_ahead = ring.ahead(self.ahead)
            self.got_back = ring.back(self.back) if self.t > 1 else None

        def take(self, *others):
            both = self.t > 1
            got = (self.got_ahead, self.got_back) if both else (self.got_ahead,)
            tied = tie(*got, *others)
            got, others = tied[: len(got)], tied[len(got) :]
            if self.t == ring.half:
                total = self.parts[0].astype(F32) + got[0].astype(F32) + got[1].astype(F32)
                return (total.astype(BF), *others)
            mine = self.parts[ring.half - self.t]
            if both:
                self.ahead, self.back = add_pairs((mine, self.parts[nb - ring.half + self.t]), got)
            else:
                self.ahead = add16(mine, got[0])
            return others

    if live:
        feed_ring = Scatter(feed_stack)
        feed_ring.send()
        back_b, far_out, _ = tie(back_b, far_out, feed_stack[0])
        back_terms = (back_parts[0], near_back, back_b)
        out_b = add16(out_parts[2], far_out)
    resid_grad, branch, *mixed_grads, turn_sums = turn_call(
        info, back_terms, resid, cot, vecs, outw_full, ns, 1
    )
    outw_parts = split_grad(info, merged, branch, ns)
    joined_grads = []
    sides = []

    grads = [
        lax.ppermute(block, "seq", pairs(ns, rel)) if rel else block for rel, block in enumerate(mixed_grads)
    ]
    if live:
        grads[0], *outw_parts = tie(grads[0], *outw_parts)
        grads = feed_ring.take(*grads)
        *grads, feed_ring.ahead, outw_near = tie(*grads, feed_ring.ahead, outw_parts[2])
        feed_ring.send()
        outw_near = lax.ppermute(outw_near, "seq", pairs(ns, 1))
    for pair in range(np):
        out, side = attend_back(joined, grads, mixed[pair], log_sums[pair], info, slopes, pair)
        joined_grads.append(out)
        sides.append(side)
        if live and pair == 0:
            out, outw_near = feed_ring.take(out, outw_near)
            outw_far = add16(outw_parts[1], outw_near[1])
            out, joined, feed_ring.ahead, feed_ring.back, outw_far = tie(
                out, joined, feed_ring.ahead, feed_ring.back, outw_far
            )
            joined_grads[0] = out
            feed_ring.send()
            outw_far = lax.ppermute(outw_far, "seq", pairs(ns, 2))
        elif live:
            joined_grads[1], outw_far = feed_ring.take(out, outw_far)

    if live:
        shares = None
        outw_share = outw_parts[0].astype(F32) + outw_near[0].astype(F32) + outw_far.astype(F32)
        outw_share = outw_share.astype(BF)
        joined_grads[1], outw_share, feed_ring.ahead, feed_ring.back, out_b = tie(
            joined_grads[1], outw_share, feed_ring.ahead, feed_ring.back, out_b
        )
        feed_ring.send()
        out_b = lax.ppermute(out_b, "seq", pairs(ns, 2))
    else:
        spread_bias = lax.dynamic_update_slice(
            jnp.zeros((nb, ns, units), F32), sum(bias_sums).reshape(nb, 1, units), (0, si, 0)
        )
        spread_bias = spread_bias.reshape(nb, 4, rows).transpose(1, 0, 2).reshape(4, dim)
        side = jnp.concatenate(sides, 1).reshape(heads, 3, HD)
        side = jnp.stack([side[:, 0], side[:, 2]], 1).reshape(2 * cw)
        side = lax.dynamic_update_slice(jnp.zeros((2 * dim,), F32), side, (si * 2 * cw,))
        side = side.reshape(nb, 2, rows).transpose(1, 0, 2).reshape(2, dim)
        none = jnp.zeros((2, dim), F32)
        shares = [none, side, turn_sums[2:3], turn_sums[0:2], spread_bias, turn_sums[3:4], none, none]
        shares = jnp.concatenate(shares, 0)
        outw_share = scatter_rel(dict(enumerate(outw_parts)), "seq", ns)
    joined_stack = joined_grad_call(
        info, normed, joined_grads, sides, outw_share, joined_full, vecs, shares, turn_sums, bias_sums, nb, live
    )
    if live:
        feed_share, *joined_stack = feed_ring.take(*joined_stack)
        feed_share, *joined_stack = tie(feed_share, *joined_stack)
        joined_ring = Scatter(joined_stack)
        joined_ring.send()
        joined_grads[0], _ = tie(joined_grads[0], joined_stack[0])
    normed_parts = last_call(info, joined_grads, joined_full, ns)

    def ordered(block):
        parts = gather_rel(block, "seq", ns)
        return [parts[rel] for rel in range(ns)]

    if live:
        sent, out_b = joined_ring.take(normed_parts[2], out_b)
        joined_ring.ahead, out_b, feed_share, sent = tie(joined_ring.ahead, out_b, feed_share, sent)
        joined_ring.send()
        got = lax.ppermute(sent, "seq", pairs(ns, 1))
        feed_parts = {0: feed_share, 2: lax.ppermute(feed_share, "seq", pairs(ns, 2))}
        out_terms = out_parts[0].astype(F32) + near_out.astype(F32) + out_b.astype(F32)
        layer_output = (resid + out_terms + vecs[11:12]).astype(BF)
        got, feed_parts[2] = joined_ring.take(got, feed_parts[2])
        far = add16(normed_parts[1], got[1])
        joined_ring.ahead, joined_ring.back, far, feed_parts[0], feed_parts[2] = tie(
            joined_ring.ahead, joined_ring.back, far, feed_parts[0], feed_parts[2]
        )
        joined_ring.send()
        norm_b = lax.ppermute(far, "seq", pairs(ns, 2))
        feed_parts[1] = lax.ppermute(feed_parts[0], "seq", pairs(ns, 1))
        feed_parts[1], feed_parts[2], layer_output = joined_ring.take(feed_parts[1], feed_parts[2], layer_output)
        joined_ring.ahead, joined_ring.back, feed_parts[1], feed_parts[2] = tie(
            joined_ring.ahead, joined_ring.back, feed_parts[1], feed_parts[2]
        )
        joined_ring.send()
        feed_parts[3] = lax.ppermute(feed_parts[2], "seq", pairs(ns, 1))
        expand_grad, shrink_grad = feed_out(info, [feed_parts[rel] for rel in range(ns)], nb, rows)
        joined_share, norm_b, expand_grad, shrink_grad = joined_ring.take(norm_b, expand_grad, shrink_grad)
        joined_share, norm_b = tie(joined_share, norm_b)
        joined_parts = {0: joined_share, 2: lax.ppermute(joined_share, "seq", pairs(ns, 2))}
        joined_parts[1] = lax.ppermute(joined_share, "seq", pairs(ns, 1))
        input_grad = end_call((normed_parts[0], got, norm_b), x, resid_grad, vecs)
        joined_parts[2], joined_parts[1], input_grad = tie(joined_parts[2], joined_parts[1], input_grad)
        joined_parts[3] = lax.ppermute(joined_parts[2], "seq", pairs(ns, 1))
        joined_parts = [joined_parts[rel] for rel in range(ns)]
    else:
        layer_output = (resid + out_a.astype(F32) + out_b.astype(F32) + vecs[11:12]).astype(BF)
        norm_terms = scatter_rel(dict(enumerate(normed_parts)), "seq", ns, last=False)
        input_grad = end_call((*norm_terms, jnp.zeros((tok, dim), BF)), x, resid_grad, vecs)
        joined_share = lax.psum_scatter(joined_stack[0], "batch", scatter_dimension=0)
        expand_share = lax.psum_scatter(feed_stack[0], "batch", scatter_dimension=0)
        shrink_share = lax.psum_scatter(feed_stack[1], "batch", scatter_dimension=0)
        seats = jnp.arange(ns, dtype=jnp.int32) ^ si
        shrink_grad = jnp.take(jnp.stack(ordered(shrink_share)), seats, axis=0).astype(F32).reshape(ns * units, dim)
        expand_grad = jnp.take(jnp.stack(ordered(expand_share)), seats, axis=0).astype(F32)
        expand_grad = expand_grad.reshape(ns, rows, nb, units).transpose(1, 2, 0, 3).reshape(rows, ns * ff)
        joined_parts = ordered(joined_share)
    joined_wgrad, outw_grad, *small = joined_out(info, joined_parts, cols)
    small = [value.reshape(-1) for value in small]
    return (
        layer_output[None],
        input_grad[None],
        small[0],
        small[1],
        joined_wgrad,
        small[2],
        outw_grad,
        small[3],
        small[4],
        small[5],
        expand_grad,
        small[6],
        shrink_grad,
        small[7],
    )


def solution(mesh):
    row = P("batch")
    mat = P("batch", None)
    act = P("batch", "seq", None)
    return jax.shard_map(
        body,
        mesh=mesh,
        in_specs=(act, row, row, row, mat, row, mat, row, row, row, mat, row, mat, row, act),
        out_specs=(act, act, row, row, mat, row, mat, row, row, row, mat, row, mat, row),
        check_vma=False,
    )
```

```python
import functools

import jax
import jax.numpy as jnp
from jax import lax
from jax.experimental import pallas as pl
from jax.experimental.pallas import tpu as pltpu
from jax.sharding import PartitionSpec as P

H = 16
HD = 64
EPSILON = 1e-05
F32 = jnp.float32
BF = jnp.bfloat16
NT = (((1,), (1,)), ((), ()))
NN = (((1,), (0,)), ((), ()))
TN = (((0,), (0,)), ((), ()))
MIB = 2**20
SHRINK = 1000


def dg(left, right, dims):
    return lax.dot_general(left, right, dims, preferred_element_type=F32)


def params(limit=56):
    return pltpu.CompilerParams(vmem_limit_bytes=limit * MIB)


def cost(flops, moved, exps=0):
    return pl.CostEstimate(flops=flops // SHRINK, bytes_accessed=moved // SHRINK, transcendentals=exps // SHRINK)


def norm_parts(values):
    mean = jnp.mean(values, axis=-1, keepdims=True)
    centered = values - mean
    scale = lax.rsqrt(jnp.mean(centered * centered, axis=-1, keepdims=True) + EPSILON)
    return centered * scale, scale


def norm_back(grad, unit, scale, gain):
    scaled = grad * gain
    return scale * (
        scaled
        - jnp.mean(scaled, axis=-1, keepdims=True)
        - unit * jnp.mean(scaled * unit, axis=-1, keepdims=True)
    )


def pairs(size, bit):
    return [(i, i ^ bit) for i in range(size)]


def bits_low_last(size):
    bits = []
    bit = 2
    while bit < size:
        bits.append(bit)
        bit *= 2
    if size > 1:
        bits.append(1)
    return bits


def add16(left, right):
    return (left.astype(F32) + right.astype(F32)).astype(BF)


def gather_rel(block, axis, size):
    out = {0: block}
    for bit in bits_low_last(size):
        for rel in list(out):
            out[rel | bit] = lax.ppermute(out[rel], axis, pairs(size, bit))
    return out


def scatter_rel(parts, axis, size, last=True):
    parts = dict(parts)
    order = bits_low_last(size)[::-1]
    for bit in order:
        for rel in sorted(parts, reverse=True):
            if rel & bit:
                other = lax.ppermute(parts.pop(rel), axis, pairs(size, bit))
                if bit == order[-1] and not last:
                    return parts[0], other
                parts[rel ^ bit] = add16(parts[rel ^ bit], other)
    return parts[0]


def tie(*values):
    return lax.optimization_barrier(values)


class Ring:
    def __init__(self, size, index, live):
        self.size = size
        self.live = live
        order = list(range(0, size, 2)) + list(range(size - 1, 0, -2))
        self.forward = [(order[i], order[(i + 1) % size]) for i in range(size)]
        self.backward = [(b, a) for a, b in self.forward]
        count = jnp.arange(size, dtype=jnp.int32)
        place = lambda k: jnp.where(k % 2 == 0, k // 2, size - (k + 1) // 2)
        if self.live:
            self.slots = (place(count) - place(index) + size) % size
            seat = (place(index) + count) % size
            self.owners = jnp.where(seat < size // 2, 2 * seat, 2 * (size - seat) - 1)
        else:
            self.slots = count
            self.owners = count
        self.half = size // 2

    def table(self):
        return jnp.concatenate([self.slots, self.owners])

    def ahead(self, value):
        return lax.ppermute(value, "batch", self.forward)

    def back(self, value):
        return lax.ppermute(value, "batch", self.backward)


def owner_at(info, live, nb, slot):
    return info[2 + nb + slot] if live else slot


def put(outs, slot, value, rows, cols):
    if len(outs) == 1:
        outs[0][slot, rows, cols] = value
        return
    for at, out in enumerate(outs):

        @pl.when(slot == at)
        def _():
            out[0, rows, cols] = value


def blocks_of(refs):
    out = []
    for ref in refs:
        out += [(ref, at) for at in range(ref.shape[0])]
    return out


def once(shape):
    return pl.BlockSpec(shape, lambda i, *_: (0,) * len(shape), pipeline_mode=pl.Buffered(1))


def first_pack_kernel(info, joined, outw, *refs):
    smalls, out = refs[:-1], refs[-1]
    rows, cols = joined.shape
    out[:rows, :cols] = joined[...]
    out[:rows, cols:] = outw[...]
    pieces = [small[...].astype(F32) for small in smalls]
    count = sum(piece.shape[0] for piece in pieces)
    pieces.append(jnp.zeros((16 - count, rows), F32))
    out[rows:, :rows] = jnp.concatenate(pieces, 0).astype(BF)
    out[rows:, rows:] = jnp.zeros((16, out.shape[1] - rows), BF)


def first_pack(info, joined, outw, smalls, cols, cw):
    rows = joined.shape[0]
    shape = (rows + 16, cols + cw)
    return pl.pallas_call(
        first_pack_kernel,
        grid_spec=pltpu.PrefetchScalarGridSpec(
            num_scalar_prefetch=1,
            grid=(1,),
            in_specs=[
                pl.BlockSpec((rows, cols), lambda i, info: (0, info[0])),
                pl.BlockSpec((rows, cw), lambda i, info: (0, info[0])),
            ]
            + [once(small.shape) for small in smalls],
            out_specs=pl.BlockSpec(shape, lambda i, info: (0, 0)),
        ),
        out_shape=jax.ShapeDtypeStruct(shape, BF),
        compiler_params=params(60),
        name="first_pack",
    )(info, joined, outw, *smalls)


def second_pack_kernel(nb, ns, units, info, expand, shrink, out):
    rows = expand.shape[0]
    for k in range(nb):
        col = pl.ds(pl.multiple_of((k * ns + info[0]) * units, units), units)
        out[:rows, k * units : (k + 1) * units] = expand[:, col]
    out[rows:] = shrink[...]


def second_pack(info, expand, shrink, nb, ns):
    rows, wide = expand.shape
    dim = shrink.shape[1]
    units = shrink.shape[0] // ns
    return pl.pallas_call(
        functools.partial(second_pack_kernel, nb, ns, units),
        grid_spec=pltpu.PrefetchScalarGridSpec(
            num_scalar_prefetch=1,
            grid=(1,),
            in_specs=[
                pl.BlockSpec((rows, wide), lambda i, info: (0, 0)),
                pl.BlockSpec((units, dim), lambda i, info: (info[0], 0)),
            ],
            out_specs=pl.BlockSpec((rows + units, dim), lambda i, info: (0, 0)),
        ),
        out_shape=jax.ShapeDtypeStruct((rows + units, dim), BF),
        compiler_params=params(60),
        name="second_pack",
    )(info, expand, shrink)


def first_kernel(starts, nb, rows, cols, live, info, *refs):
    jbias_in, refs = (None, refs) if live else (refs[0], refs[1:])
    count = len(starts) - 1
    xs, weights = refs[:count], refs[count:-6]
    normed, joined, full, outw, vecs, jbias = refs[-6:]
    step = pl.program_id(0)

    @pl.when(step == 0)
    def _():
        for slot, (ref, at) in enumerate(blocks_of(weights)):
            high = owner_at(info, live, nb, slot) * rows
            high = pl.multiple_of(high, rows) if live else high
            full[pl.ds(high, rows)] = ref[at, :rows, :cols]
            outw[pl.ds(high, rows)] = ref[at, :rows, cols:]
            vecs[:, pl.ds(high, rows)] = ref[at, rows:, :rows].astype(F32)
        if live:
            heads = cols // (3 * HD)
            for head in range(heads):
                at = info[0] * heads + head
                col = pl.ds(pl.multiple_of(lax.div(at, 2) * rows, rows), rows)
                row = vecs[0:8, col][2 + head % 2 : 3 + head % 2]
                pieces = [row[:, :HD], jnp.zeros((1, HD), F32), row[:, HD:]]
                jbias[:, head * 3 * HD : (head + 1) * 3 * HD] = jnp.concatenate(pieces, 1)
        else:
            jbias[...] = jbias_in[...]

    for at in range(count):

        @pl.when((step >= starts[at]) & (step < starts[at + 1]))
        def _():
            unit, _ = norm_parts(xs[at][...].astype(F32))
            value = (unit * vecs[0:1] + vecs[1:2]).astype(BF)
            normed[...] = value
            joined[...] = (dg(value, full[...], NN) + jbias[...]).astype(BF)


def first_call(info, jbias, xs, weights, cols, live, ns):
    dim = xs[0].shape[1]
    tok = sum(piece.shape[0] for piece in xs) // ns
    nb = sum(weight.shape[0] for weight in weights)
    rows = dim // nb
    cw = weights[0].shape[2] - cols
    tile = min(256, tok)
    nt = tok // tile
    starts = [0]
    for piece in xs:
        starts.append(starts[-1] + piece.shape[0] // tile)
    extra = [] if live else [jbias]
    place = lambda i, info: ((info[0] ^ lax.div(i, nt)) * nt + lax.rem(i, nt), 0)

    def source(at):
        last = starts[at + 1] - starts[at] - 1
        return pl.BlockSpec((tile, dim), lambda i, info: (jnp.clip(i - starts[at], 0, last), 0))

    return pl.pallas_call(
        functools.partial(first_kernel, starts, nb, rows, cols, live),
        grid_spec=pltpu.PrefetchScalarGridSpec(
            num_scalar_prefetch=1,
            grid=(ns * nt,),
            in_specs=[once(value.shape) for value in extra]
            + [source(at) for at in range(len(xs))]
            + [once(weight.shape) for weight in weights],
            out_specs=[
                pl.BlockSpec((tile, dim), place),
                pl.BlockSpec((tile, cols), place),
                once((dim, cols)),
                once((dim, cw)),
                once((16, dim)),
            ],
            scratch_shapes=[pltpu.VMEM((1, cols), F32)],
        ),
        out_shape=[
            jax.ShapeDtypeStruct((ns * tok, dim), BF),
            jax.ShapeDtypeStruct((ns * tok, cols), BF),
            jax.ShapeDtypeStruct((dim, cols), BF),
            jax.ShapeDtypeStruct((dim, cw), BF),
            jax.ShapeDtypeStruct((16, dim), F32),
        ],
        compiler_params=params(60),
        cost_estimate=cost(2 * ns * tok * dim * cols, 2 * ns * tok * (2 * dim + cols)),
        name="first",
    )(info, *extra, *xs, *weights)


def three(value):
    high = value.astype(BF)
    rest = value - high.astype(F32)
    mid = rest.astype(BF)
    return high, mid, (rest - mid.astype(F32)).astype(BF)


def spread(lane, base, columns):
    for at, column in columns:
        base = jnp.where(lane == at, column.astype(F32), base)
    return base.astype(BF)


def key_extra(count, slope, length):
    lane = lax.broadcasted_iota(jnp.int32, (count, HD), 1)
    pos = lax.broadcasted_iota(jnp.int32, (count, HD), 0)
    high, mid, low = three(slope * pos.astype(F32))
    dead = jnp.where(pos < length, 0.0, -1e30)
    return spread(lane, jnp.where(lane < 7, 1.0, 0.0), [(0, high), (1, mid), (2, low), (3, dead)])


def attend_kernel(count, size, pair, info, slopes, joined, mixed, sums, keys):
    lane = lax.broadcasted_iota(jnp.int32, (size, HD), 1)
    ones = jnp.where(lane < 4, 1.0, 0.0).astype(BF)
    for hh in range(2):
        base = 3 * HD * hh
        extra = key_extra(count, slopes[2 * pair + hh], info[1])
        keys[hh] = jnp.concatenate([joined[:, base + HD : base + 2 * HD], extra], 1)
    query_at = lax.broadcasted_iota(jnp.int32, (size, size), 0)
    key_at = lax.broadcasted_iota(jnp.int32, (size, size), 1)
    for block in range(count // size):
        low = block * size
        high = low + size
        outs = []
        logs = []
        for hh in range(2):
            base = 3 * HD * hh
            query = (joined[low:high, base : base + HD].astype(F32) * 0.125).astype(BF)
            query = jnp.concatenate([query, ones], 1)
            near = jnp.where(key_at <= query_at, dg(query, keys[hh, low:high], NT), -1e30)
            top = jnp.max(near, axis=1, keepdims=True)
            if block:
                far = dg(query, keys[hh, 0:low], NT)
                top = jnp.maximum(top, jnp.max(far, axis=1, keepdims=True))
            near = jnp.exp(near - top)
            total = jnp.sum(near, axis=1, keepdims=True)
            acc = dg(near.astype(BF), joined[low:high, base + 2 * HD : base + 3 * HD], NN)
            if block:
                far = jnp.exp(far - top)
                total += jnp.sum(far, axis=1, keepdims=True)
                acc += dg(far.astype(BF), joined[0:low, base + 2 * HD : base + 3 * HD], NN)
            outs.append(acc / total)
            logs.append(jnp.broadcast_to(top + jnp.log(total), (size, HD)))
        mixed[low:high] = jnp.concatenate(outs, 1).astype(BF)
        sums[low:high] = jnp.concatenate(logs, 1)


def attend(joined, info, slopes, pair, held):
    count, width = joined.shape
    groups = width // (6 * HD)
    smem = pl.BlockSpec(memory_space=pltpu.SMEM)
    narrow = pl.BlockSpec((count, 2 * HD), lambda i: (0, pair))
    area = count * count
    extra = [] if held is None else list(held)

    def kernel(*refs):
        attend_kernel(count, min(512, count), pair, *refs[:3], *refs[3 + len(extra) :])

    return pl.pallas_call(
        kernel,
        grid=(1,),
        in_specs=[smem, smem, pl.BlockSpec((count, 6 * HD), lambda i: (0, pair))]
        + [pl.BlockSpec(memory_space=pl.ANY)] * len(extra),
        out_specs=[narrow, narrow],
        out_shape=[
            jax.ShapeDtypeStruct((count, groups * 2 * HD), BF),
            jax.ShapeDtypeStruct((count, groups * 2 * HD), F32),
        ],
        input_output_aliases={3: 0, 4: 1} if extra else {},
        scratch_shapes=[pltpu.VMEM((2, count, 2 * HD), BF)],
        compiler_params=params(60),
        cost_estimate=cost(area * 1024, 20 * count * HD, area),
        name="attend",
    )(info, slopes, joined, *extra)


def attend_back_kernel(count, size, ns, pair, info, slopes, joined, mixed, sums, *refs):
    pieces_in = refs[:ns]
    out, sides, keys, queries, values, grads, query_grad = refs[ns:]
    tok = count // ns
    lane = lax.broadcasted_iota(jnp.int32, (count, HD), 1)
    near_lane = lax.broadcasted_iota(jnp.int32, (tok, HD), 1)
    for hh in range(2):
        base = 3 * HD * hh
        half = slice(hh * HD, (hh + 1) * HD)
        extra = key_extra(count, slopes[2 * pair + hh], info[1])
        keys[hh] = jnp.concatenate([joined[:, base + HD : base + 2 * HD], extra], 1)
        query = (joined[:, base : base + HD].astype(F32) * 0.125).astype(BF)
        high, mid, low = three(-sums[:, half])
        extra = spread(lane, jnp.where(lane < 4, 1.0, 0.0), [(4, high), (5, mid), (6, low)])
        queries[hh] = jnp.concatenate([query, extra], 1)
        ones = jnp.where(lane < 3, 1.0, 0.0).astype(BF)
        values[hh] = jnp.concatenate([joined[:, base + 2 * HD : base + 3 * HD], ones], 1)
        for rel in range(ns):
            at = pl.ds(pl.multiple_of((info[0] ^ rel) * tok, tok), tok)
            part = pieces_in[rel][:, half]
            inner = jnp.sum(part.astype(F32) * mixed[at, half].astype(F32), axis=1, keepdims=True)
            high, mid, low = three(jnp.broadcast_to(-inner, (tok, HD)))
            extra = spread(near_lane, jnp.zeros((tok, HD), F32), [(0, high), (1, mid), (2, low)])
            grads[hh, at] = jnp.concatenate([part, extra], 1)
    key_at = lax.broadcasted_iota(jnp.int32, (size, size), 0)
    query_at = lax.broadcasted_iota(jnp.int32, (size, size), 1)
    blocks = count // size
    for j in range(blocks):
        ks = slice(j * size, (j + 1) * size)
        pieces = []
        for hh in range(2):
            key_sum = None
            for i in range(j, blocks):
                qs = slice(i * size, (i + 1) * size)
                probs = jnp.exp(dg(keys[hh, ks], queries[hh, qs], NT))
                if i == j:
                    probs = jnp.where(key_at <= query_at, probs, 0.0)
                slope = (probs * dg(values[hh, ks], grads[hh, qs], NT)).astype(BF)
                value_part = dg(probs.astype(BF), grads[hh, qs], NN)
                key_part = dg(slope, queries[hh, qs], NN)
                query_part = dg(keys[hh, ks], slope, TN)
                value_sum = value_part if key_sum is None else value_sum + value_part
                key_sum = key_part if key_sum is None else key_sum + key_part
                query_grad[hh, :, qs] = query_part if j == 0 else query_grad[hh, :, qs] + query_part
            pieces += [jnp.zeros((size, HD), F32), key_sum[:, :HD], value_sum[:, :HD]]
        out[ks] = jnp.concatenate(pieces, 1).astype(BF)
    for hh in range(2):
        base = 3 * HD * hh
        out[:, base : base + HD] = (query_grad[hh].T[:, :HD] * 0.125).astype(BF)
    sides[...] = jnp.sum(out[...].astype(F32), axis=0, keepdims=True)


def attend_back(joined, grads, mixed, sums, info, slopes, pair, held):
    count, width = joined.shape
    ns = len(grads)
    smem = pl.BlockSpec(memory_space=pltpu.SMEM)
    wide = pl.BlockSpec((count, 6 * HD), lambda i: (0, pair))
    narrow = pl.BlockSpec((count, 2 * HD), lambda i: (0, pair))
    piece = pl.BlockSpec((count // ns, 2 * HD), lambda i: (0, pair))
    area = count * count
    extra = [] if held is None else [held]

    def kernel(*refs):
        inputs, rest = refs[: 5 + ns], refs[5 + ns + len(extra) :]
        attend_back_kernel(count, min(512, count), ns, pair, *inputs, *rest)

    return pl.pallas_call(
        kernel,
        grid=(1,),
        in_specs=[smem, smem, wide, narrow, narrow]
        + [piece] * ns
        + [pl.BlockSpec(memory_space=pl.ANY)] * len(extra),
        out_specs=[wide, pl.BlockSpec((1, 6 * HD), lambda i: (0, 0))],
        out_shape=[jax.ShapeDtypeStruct((count, width), BF), jax.ShapeDtypeStruct((1, 6 * HD), F32)],
        input_output_aliases={5 + ns: 0} if extra else {},
        scratch_shapes=[pltpu.VMEM((2, count, 2 * HD), BF)] * 4 + [pltpu.VMEM((2, 2 * HD, count), F32)],
        compiler_params=params(60),
        cost_estimate=cost(area * 2560, 40 * count * HD, area),
        name="attend_back",
    )(info, slopes, joined, mixed, sums, *grads, *extra)


def middle_kernel(ns, np, info, x, vecs, *refs):
    mixed, weights = refs[: ns * np], refs[ns * np : ns * np + ns]
    merged, resid, second, full = refs[ns * np + ns :]
    cw = weights[0].shape[1]
    pw = cw // np

    @pl.when(pl.program_id(0) == 0)
    def _():
        for rel in range(ns):
            full[:, pl.ds(pl.multiple_of((info[0] ^ rel) * cw, cw), cw)] = weights[rel][...]

    for pair in range(np):
        for rel in range(ns):
            col = pl.ds(pl.multiple_of((info[0] ^ rel) * cw + pair * pw, pw), pw)
            merged[:, col] = mixed[pair * ns + rel][...]
    value = x[...].astype(F32) + dg(merged[...], full[...], NN) + vecs[4:5]
    resid[...] = value
    unit, _ = norm_parts(value)
    second[...] = (unit * vecs[5:6] + vecs[6:7]).astype(BF)


def middle_call(info, x, vecs, mixed, weights):
    tok, dim = x.shape
    ns = len(weights)
    np = len(mixed) // ns
    tile = min(256, tok)
    part = lambda width: pl.BlockSpec((tile, width), lambda i, info: (i, 0))
    return pl.pallas_call(
        functools.partial(middle_kernel, ns, np),
        grid_spec=pltpu.PrefetchScalarGridSpec(
            num_scalar_prefetch=1,
            grid=(tok // tile,),
            in_specs=[part(dim), once(vecs.shape)]
            + [part(block.shape[1]) for block in mixed]
            + [once(weight.shape) for weight in weights],
            out_specs=[part(dim), part(dim), part(dim), once((dim, dim))],
        ),
        out_shape=[
            jax.ShapeDtypeStruct((tok, dim), BF),
            jax.ShapeDtypeStruct((tok, dim), F32),
            jax.ShapeDtypeStruct((tok, dim), BF),
            jax.ShapeDtypeStruct((dim, dim), BF),
        ],
        compiler_params=params(60),
        cost_estimate=cost(2 * tok * dim * dim, 12 * tok * dim + 4 * dim * dim),
        name="middle",
    )(info, x, vecs, *mixed, *weights)


def feed_kernel(nt, nb, rows, units, live, info, sa, sb, ca, cb, ebias, *refs):
    weights = refs[:-9]
    activ, pre_grad, oa, ob, ba, bb, bgrad, wide, tall = refs[-9:]
    step = pl.program_id(0)
    bias = ebias[...]
    if live:
        row = lax.broadcasted_iota(jnp.int32, bias.shape, 0)
        bias = jnp.sum(jnp.where(row == 7 + info[0], bias, 0.0), axis=0, keepdims=True)

    @pl.when(step == 0)
    def _():
        blocks = blocks_of(weights)
        for slot in range(nb):
            owner = owner_at(info, live, nb, slot)
            high = pl.multiple_of(owner * rows, rows) if live else owner * rows
            deep = pl.multiple_of(owner * units, units) if live else owner * units
            if len(blocks) == nb:
                ref, at = blocks[slot]
                wide[pl.ds(high, rows)] = ref[at, :rows]
                tall[pl.ds(deep, units)] = ref[at, rows:]
            else:
                wide[pl.ds(high, rows)] = weights[0][slot]
                tall[pl.ds(deep, units)] = weights[1][slot]
        bgrad[...] = jnp.zeros_like(bgrad)

    def work(second, cot, out, back):
        pre = dg(second[...], wide[...], NN) + bias
        square = pre * pre
        bend = jnp.tanh(0.7978845608028654 * pre * (1.0 + 0.044715 * square))
        half = 0.5 + 0.5 * bend
        act = (pre * half).astype(BF)
        activ[...] = act
        out[...] = dg(act, tall[...], NN).astype(BF)
        steep = half + pre * (0.5 - 0.5 * bend * bend) * (0.7978845608028654 + 0.10703222440890037 * square)
        grad = (dg(cot[...], tall[...], NT) * steep).astype(BF)
        pre_grad[...] = grad
        bgrad[...] += jnp.sum(grad.astype(F32), axis=0, keepdims=True)
        back[...] = dg(grad, wide[...], NT).astype(BF)

    @pl.when(step < nt)
    def _():
        work(sa, ca, oa, ba)

    @pl.when(step >= nt)
    def _():
        work(sb, cb, ob, bb)


def feed_call(info, sa, sb, ca, cb, ebias, weights, rows, units, nb, live):
    tok, dim = sa.shape
    ff = ebias.shape[1]
    tile = min(256, tok)
    nt = tok // tile
    left = pl.BlockSpec((tile, dim), lambda i, info: (jnp.minimum(i, nt - 1), 0))
    right = pl.BlockSpec((tile, dim), lambda i, info: (jnp.maximum(i - nt, 0), 0))
    flat = pl.BlockSpec((tile, ff), lambda i, info: (i, 0))
    shape = jax.ShapeDtypeStruct((tok, dim), BF)
    return pl.pallas_call(
        functools.partial(feed_kernel, nt, nb, rows, units, live),
        grid_spec=pltpu.PrefetchScalarGridSpec(
            num_scalar_prefetch=1,
            grid=(2 * nt,),
            in_specs=[left, right, left, right, once(ebias.shape)] + [once(weight.shape) for weight in weights],
            out_specs=[flat, flat, left, right, left, right, pl.BlockSpec((1, ff), lambda i, info: (0, 0))],
            scratch_shapes=[pltpu.VMEM((dim, ff), BF), pltpu.VMEM((ff, dim), BF)],
        ),
        out_shape=[jax.ShapeDtypeStruct((2 * tok, ff), BF)] * 2
        + [shape] * 4
        + [jax.ShapeDtypeStruct((1, ff), F32)],
        compiler_params=params(60),
        cost_estimate=cost(16 * tok * dim * ff, 16 * tok * dim + 8 * dim * ff, 2 * tok * ff),
        name="feed",
    )(info, sa, sb, ca, cb, ebias, *weights)


def feed_grad_kernel(ns, nb, rows, units, steps, info, *refs):
    half = ns // 2
    activs, cots, seconds, grads = refs[:half], refs[half : half + ns], refs[half + ns : half + 2 * ns], refs[half + 2 * ns : 2 * half + 2 * ns]
    outs = refs[2 * half + 2 * ns :]
    step = pl.program_id(0)

    def total(wides, thins, wide_left):
        out = None
        for rel in range(ns):
            thin = thins[rel]
            tok = thin.shape[0]
            wide = wides[rel // 2][(rel % 2) * tok : (rel % 2 + 1) * tok]
            term = dg(wide, thin[...], TN) if wide_left else dg(thin[...], wide, TN)
            out = term if out is None else out + term
        return out.astype(BF)

    def store(value, high, count, at, low):
        for k in range(value.shape[0] // count):
            slot = info[2 + at * (value.shape[0] // count) + k]
            piece = value[k * count : (k + 1) * count]
            if len(outs) == nb:
                for mine, out in enumerate(outs):

                    @pl.when(slot == mine)
                    def _():
                        out[0, low : low + count] = piece

            else:
                outs[0 if high else 1][slot] = piece

    @pl.when(step < steps)
    def _():
        store(total(activs, cots, True), False, units, step, rows)

    @pl.when(step >= steps)
    def _():
        store(total(grads, seconds, False), True, rows, step - steps, 0)


def feed_grad_call(info, activs, cots, seconds, grads, nb, live):
    ns = len(cots)
    dim = cots[0].shape[1]
    ff = activs[0].shape[1]
    rows, units = dim // nb, ff // nb
    tile = 256
    steps = ff // tile
    tok = ns * cots[0].shape[0]
    left = lambda a: pl.BlockSpec((a.shape[0], tile), lambda i, info: (0, jnp.minimum(i, steps - 1)))
    right = lambda a: pl.BlockSpec((a.shape[0], tile), lambda i, info: (0, jnp.maximum(i - steps, 0)))
    fixed = lambda a: once(a.shape)
    shapes = [(1, rows + units, dim)] * nb if live else [(nb, rows, ff), (nb, units, dim)]
    return pl.pallas_call(
        functools.partial(feed_grad_kernel, ns, nb, rows, units, steps),
        grid_spec=pltpu.PrefetchScalarGridSpec(
            num_scalar_prefetch=1,
            grid=(steps + dim // tile,),
            in_specs=[left(a) for a in activs]
            + [fixed(a) for a in cots]
            + [right(a) for a in seconds]
            + [fixed(a) for a in grads],
            out_specs=[once(shape) for shape in shapes],
        ),
        out_shape=[jax.ShapeDtypeStruct(shape, BF) for shape in shapes],
        compiler_params=params(60),
        cost_estimate=cost(4 * tok * dim * ff, 4 * tok * (dim + ff) + 4 * dim * ff),
        name="feed_grad",
    )(info, *activs, *cots, *seconds, *grads)


def pair_shapes(shape, ns):
    return [shape, shape, (2, *shape)] if ns == 4 else [shape] * ns


def pair_put(outs, ns, rel, rows, value):
    if ns == 4 and rel % 2:
        outs[2][rel // 2, rows] = value
    elif ns == 4:
        outs[rel // 2][rows] = value
    else:
        outs[rel][rows] = value


def split_grad_kernel(ns, info, left, right, *refs):
    outs, held = refs[:-1], refs[-1]
    held[...] = dg(left[...], right[...], TN)
    tile = held.shape[0]
    cw = held.shape[1] // ns
    rows = pl.ds(pl.multiple_of(pl.program_id(0) * tile, tile), tile)
    for rel in range(ns):
        col = pl.ds(pl.multiple_of((info[0] ^ rel) * cw, cw), cw)
        pair_put(outs, ns, rel, rows, held[:, col].astype(BF))


def split_grad(info, left, right, ns):
    tok, dim = left.shape
    tile = 256
    shapes = pair_shapes((dim, dim // ns), ns)
    return pl.pallas_call(
        functools.partial(split_grad_kernel, ns),
        grid_spec=pltpu.PrefetchScalarGridSpec(
            num_scalar_prefetch=1,
            grid=(dim // tile,),
            in_specs=[pl.BlockSpec((tok, tile), lambda i, info: (0, i)), once((tok, dim))],
            out_specs=[once(shape) for shape in shapes],
            scratch_shapes=[pltpu.VMEM((tile, dim), F32)],
        ),
        out_shape=[jax.ShapeDtypeStruct(shape, BF) for shape in shapes],
        compiler_params=params(60),
        cost_estimate=cost(2 * tok * dim * dim, 6 * dim * dim),
        name="split_grad",
    )(info, left, right)


def joined_grad_kernel(nb, rows, np, live, info, left, other, weight, vecs, *refs):
    smalls, refs = (refs[:3], refs[3:]) if live else (refs[:1], refs[1:])
    right, sides, outs = refs[0], refs[1 : 1 + np], refs[1 + np :]
    total = dg(left[...], right[...], TN)
    tile, cw = other.shape
    cols = weight.shape[1]
    first = pl.program_id(0) * (tile // rows)
    low = total.astype(BF)
    weights = weight[...].astype(F32)
    moment = jnp.sum(total * weights, axis=1, keepdims=True)
    shift = jnp.sum(jnp.concatenate([side[...] for side in sides], 1) * weights, axis=1, keepdims=True)
    moment = jnp.broadcast_to(moment, (tile, 128)).T[:1]
    shift = jnp.broadcast_to(shift, (tile, 128)).T[:1]
    gain = (moment - vecs[1:2] * shift) / vecs[0:1]
    row = lax.broadcasted_iota(jnp.int32, (16, tile), 0)
    held = jnp.zeros((16, tile), F32) if live else smalls[0][...]
    held = jnp.where(row == 0, gain, jnp.where(row == 1, shift, held))
    if live:
        turned = smalls[0][...]
        for at, source in ((4, 2), (5, 0), (6, 1), (11, 3)):
            held = jnp.where(row == at, turned[source : source + 1], held)
        held = jnp.where(row == 7 + info[0], smalls[1][...] + smalls[2][...], held)
        for part in range(2):
            pieces = []
            for side in sides:
                base = part * 3 * HD
                pieces += [side[:, base : base + HD], side[:, base + 2 * HD : base + 3 * HD]]
            bias = jnp.where(pl.program_id(0) == info[0], jnp.concatenate(pieces, 1), 0.0)
            held = jnp.where(row == 2 + part, bias, held)
    held = held.astype(BF)
    for k in range(tile // rows):
        slot = info[2 + first + k]
        high = slice(k * rows, (k + 1) * rows)
        put(outs, slot, low[high], slice(0, rows), slice(0, cols))
        put(outs, slot, other[high], slice(0, rows), slice(cols, cols + cw))
        put(outs, slot, held[:, high], slice(rows, rows + 16), slice(0, rows))


def joined_grad_call(info, left, right, sides, other, weight, vecs, shares, turned, biases, nb, live):
    count, dim = left.shape
    cols = weight.shape[1]
    cw = other.shape[1]
    rows = dim // nb
    tile = 256
    wide = (rows + 16, cols + cw)
    shapes = [(1, *wide)] * nb if live else [(nb, *wide)]
    flat = lambda width: pl.BlockSpec((tile, width), lambda i, info: (i, 0))
    tall = lambda value: pl.BlockSpec((value.shape[0], tile), lambda i, info: (0, i))
    smalls = (turned, *biases) if live else (shares,)
    return pl.pallas_call(
        functools.partial(joined_grad_kernel, nb, rows, len(sides), live),
        grid_spec=pltpu.PrefetchScalarGridSpec(
            num_scalar_prefetch=1,
            grid=(dim // tile,),
            in_specs=[pl.BlockSpec((count, tile), lambda i, info: (0, i)), flat(cw), flat(cols), tall(vecs)]
            + [tall(value) for value in smalls]
            + [once(value.shape) for value in (right, *sides)],
            out_specs=[once(shape) for shape in shapes],
        ),
        out_shape=[jax.ShapeDtypeStruct(shape, BF) for shape in shapes],
        compiler_params=params(60),
        cost_estimate=cost(2 * count * dim * cols, 2 * count * (dim + cols) + 4 * dim * dim),
        name="joined_grad",
    )(info, left, other, weight, vecs, *smalls, right, *sides)


def turn_kernel(ns, np, cw, info, ga, gb, gc, resid, cot, vecs, full, resid_grad, branch, *refs):
    mixed_grads, sums, held = refs[: ns * np], refs[ns * np], refs[ns * np + 1]

    @pl.when(pl.program_id(0) == 0)
    def _():
        sums[...] = jnp.zeros_like(sums)

    grad = ga[...].astype(F32) + gb[...].astype(F32) + gc[...].astype(F32)
    unit, scale = norm_parts(resid[...])
    outer = cot[...].astype(F32)
    value = outer + norm_back(grad, unit, scale, vecs[5:6])
    resid_grad[...] = value
    low = value.astype(BF)
    branch[...] = low
    held[...] = dg(low, full[...], NT).astype(BF)
    pw = cw // np
    for pair in range(np):
        for rel in range(ns):
            col = pl.ds(pl.multiple_of((info[0] ^ rel) * cw + pair * pw, pw), pw)
            mixed_grads[pair * ns + rel][...] = held[:, col]
    for at, term in enumerate((grad * unit, grad, low.astype(F32), outer)):
        sums[at : at + 1] += jnp.sum(term, axis=0, keepdims=True)


def turn_call(info, terms, resid, cot, vecs, full, ns, np):
    tok, dim = resid.shape
    cw = dim // ns
    tile = min(256, tok)
    part = pl.BlockSpec((tile, dim), lambda i, info: (i, 0))
    return pl.pallas_call(
        functools.partial(turn_kernel, ns, np, cw),
        grid_spec=pltpu.PrefetchScalarGridSpec(
            num_scalar_prefetch=1,
            grid=(tok // tile,),
            in_specs=[part, part, part, part, part, once(vecs.shape), once(full.shape)],
            out_specs=[part, part]
            + [pl.BlockSpec((tile, cw // np), lambda i, info: (i, 0))] * (ns * np)
            + [pl.BlockSpec((8, dim), lambda i, info: (0, 0))],
            scratch_shapes=[pltpu.VMEM((tile, dim), BF)],
        ),
        out_shape=[
            jax.ShapeDtypeStruct((tok, dim), F32),
            jax.ShapeDtypeStruct((tok, dim), BF),
        ]
        + [jax.ShapeDtypeStruct((tok, cw // np), BF)] * (ns * np)
        + [jax.ShapeDtypeStruct((8, dim), F32)],
        compiler_params=params(60),
        cost_estimate=cost(2 * tok * dim * dim, 16 * tok * dim + 2 * dim * dim),
        name="turn",
    )(info, *terms, resid, cot, vecs, full)


def last_kernel(ns, info, weight, right, *outs):
    step = pl.program_id(0)
    low = dg(right[...], weight[...], NT).astype(BF)
    for rel in range(ns):

        @pl.when(ns - 1 - step == rel)
        def _():
            if ns == 4 and rel % 2:
                outs[2][0] = low
            else:
                outs[rel // 2 if ns == 4 else rel][...] = low


def last_call(info, right, weight, ns):
    count = right.shape[0]
    dim, cols = weight.shape
    tok = count // ns
    shapes = pair_shapes((tok, dim), ns)
    specs = [pl.BlockSpec((tok, dim), lambda i, info: (0, 0))] * ns
    if ns == 4:
        specs[2:] = [pl.BlockSpec((1, tok, dim), lambda i, info: (jnp.where(i < 2, 1, 0), 0, 0))]
    return pl.pallas_call(
        functools.partial(last_kernel, ns),
        grid_spec=pltpu.PrefetchScalarGridSpec(
            num_scalar_prefetch=1,
            grid=(ns,),
            in_specs=[
                once(weight.shape),
                pl.BlockSpec((tok, cols), lambda i, info: (info[0] ^ (ns - 1 - i), 0)),
            ],
            out_specs=specs,
        ),
        out_shape=[jax.ShapeDtypeStruct(shape, BF) for shape in shapes],
        compiler_params=params(60),
        cost_estimate=cost(2 * count * dim * cols, 2 * count * (2 * dim + cols)),
        name="last",
    )(info, weight, right)


def end_kernel(ga, gb, gc, x, resid_grad, vecs, out):
    grad = ga[...].astype(F32) + gb[...].astype(F32) + gc[...].astype(F32)
    unit, scale = norm_parts(x[...].astype(F32))
    out[...] = resid_grad[...] + norm_back(grad, unit, scale, vecs[0:1])


def end_call(terms, x, resid_grad, vecs):
    tok, dim = x.shape
    tile = min(128, tok)
    part = pl.BlockSpec((tile, dim), lambda i: (i, 0))
    head = pl.BlockSpec((None, tile, dim), lambda i: (0, i, 0))
    return pl.pallas_call(
        end_kernel,
        grid=(tok // tile,),
        in_specs=[head if term.ndim == 3 else part for term in terms]
        + [part, part, pl.BlockSpec(vecs.shape, lambda i: (0, 0))],
        out_specs=part,
        out_shape=jax.ShapeDtypeStruct((tok, dim), F32),
        compiler_params=params(40),
        cost_estimate=cost(20 * tok * dim, 14 * tok * dim),
        name="end",
    )(*terms, x, resid_grad, vecs)


def add_pairs_kernel(count, *refs):
    for at in range(count):
        left, right, out = refs[at], refs[count + at], refs[2 * count + at]
        out[...] = (left[...].astype(F32) + right[...].astype(F32)).astype(BF)


def add_pairs(lefts, rights):
    count = len(lefts)
    return pl.pallas_call(
        functools.partial(add_pairs_kernel, count),
        in_specs=[pl.BlockSpec(memory_space=pltpu.VMEM)] * (2 * count),
        out_specs=[pl.BlockSpec(memory_space=pltpu.VMEM)] * count,
        out_shape=[jax.ShapeDtypeStruct(left.shape, BF) for left in lefts],
        compiler_params=params(20),
        cost_estimate=cost(1, 1),
        name="add_pairs",
    )(*lefts, *rights)


def joined_out_kernel(ns, cols, info, *refs):
    parts, joined, outw, smalls = refs[:ns], refs[ns], refs[ns + 1], refs[ns + 2 :]
    rows = joined.shape[0]
    cw = parts[0].shape[1] - cols
    total = None
    for rel in range(ns):
        part = parts[rel]
        joined[:, pl.ds(pl.multiple_of((info[0] ^ rel) * cols, cols), cols)] = part[:rows, :cols].astype(F32)
        outw[:, pl.ds(pl.multiple_of((info[0] ^ rel) * cw, cw), cw)] = part[:rows, cols:].astype(F32)
        term = part[rows:, :rows].astype(F32)
        total = term if total is None else total + term
    at = 0
    for small in smalls:
        for row in range(small.shape[0]):
            small[row : row + 1] = total[at + row : at + row + 1]
        at += small.shape[0]


def joined_out(info, parts, cols):
    ns = len(parts)
    high, wide = parts[0].shape
    rows = high - 16
    shapes = [(rows, ns * cols), (rows, ns * (wide - cols))]
    shapes += [(count, rows) for count in (1, 1, 2, 1, 1, 1, 4, 1)]
    return pl.pallas_call(
        functools.partial(joined_out_kernel, ns, cols),
        grid_spec=pltpu.PrefetchScalarGridSpec(
            num_scalar_prefetch=1,
            grid=(1,),
            in_specs=[once(part.shape) for part in parts],
            out_specs=[once(shape) for shape in shapes],
        ),
        out_shape=[jax.ShapeDtypeStruct(shape, F32) for shape in shapes],
        compiler_params=params(60),
        cost_estimate=cost(0, 6 * ns * rows * wide),
        name="joined_out",
    )(info, *parts)


def feed_out_kernel(ns, nb, rows, units, info, *refs):
    parts, expand, shrink = refs[:ns], refs[ns], refs[ns + 1]
    for rel in range(ns):
        seat = info[0] ^ rel
        shrink[pl.ds(pl.multiple_of(seat * units, units), units)] = parts[rel][rows:].astype(F32)
        for k in range(nb):
            col = pl.ds(pl.multiple_of((k * ns + seat) * units, units), units)
            expand[:, col] = parts[rel][:rows, k * units : (k + 1) * units].astype(F32)


def feed_out(info, parts, nb, rows):
    ns = len(parts)
    high, dim = parts[0].shape
    units = high - rows
    shapes = [(rows, ns * units * nb), (ns * units, dim)]
    return pl.pallas_call(
        functools.partial(feed_out_kernel, ns, nb, rows, units),
        grid_spec=pltpu.PrefetchScalarGridSpec(
            num_scalar_prefetch=1,
            grid=(1,),
            in_specs=[once(part.shape) for part in parts],
            out_specs=[once(shape) for shape in shapes],
        ),
        out_shape=[jax.ShapeDtypeStruct(shape, F32) for shape in shapes],
        compiler_params=params(60),
        cost_estimate=cost(0, 6 * ns * high * dim),
        name="feed_out",
    )(info, *parts)


def body(
    layer_input,
    lengths,
    first_gain,
    first_shift,
    joined_weight,
    joined_bias,
    output_weight,
    output_bias,
    second_gain,
    second_shift,
    expand_weight,
    expand_bias,
    shrink_weight,
    shrink_bias,
    out_grad,
):
    ns = lax.axis_size("seq")
    nb = lax.axis_size("batch")
    si = lax.axis_index("seq")
    bi = lax.axis_index("batch")
    tok = layer_input.shape[1]
    dim = layer_input.shape[2]
    heads = H // ns
    np = heads // 2
    cols = 3 * HD * heads
    cw = HD * heads
    rows = dim // nb
    ff = expand_weight.shape[1] // ns
    units = ff // nb
    x = layer_input[0]
    cot = out_grad[0]
    live = ns == 4 and nb == 8
    ring = Ring(nb, bi, live)
    info = jnp.concatenate([jnp.stack([si, lengths[0]]), ring.table()]).astype(jnp.int32)
    head_ids = si * heads + jnp.arange(heads, dtype=jnp.int32) + 1
    slopes = 2.0 ** (-8.0 * head_ids.astype(F32) / H)

    smalls = (first_gain, first_shift, joined_bias, output_bias, second_gain, second_shift, expand_bias, shrink_bias)
    smalls = [small.reshape(-1, rows) for small in smalls]
    seat = si.reshape(1).astype(jnp.int32)
    one = first_pack(seat, joined_weight, output_weight, smalls, cols, cw)
    jbias = None

    def step(held, t):
        if t < ring.half:
            held[t] = ring.back(held[t - 1])
        held[nb - t] = ring.ahead(held[(nb - t + 1) % nb])

    if live:
        cot, one = tie(cot, one)
        ones = {0: one}
        step(ones, 1)
        half = tok // 2
        near = lax.ppermute(x, "seq", pairs(ns, 1))
        far_a = lax.ppermute(x[:half], "seq", pairs(ns, 2))
        expand_weight, shrink_weight, _ = tie(expand_weight, shrink_weight, one)
        two = second_pack(seat, expand_weight, shrink_weight, nb, ns)
        ones[1], ones[7], two, near, cot, x = tie(ones[1], ones[7], two, near, cot, x)
        step(ones, 2)
        far_b = lax.ppermute(x[half:], "seq", pairs(ns, 2))
        cots = {0: cot, 1: lax.ppermute(cot, "seq", pairs(ns, 1))}
        ones[2], ones[6], cots[1], far_a, cot = tie(ones[2], ones[6], cots[1], far_a, cot)
        step(ones, 3)
        far_c = lax.ppermute(far_a, "seq", pairs(ns, 1))
        ones[3], ones[5], far_b, far_c, cot = tie(ones[3], ones[5], far_b, far_c, cot)
        step(ones, 4)
        far_d = lax.ppermute(far_b, "seq", pairs(ns, 1))
        cots[2] = lax.ppermute(cot, "seq", pairs(ns, 2))
        xs = [x, near, far_a, far_b, far_c, far_d]
        ones[4], two = tie(ones[4], two)
        twos = {0: two}
        step(twos, 1)
        one_parts = [ones[slot][None] for slot in range(nb)]
    else:
        xs = gather_rel(x, "seq", ns)
        xs = [xs[rel] for rel in range(ns)]
        cots = gather_rel(cot, "seq", ns)
        one_parts = [lax.all_gather(one, "batch")]
        low = one_parts[0][:, rows + 2 : rows + 4, :rows].astype(F32).reshape(2 * dim)
        low = lax.dynamic_slice(low, (si * 2 * cw,), (2 * cw,)).reshape(heads, 2, HD)
        jbias = jnp.stack([low[:, 0], jnp.zeros_like(low[:, 0]), low[:, 1]], 1).reshape(1, cols)

    normed, joined, joined_full, outw_own, vecs = first_call(
        info, jbias, xs, one_parts, cols, live, ns
    )
    if live:
        joined, twos[1], twos[7] = tie(joined, twos[1], twos[7])
        step(twos, 2)
    if live:
        ebias = vecs
    else:
        ebias = vecs[7:11].reshape(4, nb, rows).transpose(1, 0, 2).reshape(nb, ns, units)
        ebias = lax.dynamic_slice(ebias, (0, si, 0), (nb, 1, units)).reshape(1, ff)
    outw_all = gather_rel(outw_own, "seq", ns)
    attended = None
    for pair in range(np):
        attended = attend(joined, info, slopes, pair, attended)
        if live and pair == 0:
            out, joined, twos[2], twos[6], outw_all[1], outw_all[2], cots[2] = tie(
                attended[0], joined, twos[2], twos[6], outw_all[1], outw_all[2], cots[2]
            )
            attended = (out, attended[1])
            step(twos, 3)
            outw_all[3] = lax.ppermute(outw_all[2], "seq", pairs(ns, 1))
    mixed, log_sums = attended
    if live:
        mixed, twos[3], twos[5], outw_all[3], cots[2] = tie(mixed, twos[3], twos[5], outw_all[3], cots[2])
        step(twos, 4)
        cots[3] = lax.ppermute(cots[2], "seq", pairs(ns, 1))
    merged_parts = []
    for rel in range(ns):
        block = lax.dynamic_slice(mixed, ((si ^ rel) * tok, 0), (tok, cw))
        merged_parts.append(lax.ppermute(block, "seq", pairs(ns, rel)) if rel else block)
    if live:
        cots[3], twos[4], *merged_parts = tie(cots[3], twos[4], *merged_parts)
    merged, resid, second, outw_full = middle_call(
        info, x, vecs, merged_parts, [outw_all[rel] for rel in range(ns)]
    )
    out_parts = {}
    back_parts = {}
    activs = []
    pre_grads = []
    bias_sums = []
    if live:
        seconds = {0: second, 2: lax.ppermute(second, "seq", pairs(ns, 2)), 1: lax.ppermute(second, "seq", pairs(ns, 1))}
        two_parts = [twos[slot][None] for slot in range(nb)]
    else:
        seconds = gather_rel(second, "seq", ns)
        expand_part = expand_weight.reshape(rows, nb, ns, units)
        expand_part = lax.dynamic_slice(expand_part, (0, 0, si, 0), (rows, nb, 1, units)).reshape(rows, ff)
        shrink_part = lax.dynamic_slice(shrink_weight, (si * units, 0), (units, dim))
        two_parts = [lax.all_gather(expand_part, "batch"), lax.all_gather(shrink_part, "batch")]
    for rel in range(0, ns, 2):
        activ, pre_grad, oa, ob, ba, bb, bgrad = feed_call(
            info, seconds[rel], seconds[rel + 1], cots[rel], cots[rel + 1], ebias, two_parts, rows, units, nb, live
        )
        if live and rel == 0:
            activ, ob, bb, seconds[2] = tie(activ, ob, bb, seconds[2])
            seconds[3] = lax.ppermute(seconds[2], "seq", pairs(ns, 1))
            seconds[2], seconds[3] = tie(seconds[2], seconds[3])
            near_back = lax.ppermute(bb, "seq", pairs(ns, 1))
            near_out = lax.ppermute(ob, "seq", pairs(ns, 1))
        activs.append(activ)
        pre_grads.append(pre_grad)
        bias_sums.append(bgrad)
        out_parts.update({rel: oa, rel + 1: ob})
        back_parts.update({rel: ba, rel + 1: bb})
    if live:
        back_parts[3], near_back, near_out = tie(back_parts[3], near_back, near_out)
        far_back = lax.ppermute(back_parts[3], "seq", pairs(ns, 1))
        far_back, out_far = tie(far_back, out_parts[3])
        back_b = lax.ppermute(add16(back_parts[2], far_back), "seq", pairs(ns, 2))
        far_out = lax.ppermute(out_far, "seq", pairs(ns, 1))
    else:
        back_terms = (*scatter_rel(back_parts, "seq", ns, last=False), jnp.zeros((tok, dim), BF))
        out_a, out_b = scatter_rel(out_parts, "seq", ns, last=False)
    feed_stack = feed_grad_call(
        info,
        activs,
        [cots[rel] for rel in range(ns)],
        [seconds[rel] for rel in range(ns)],
        pre_grads,
        nb,
        live,
    )

    class Scatter:
        def __init__(self, parts):
            self.parts = [part[0] for part in parts]
            self.t = 0
            self.ahead = self.parts[ring.half]
            self.back = self.parts[ring.half + 1]

        def send(self):
            self.t += 1
            self.got_ahead = ring.ahead(self.ahead)
            self.got_back = ring.back(self.back) if self.t > 1 else None

        def take(self, *others):
            both = self.t > 1
            got = (self.got_ahead, self.got_back) if both else (self.got_ahead,)
            tied = tie(*got, *others)
            got, others = tied[: len(got)], tied[len(got) :]
            if self.t == ring.half:
                total = self.parts[0].astype(F32) + got[0].astype(F32) + got[1].astype(F32)
                return (total.astype(BF), *others)
            mine = self.parts[ring.half - self.t]
            if both:
                self.ahead, self.back = add_pairs((mine, self.parts[nb - ring.half + self.t]), got)
            else:
                self.ahead = add16(mine, got[0])
            return others

    if live:
        feed_ring = Scatter(feed_stack)
        feed_ring.send()
        back_b, far_out, _ = tie(back_b, far_out, feed_stack[0])
        out_b = add16(out_parts[2], far_out)
        back_b, out_b = tie(back_b, out_b)
        back_terms = (back_parts[0], near_back, back_b)
    resid_grad, branch, *mixed_grads, turn_sums = turn_call(
        info, back_terms, resid, cot, vecs, outw_full, ns, 1
    )
    outw_parts = split_grad(info, merged, branch, ns)
    sides = []

    grads = [
        lax.ppermute(block, "seq", pairs(ns, rel)) if rel else block for rel, block in enumerate(mixed_grads)
    ]
    if live:
        grads[0], *outw_parts = tie(grads[0], *outw_parts)
        grads = feed_ring.take(*grads)
        *grads, feed_ring.ahead, outw_near, out_b = tie(*grads, feed_ring.ahead, outw_parts[2], out_b)
        out_b = lax.ppermute(out_b, "seq", pairs(ns, 2))
        feed_ring.send()
        outw_near = lax.ppermute(outw_near, "seq", pairs(ns, 1))
    joined_grad = None
    for pair in range(np):
        joined_grad, side = attend_back(joined, grads, mixed, log_sums, info, slopes, pair, joined_grad)
        sides.append(side)
        if live and pair == 0:
            joined_grad, outw_near = feed_ring.take(joined_grad, outw_near)
            outw_far = add16(outw_parts[1], outw_near[1])
            joined_grad, joined, feed_ring.ahead, feed_ring.back, outw_far = tie(
                joined_grad, joined, feed_ring.ahead, feed_ring.back, outw_far
            )
            feed_ring.send()
            outw_far = lax.ppermute(outw_far, "seq", pairs(ns, 2))
        elif live:
            joined_grad, outw_far, out_b = feed_ring.take(joined_grad, outw_far, out_b)

    if live:
        shares = None
        outw_share = outw_parts[0].astype(F32) + outw_near[0].astype(F32) + outw_far.astype(F32)
        outw_share = outw_share.astype(BF)
        joined_grad, outw_share, feed_ring.ahead, feed_ring.back = tie(
            joined_grad, outw_share, feed_ring.ahead, feed_ring.back
        )
        feed_ring.send()
    else:
        spread_bias = lax.dynamic_update_slice(
            jnp.zeros((nb, ns, units), F32), sum(bias_sums).reshape(nb, 1, units), (0, si, 0)
        )
        spread_bias = spread_bias.reshape(nb, 4, rows).transpose(1, 0, 2).reshape(4, dim)
        side = jnp.concatenate(sides, 1).reshape(heads, 3, HD)
        side = jnp.stack([side[:, 0], side[:, 2]], 1).reshape(2 * cw)
        side = lax.dynamic_update_slice(jnp.zeros((2 * dim,), F32), side, (si * 2 * cw,))
        side = side.reshape(nb, 2, rows).transpose(1, 0, 2).reshape(2, dim)
        none = jnp.zeros((2, dim), F32)
        shares = [none, side, turn_sums[2:3], turn_sums[0:2], spread_bias, turn_sums[3:4], none, none]
        shares = jnp.concatenate(shares, 0)
        outw_share = scatter_rel(dict(enumerate(outw_parts)), "seq", ns)
    joined_stack = joined_grad_call(
        info, normed, joined_grad, sides, outw_share, joined_full, vecs, shares, turn_sums, bias_sums, nb, live
    )
    if live:
        feed_share, *joined_stack = feed_ring.take(*joined_stack)
        feed_share, *joined_stack = tie(feed_share, *joined_stack)
        feed_parts = {0: feed_share, 2: lax.ppermute(feed_share, "seq", pairs(ns, 2))}
        joined_ring = Scatter(joined_stack)
        joined_ring.send()
        joined_grad, _ = tie(joined_grad, joined_stack[0])
    normed_parts = last_call(info, joined_grad, joined_full, ns)

    def ordered(block):
        parts = gather_rel(block, "seq", ns)
        return [parts[rel] for rel in range(ns)]

    if live:
        sent, feed_parts[2] = joined_ring.take(normed_parts[2], feed_parts[2])
        joined_ring.ahead, sent = tie(joined_ring.ahead, sent)
        joined_ring.send()
        got = lax.ppermute(sent, "seq", pairs(ns, 1))
        far = add16(normed_parts[1], got[1])
        (far,) = joined_ring.take(far)
        joined_ring.ahead, joined_ring.back, far = tie(joined_ring.ahead, joined_ring.back, far)
        joined_ring.send()
        norm_b = lax.ppermute(far, "seq", pairs(ns, 2))
        out_b, out_parts[0], _ = tie(out_b, out_parts[0], far)
        out_terms = out_parts[0].astype(F32) + near_out.astype(F32) + out_b.astype(F32)
        layer_output = (resid + out_terms + vecs[11:12]).astype(BF)
        layer_output, feed_parts[0], feed_parts[2] = joined_ring.take(layer_output, feed_parts[0], feed_parts[2])
        joined_ring.ahead, joined_ring.back, feed_parts[0], feed_parts[2] = tie(
            joined_ring.ahead, joined_ring.back, feed_parts[0], feed_parts[2]
        )
        joined_ring.send()
        feed_parts[1] = lax.ppermute(feed_parts[0], "seq", pairs(ns, 1))
        feed_parts[3] = lax.ppermute(feed_parts[2], "seq", pairs(ns, 1))
        joined_share, norm_b, feed_parts[1], feed_parts[3] = joined_ring.take(norm_b, feed_parts[1], feed_parts[3])
        joined_share, norm_b, feed_parts[1] = tie(joined_share, norm_b, feed_parts[1])
        joined_parts = {0: joined_share, 2: lax.ppermute(joined_share, "seq", pairs(ns, 2))}
        joined_parts[1] = lax.ppermute(joined_share, "seq", pairs(ns, 1))
        expand_grad, shrink_grad = feed_out(info, [feed_parts[rel] for rel in range(ns)], nb, rows)
        input_grad = end_call((normed_parts[0], got, norm_b), x, resid_grad, vecs)
        joined_parts[2], joined_parts[1], input_grad, expand_grad, shrink_grad = tie(
            joined_parts[2], joined_parts[1], input_grad, expand_grad, shrink_grad
        )
        joined_parts[3] = lax.ppermute(joined_parts[2], "seq", pairs(ns, 1))
        joined_parts = [joined_parts[rel] for rel in range(ns)]
    else:
        layer_output = (resid + out_a.astype(F32) + out_b.astype(F32) + vecs[11:12]).astype(BF)
        norm_terms = scatter_rel(dict(enumerate(normed_parts)), "seq", ns, last=False)
        input_grad = end_call((*norm_terms, jnp.zeros((tok, dim), BF)), x, resid_grad, vecs)
        joined_share = lax.psum_scatter(joined_stack[0], "batch", scatter_dimension=0)
        expand_share = lax.psum_scatter(feed_stack[0], "batch", scatter_dimension=0)
        shrink_share = lax.psum_scatter(feed_stack[1], "batch", scatter_dimension=0)
        seats = jnp.arange(ns, dtype=jnp.int32) ^ si
        shrink_grad = jnp.take(jnp.stack(ordered(shrink_share)), seats, axis=0).astype(F32).reshape(ns * units, dim)
        expand_grad = jnp.take(jnp.stack(ordered(expand_share)), seats, axis=0).astype(F32)
        expand_grad = expand_grad.reshape(ns, rows, nb, units).transpose(1, 2, 0, 3).reshape(rows, ns * ff)
        joined_parts = ordered(joined_share)
    joined_wgrad, outw_grad, *small = joined_out(info, joined_parts, cols)
    small = [value.reshape(-1) for value in small]
    return (
        layer_output[None],
        input_grad[None],
        small[0],
        small[1],
        joined_wgrad,
        small[2],
        outw_grad,
        small[3],
        small[4],
        small[5],
        expand_grad,
        small[6],
        shrink_grad,
        small[7],
    )


def solution(mesh):
    row = P("batch")
    mat = P("batch", None)
    act = P("batch", "seq", None)
    return jax.shard_map(
        body,
        mesh=mesh,
        in_specs=(act, row, row, row, mat, row, mat, row, row, row, mat, row, mat, row, act),
        out_specs=(act, act, row, row, mat, row, mat, row, row, row, mat, row, mat, row),
        check_vma=False,
    )
```

```python
import functools

import jax
import jax.numpy as jnp
from jax import lax
from jax.experimental import pallas as pl
from jax.experimental.pallas import tpu as pltpu
from jax.sharding import PartitionSpec as P

H = 16
HD = 64
EPSILON = 1e-05
F32 = jnp.float32
BF = jnp.bfloat16
NT = (((1,), (1,)), ((), ()))
NN = (((1,), (0,)), ((), ()))
TN = (((0,), (0,)), ((), ()))
MIB = 2**20
SHRINK = 1000


def dg(left, right, dims):
    return lax.dot_general(left, right, dims, preferred_element_type=F32)


def params(limit=56):
    return pltpu.CompilerParams(vmem_limit_bytes=limit * MIB)


def cost(flops, moved, exps=0):
    return pl.CostEstimate(flops=flops // SHRINK, bytes_accessed=moved // SHRINK, transcendentals=exps // SHRINK)


def norm_parts(values):
    mean = jnp.mean(values, axis=-1, keepdims=True)
    centered = values - mean
    scale = lax.rsqrt(jnp.mean(centered * centered, axis=-1, keepdims=True) + EPSILON)
    return centered * scale, scale


def norm_back(grad, unit, scale, gain):
    scaled = grad * gain
    return scale * (
        scaled
        - jnp.mean(scaled, axis=-1, keepdims=True)
        - unit * jnp.mean(scaled * unit, axis=-1, keepdims=True)
    )


def pairs(size, bit):
    return [(i, i ^ bit) for i in range(size)]


def bits_low_last(size):
    bits = []
    bit = 2
    while bit < size:
        bits.append(bit)
        bit *= 2
    if size > 1:
        bits.append(1)
    return bits


def add16(left, right):
    return (left.astype(F32) + right.astype(F32)).astype(BF)


def gather_rel(block, axis, size):
    out = {0: block}
    for bit in bits_low_last(size):
        for rel in list(out):
            out[rel | bit] = lax.ppermute(out[rel], axis, pairs(size, bit))
    return out


def scatter_rel(parts, axis, size, last=True):
    parts = dict(parts)
    order = bits_low_last(size)[::-1]
    for bit in order:
        for rel in sorted(parts, reverse=True):
            if rel & bit:
                other = lax.ppermute(parts.pop(rel), axis, pairs(size, bit))
                if bit == order[-1] and not last:
                    return parts[0], other
                parts[rel ^ bit] = add16(parts[rel ^ bit], other)
    return parts[0]


def tie(*values):
    return lax.optimization_barrier(values)


class Ring:
    def __init__(self, size, index, live):
        self.size = size
        self.live = live
        order = list(range(0, size, 2)) + list(range(size - 1, 0, -2))
        self.forward = [(order[i], order[(i + 1) % size]) for i in range(size)]
        self.backward = [(b, a) for a, b in self.forward]
        count = jnp.arange(size, dtype=jnp.int32)
        place = lambda k: jnp.where(k % 2 == 0, k // 2, size - (k + 1) // 2)
        if self.live:
            self.slots = (place(count) - place(index) + size) % size
            seat = (place(index) + count) % size
            self.owners = jnp.where(seat < size // 2, 2 * seat, 2 * (size - seat) - 1)
        else:
            self.slots = count
            self.owners = count
        self.half = size // 2

    def table(self):
        return jnp.concatenate([self.slots, self.owners])

    def ahead(self, value):
        return lax.ppermute(value, "batch", self.forward)

    def back(self, value):
        return lax.ppermute(value, "batch", self.backward)


def owner_at(info, live, nb, slot):
    return info[2 + nb + slot] if live else slot


def put(outs, slot, value, rows, cols):
    if len(outs) == 1:
        outs[0][slot, rows, cols] = value
        return
    for at, out in enumerate(outs):

        @pl.when(slot == at)
        def _():
            out[0, rows, cols] = value


def blocks_of(refs):
    out = []
    for ref in refs:
        out += [(ref, at) for at in range(ref.shape[0])]
    return out


def once(shape):
    return pl.BlockSpec(shape, lambda i, *_: (0,) * len(shape), pipeline_mode=pl.Buffered(1))


def first_pack_kernel(info, joined, outw, *refs):
    smalls, out = refs[:-1], refs[-1]
    rows, cols = joined.shape
    out[:rows, :cols] = joined[...]
    out[:rows, cols:] = outw[...]
    pieces = [small[...].astype(F32) for small in smalls]
    count = sum(piece.shape[0] for piece in pieces)
    pieces.append(jnp.zeros((16 - count, rows), F32))
    out[rows:, :rows] = jnp.concatenate(pieces, 0).astype(BF)
    out[rows:, rows:] = jnp.zeros((16, out.shape[1] - rows), BF)


def first_pack(info, joined, outw, smalls, cols, cw):
    rows = joined.shape[0]
    shape = (rows + 16, cols + cw)
    return pl.pallas_call(
        first_pack_kernel,
        grid_spec=pltpu.PrefetchScalarGridSpec(
            num_scalar_prefetch=1,
            grid=(1,),
            in_specs=[
                pl.BlockSpec((rows, cols), lambda i, info: (0, info[0])),
                pl.BlockSpec((rows, cw), lambda i, info: (0, info[0])),
            ]
            + [once(small.shape) for small in smalls],
            out_specs=pl.BlockSpec(shape, lambda i, info: (0, 0)),
        ),
        out_shape=jax.ShapeDtypeStruct(shape, BF),
        compiler_params=params(60),
        name="first_pack",
    )(info, joined, outw, *smalls)


def second_pack_kernel(nb, ns, units, info, expand, shrink, out):
    rows = expand.shape[0]
    for k in range(nb):
        col = pl.ds(pl.multiple_of((k * ns + info[0]) * units, units), units)
        out[:rows, k * units : (k + 1) * units] = expand[:, col]
    out[rows:] = shrink[...]


def second_pack(info, expand, shrink, nb, ns):
    rows, wide = expand.shape
    dim = shrink.shape[1]
    units = shrink.shape[0] // ns
    return pl.pallas_call(
        functools.partial(second_pack_kernel, nb, ns, units),
        grid_spec=pltpu.PrefetchScalarGridSpec(
            num_scalar_prefetch=1,
            grid=(1,),
            in_specs=[
                pl.BlockSpec((rows, wide), lambda i, info: (0, 0)),
                pl.BlockSpec((units, dim), lambda i, info: (info[0], 0)),
            ],
            out_specs=pl.BlockSpec((rows + units, dim), lambda i, info: (0, 0)),
        ),
        out_shape=jax.ShapeDtypeStruct((rows + units, dim), BF),
        compiler_params=params(60),
        name="second_pack",
    )(info, expand, shrink)


def first_kernel(starts, nb, rows, cols, live, info, *refs):
    jbias_in, refs = (None, refs) if live else (refs[0], refs[1:])
    count = len(starts) - 1
    xs, weights = refs[:count], refs[count:-6]
    normed, joined, full, outw, vecs, jbias = refs[-6:]
    step = pl.program_id(0)

    @pl.when(step == 0)
    def _():
        for slot, (ref, at) in enumerate(blocks_of(weights)):
            high = owner_at(info, live, nb, slot) * rows
            high = pl.multiple_of(high, rows) if live else high
            full[pl.ds(high, rows)] = ref[at, :rows, :cols]
            outw[pl.ds(high, rows)] = ref[at, :rows, cols:]
            vecs[:, pl.ds(high, rows)] = ref[at, rows:, :rows].astype(F32)
        if live:
            heads = cols // (3 * HD)
            for head in range(heads):
                at = info[0] * heads + head
                col = pl.ds(pl.multiple_of(lax.div(at, 2) * rows, rows), rows)
                row = vecs[0:8, col][2 + head % 2 : 3 + head % 2]
                pieces = [row[:, :HD], jnp.zeros((1, HD), F32), row[:, HD:]]
                jbias[:, head * 3 * HD : (head + 1) * 3 * HD] = jnp.concatenate(pieces, 1)
        else:
            jbias[...] = jbias_in[...]

    for at in range(count):

        @pl.when((step >= starts[at]) & (step < starts[at + 1]))
        def _():
            unit, _ = norm_parts(xs[at][...].astype(F32))
            value = (unit * vecs[0:1] + vecs[1:2]).astype(BF)
            normed[...] = value
            joined[...] = (dg(value, full[...], NN) + jbias[...]).astype(BF)


def first_call(info, jbias, xs, weights, cols, live, ns):
    dim = xs[0].shape[1]
    tok = sum(piece.shape[0] for piece in xs) // ns
    nb = sum(weight.shape[0] for weight in weights)
    rows = dim // nb
    cw = weights[0].shape[2] - cols
    tile = min(256, tok)
    nt = tok // tile
    starts = [0]
    for piece in xs:
        starts.append(starts[-1] + piece.shape[0] // tile)
    extra = [] if live else [jbias]
    place = lambda i, info: ((info[0] ^ lax.div(i, nt)) * nt + lax.rem(i, nt), 0)

    def source(at):
        last = starts[at + 1] - starts[at] - 1
        return pl.BlockSpec((tile, dim), lambda i, info: (jnp.clip(i - starts[at], 0, last), 0))

    return pl.pallas_call(
        functools.partial(first_kernel, starts, nb, rows, cols, live),
        grid_spec=pltpu.PrefetchScalarGridSpec(
            num_scalar_prefetch=1,
            grid=(ns * nt,),
            in_specs=[once(value.shape) for value in extra]
            + [source(at) for at in range(len(xs))]
            + [once(weight.shape) for weight in weights],
            out_specs=[
                pl.BlockSpec((tile, dim), place),
                pl.BlockSpec((tile, cols), place),
                once((dim, cols)),
                once((dim, cw)),
                once((16, dim)),
            ],
            scratch_shapes=[pltpu.VMEM((1, cols), F32)],
        ),
        out_shape=[
            jax.ShapeDtypeStruct((ns * tok, dim), BF),
            jax.ShapeDtypeStruct((ns * tok, cols), BF),
            jax.ShapeDtypeStruct((dim, cols), BF),
            jax.ShapeDtypeStruct((dim, cw), BF),
            jax.ShapeDtypeStruct((16, dim), F32),
        ],
        compiler_params=params(60),
        cost_estimate=cost(2 * ns * tok * dim * cols, 2 * ns * tok * (2 * dim + cols)),
        name="first",
    )(info, *extra, *xs, *weights)


def three(value):
    high = value.astype(BF)
    rest = value - high.astype(F32)
    mid = rest.astype(BF)
    return high, mid, (rest - mid.astype(F32)).astype(BF)


def spread(lane, base, columns):
    for at, column in columns:
        base = jnp.where(lane == at, column.astype(F32), base)
    return base.astype(BF)


def key_extra(count, slope, length):
    lane = lax.broadcasted_iota(jnp.int32, (count, HD), 1)
    pos = lax.broadcasted_iota(jnp.int32, (count, HD), 0)
    high, mid, low = three(slope * pos.astype(F32))
    dead = jnp.where(pos < length, 0.0, -1e30)
    return spread(lane, jnp.where(lane < 7, 1.0, 0.0), [(0, high), (1, mid), (2, low), (3, dead)])


def attend_kernel(count, size, pair, info, slopes, joined, mixed, sums, keys):
    lane = lax.broadcasted_iota(jnp.int32, (size, HD), 1)
    ones = jnp.where(lane < 4, 1.0, 0.0).astype(BF)
    for hh in range(2):
        base = 3 * HD * hh
        extra = key_extra(count, slopes[2 * pair + hh], info[1])
        keys[hh] = jnp.concatenate([joined[:, base + HD : base + 2 * HD], extra], 1)
    query_at = lax.broadcasted_iota(jnp.int32, (size, size), 0)
    key_at = lax.broadcasted_iota(jnp.int32, (size, size), 1)
    for block in range(count // size):
        low = block * size
        high = low + size
        outs = []
        logs = []
        for hh in range(2):
            base = 3 * HD * hh
            query = (joined[low:high, base : base + HD].astype(F32) * 0.125).astype(BF)
            query = jnp.concatenate([query, ones], 1)
            near = jnp.where(key_at <= query_at, dg(query, keys[hh, low:high], NT), -1e30)
            top = jnp.max(near, axis=1, keepdims=True)
            if block:
                far = dg(query, keys[hh, 0:low], NT)
                top = jnp.maximum(top, jnp.max(far, axis=1, keepdims=True))
            near = jnp.exp(near - top)
            total = jnp.sum(near, axis=1, keepdims=True)
            acc = dg(near.astype(BF), joined[low:high, base + 2 * HD : base + 3 * HD], NN)
            if block:
                far = jnp.exp(far - top)
                total += jnp.sum(far, axis=1, keepdims=True)
                acc += dg(far.astype(BF), joined[0:low, base + 2 * HD : base + 3 * HD], NN)
            outs.append(acc / total)
            logs.append(jnp.broadcast_to(top + jnp.log(total), (size, HD)))
        mixed[low:high] = jnp.concatenate(outs, 1).astype(BF)
        sums[low:high] = jnp.concatenate(logs, 1)


def attend(joined, info, slopes, pair, held):
    count, width = joined.shape
    groups = width // (6 * HD)
    smem = pl.BlockSpec(memory_space=pltpu.SMEM)
    narrow = pl.BlockSpec((count, 2 * HD), lambda i: (0, pair))
    area = count * count
    extra = [] if held is None else list(held)

    def kernel(*refs):
        attend_kernel(count, min(512, count), pair, *refs[:3], *refs[3 + len(extra) :])

    return pl.pallas_call(
        kernel,
        grid=(1,),
        in_specs=[smem, smem, pl.BlockSpec((count, 6 * HD), lambda i: (0, pair))]
        + [pl.BlockSpec(memory_space=pl.ANY)] * len(extra),
        out_specs=[narrow, narrow],
        out_shape=[
            jax.ShapeDtypeStruct((count, groups * 2 * HD), BF),
            jax.ShapeDtypeStruct((count, groups * 2 * HD), F32),
        ],
        input_output_aliases={3: 0, 4: 1} if extra else {},
        scratch_shapes=[pltpu.VMEM((2, count, 2 * HD), BF)],
        compiler_params=params(60),
        cost_estimate=cost(area * 1024, 20 * count * HD, area),
        name="attend",
    )(info, slopes, joined, *extra)


def attend_back_kernel(count, size, ns, pair, info, slopes, joined, mixed, sums, *refs):
    pieces_in = refs[:ns]
    out, sides, keys, queries, values, grads, query_grad = refs[ns:]
    tok = count // ns
    lane = lax.broadcasted_iota(jnp.int32, (count, HD), 1)
    near_lane = lax.broadcasted_iota(jnp.int32, (tok, HD), 1)
    for hh in range(2):
        base = 3 * HD * hh
        half = slice(hh * HD, (hh + 1) * HD)
        extra = key_extra(count, slopes[2 * pair + hh], info[1])
        keys[hh] = jnp.concatenate([joined[:, base + HD : base + 2 * HD], extra], 1)
        query = (joined[:, base : base + HD].astype(F32) * 0.125).astype(BF)
        high, mid, low = three(-sums[:, half])
        extra = spread(lane, jnp.where(lane < 4, 1.0, 0.0), [(4, high), (5, mid), (6, low)])
        queries[hh] = jnp.concatenate([query, extra], 1)
        ones = jnp.where(lane < 3, 1.0, 0.0).astype(BF)
        values[hh] = jnp.concatenate([joined[:, base + 2 * HD : base + 3 * HD], ones], 1)
        for rel in range(ns):
            at = pl.ds(pl.multiple_of((info[0] ^ rel) * tok, tok), tok)
            part = pieces_in[rel][:, half]
            inner = jnp.sum(part.astype(F32) * mixed[at, half].astype(F32), axis=1, keepdims=True)
            high, mid, low = three(jnp.broadcast_to(-inner, (tok, HD)))
            extra = spread(near_lane, jnp.zeros((tok, HD), F32), [(0, high), (1, mid), (2, low)])
            grads[hh, at] = jnp.concatenate([part, extra], 1)
    key_at = lax.broadcasted_iota(jnp.int32, (size, size), 0)
    query_at = lax.broadcasted_iota(jnp.int32, (size, size), 1)
    blocks = count // size
    for j in range(blocks):
        ks = slice(j * size, (j + 1) * size)
        pieces = []
        for hh in range(2):
            key_sum = None
            for i in range(j, blocks):
                qs = slice(i * size, (i + 1) * size)
                probs = jnp.exp(dg(keys[hh, ks], queries[hh, qs], NT))
                if i == j:
                    probs = jnp.where(key_at <= query_at, probs, 0.0)
                slope = (probs * dg(values[hh, ks], grads[hh, qs], NT)).astype(BF)
                value_part = dg(probs.astype(BF), grads[hh, qs], NN)
                key_part = dg(slope, queries[hh, qs], NN)
                query_part = dg(keys[hh, ks], slope, TN)
                value_sum = value_part if key_sum is None else value_sum + value_part
                key_sum = key_part if key_sum is None else key_sum + key_part
                query_grad[hh, :, qs] = query_part if j == 0 else query_grad[hh, :, qs] + query_part
            pieces += [jnp.zeros((size, HD), F32), key_sum[:, :HD], value_sum[:, :HD]]
        out[ks] = jnp.concatenate(pieces, 1).astype(BF)
    for hh in range(2):
        base = 3 * HD * hh
        out[:, base : base + HD] = (query_grad[hh].T[:, :HD] * 0.125).astype(BF)
    sides[...] = jnp.sum(out[...].astype(F32), axis=0, keepdims=True)


def attend_back(joined, grads, mixed, sums, info, slopes, pair, held):
    count, width = joined.shape
    ns = len(grads)
    smem = pl.BlockSpec(memory_space=pltpu.SMEM)
    wide = pl.BlockSpec((count, 6 * HD), lambda i: (0, pair))
    narrow = pl.BlockSpec((count, 2 * HD), lambda i: (0, pair))
    piece = pl.BlockSpec((count // ns, 2 * HD), lambda i: (0, pair))
    area = count * count
    extra = [] if held is None else [held]

    def kernel(*refs):
        inputs, rest = refs[: 5 + ns], refs[5 + ns + len(extra) :]
        attend_back_kernel(count, min(512, count), ns, pair, *inputs, *rest)

    return pl.pallas_call(
        kernel,
        grid=(1,),
        in_specs=[smem, smem, wide, narrow, narrow]
        + [piece] * ns
        + [pl.BlockSpec(memory_space=pl.ANY)] * len(extra),
        out_specs=[wide, pl.BlockSpec((1, 6 * HD), lambda i: (0, 0))],
        out_shape=[jax.ShapeDtypeStruct((count, width), BF), jax.ShapeDtypeStruct((1, 6 * HD), F32)],
        input_output_aliases={5 + ns: 0} if extra else {},
        scratch_shapes=[pltpu.VMEM((2, count, 2 * HD), BF)] * 4 + [pltpu.VMEM((2, 2 * HD, count), F32)],
        compiler_params=params(60),
        cost_estimate=cost(area * 2560, 40 * count * HD, area),
        name="attend_back",
    )(info, slopes, joined, mixed, sums, *grads, *extra)


def middle_kernel(ns, np, info, x, vecs, *refs):
    mixed, weights = refs[: ns * np], refs[ns * np : ns * np + ns]
    merged, resid, second, full = refs[ns * np + ns :]
    cw = weights[0].shape[1]
    pw = cw // np

    @pl.when(pl.program_id(0) == 0)
    def _():
        for rel in range(ns):
            full[:, pl.ds(pl.multiple_of((info[0] ^ rel) * cw, cw), cw)] = weights[rel][...]

    for pair in range(np):
        for rel in range(ns):
            col = pl.ds(pl.multiple_of((info[0] ^ rel) * cw + pair * pw, pw), pw)
            merged[:, col] = mixed[pair * ns + rel][...]
    value = x[...].astype(F32) + dg(merged[...], full[...], NN) + vecs[4:5]
    resid[...] = value
    unit, _ = norm_parts(value)
    second[...] = (unit * vecs[5:6] + vecs[6:7]).astype(BF)


def middle_call(info, x, vecs, mixed, weights):
    tok, dim = x.shape
    ns = len(weights)
    np = len(mixed) // ns
    tile = min(256, tok)
    part = lambda width: pl.BlockSpec((tile, width), lambda i, info: (i, 0))
    return pl.pallas_call(
        functools.partial(middle_kernel, ns, np),
        grid_spec=pltpu.PrefetchScalarGridSpec(
            num_scalar_prefetch=1,
            grid=(tok // tile,),
            in_specs=[part(dim), once(vecs.shape)]
            + [part(block.shape[1]) for block in mixed]
            + [once(weight.shape) for weight in weights],
            out_specs=[part(dim), part(dim), part(dim), once((dim, dim))],
        ),
        out_shape=[
            jax.ShapeDtypeStruct((tok, dim), BF),
            jax.ShapeDtypeStruct((tok, dim), F32),
            jax.ShapeDtypeStruct((tok, dim), BF),
            jax.ShapeDtypeStruct((dim, dim), BF),
        ],
        compiler_params=params(60),
        cost_estimate=cost(2 * tok * dim * dim, 12 * tok * dim + 4 * dim * dim),
        name="middle",
    )(info, x, vecs, *mixed, *weights)


def feed_kernel(nt, nb, rows, units, live, info, sa, sb, ca, cb, ebias, *refs):
    weights = refs[:-9]
    activ, pre_grad, oa, ob, ba, bb, bgrad, wide, tall = refs[-9:]
    step = pl.program_id(0)
    bias = ebias[...]
    if live:
        row = lax.broadcasted_iota(jnp.int32, bias.shape, 0)
        bias = jnp.sum(jnp.where(row == 7 + info[0], bias, 0.0), axis=0, keepdims=True)

    @pl.when(step == 0)
    def _():
        blocks = blocks_of(weights)
        for slot in range(nb):
            owner = owner_at(info, live, nb, slot)
            high = pl.multiple_of(owner * rows, rows) if live else owner * rows
            deep = pl.multiple_of(owner * units, units) if live else owner * units
            if len(blocks) == nb:
                ref, at = blocks[slot]
                wide[pl.ds(high, rows)] = ref[at, :rows]
                tall[pl.ds(deep, units)] = ref[at, rows:]
            else:
                wide[pl.ds(high, rows)] = weights[0][slot]
                tall[pl.ds(deep, units)] = weights[1][slot]
        bgrad[...] = jnp.zeros_like(bgrad)

    def work(second, cot, out, back):
        pre = dg(second[...], wide[...], NN) + bias
        square = pre * pre
        bend = jnp.tanh(0.7978845608028654 * pre * (1.0 + 0.044715 * square))
        half = 0.5 + 0.5 * bend
        act = (pre * half).astype(BF)
        activ[...] = act
        out[...] = dg(act, tall[...], NN).astype(BF)
        steep = half + pre * (0.5 - 0.5 * bend * bend) * (0.7978845608028654 + 0.10703222440890037 * square)
        grad = (dg(cot[...], tall[...], NT) * steep).astype(BF)
        pre_grad[...] = grad
        bgrad[...] += jnp.sum(grad.astype(F32), axis=0, keepdims=True)
        back[...] = dg(grad, wide[...], NT).astype(BF)

    @pl.when(step < nt)
    def _():
        work(sa, ca, oa, ba)

    @pl.when(step >= nt)
    def _():
        work(sb, cb, ob, bb)


def feed_call(info, sa, sb, ca, cb, ebias, weights, rows, units, nb, live):
    tok, dim = sa.shape
    ff = ebias.shape[1]
    tile = min(256, tok)
    nt = tok // tile
    left = pl.BlockSpec((tile, dim), lambda i, info: (jnp.minimum(i, nt - 1), 0))
    right = pl.BlockSpec((tile, dim), lambda i, info: (jnp.maximum(i - nt, 0), 0))
    flat = pl.BlockSpec((tile, ff), lambda i, info: (i, 0))
    shape = jax.ShapeDtypeStruct((tok, dim), BF)
    return pl.pallas_call(
        functools.partial(feed_kernel, nt, nb, rows, units, live),
        grid_spec=pltpu.PrefetchScalarGridSpec(
            num_scalar_prefetch=1,
            grid=(2 * nt,),
            in_specs=[left, right, left, right, once(ebias.shape)] + [once(weight.shape) for weight in weights],
            out_specs=[flat, flat, left, right, left, right, pl.BlockSpec((1, ff), lambda i, info: (0, 0))],
            scratch_shapes=[pltpu.VMEM((dim, ff), BF), pltpu.VMEM((ff, dim), BF)],
        ),
        out_shape=[jax.ShapeDtypeStruct((2 * tok, ff), BF)] * 2
        + [shape] * 4
        + [jax.ShapeDtypeStruct((1, ff), F32)],
        compiler_params=params(60),
        cost_estimate=cost(16 * tok * dim * ff, 16 * tok * dim + 8 * dim * ff, 2 * tok * ff),
        name="feed",
    )(info, sa, sb, ca, cb, ebias, *weights)


def feed_grad_kernel(ns, nb, rows, units, steps, info, *refs):
    half = ns // 2
    activs, cots, seconds, grads = refs[:half], refs[half : half + ns], refs[half + ns : half + 2 * ns], refs[half + 2 * ns : 2 * half + 2 * ns]
    outs = refs[2 * half + 2 * ns :]
    step = pl.program_id(0)

    def total(wides, thins, wide_left):
        out = None
        for rel in range(ns):
            thin = thins[rel]
            tok = thin.shape[0]
            wide = wides[rel // 2][(rel % 2) * tok : (rel % 2 + 1) * tok]
            term = dg(wide, thin[...], TN) if wide_left else dg(thin[...], wide, TN)
            out = term if out is None else out + term
        return out.astype(BF)

    def store(value, high, count, at, low):
        for k in range(value.shape[0] // count):
            slot = info[2 + at * (value.shape[0] // count) + k]
            piece = value[k * count : (k + 1) * count]
            if len(outs) == nb:
                for mine, out in enumerate(outs):

                    @pl.when(slot == mine)
                    def _():
                        out[0, low : low + count] = piece

            else:
                outs[0 if high else 1][slot] = piece

    @pl.when(step < steps)
    def _():
        store(total(activs, cots, True), False, units, step, rows)

    @pl.when(step >= steps)
    def _():
        store(total(grads, seconds, False), True, rows, step - steps, 0)


def feed_grad_call(info, activs, cots, seconds, grads, nb, live):
    ns = len(cots)
    dim = cots[0].shape[1]
    ff = activs[0].shape[1]
    rows, units = dim // nb, ff // nb
    tile = 512
    steps = ff // tile
    tok = ns * cots[0].shape[0]
    left = lambda a: pl.BlockSpec((a.shape[0], tile), lambda i, info: (0, jnp.minimum(i, steps - 1)))
    right = lambda a: pl.BlockSpec((a.shape[0], tile), lambda i, info: (0, jnp.maximum(i - steps, 0)))
    fixed = lambda a: once(a.shape)
    shapes = [(1, rows + units, dim)] * nb if live else [(nb, rows, ff), (nb, units, dim)]
    return pl.pallas_call(
        functools.partial(feed_grad_kernel, ns, nb, rows, units, steps),
        grid_spec=pltpu.PrefetchScalarGridSpec(
            num_scalar_prefetch=1,
            grid=(steps + dim // tile,),
            in_specs=[left(a) for a in activs]
            + [fixed(a) for a in cots]
            + [right(a) for a in seconds]
            + [fixed(a) for a in grads],
            out_specs=[once(shape) for shape in shapes],
        ),
        out_shape=[jax.ShapeDtypeStruct(shape, BF) for shape in shapes],
        compiler_params=params(60),
        cost_estimate=cost(4 * tok * dim * ff, 4 * tok * (dim + ff) + 4 * dim * ff),
        name="feed_grad",
    )(info, *activs, *cots, *seconds, *grads)


def pair_shapes(shape, ns):
    return [shape, shape, (2, *shape)] if ns == 4 else [shape] * ns


def pair_put(outs, ns, rel, rows, value):
    if ns == 4 and rel % 2:
        outs[2][rel // 2, rows] = value
    elif ns == 4:
        outs[rel // 2][rows] = value
    else:
        outs[rel][rows] = value


def split_grad_kernel(ns, info, left, right, *refs):
    outs, held = refs[:-1], refs[-1]
    held[...] = dg(left[...], right[...], TN)
    tile = held.shape[0]
    cw = held.shape[1] // ns
    rows = pl.ds(pl.multiple_of(pl.program_id(0) * tile, tile), tile)
    for rel in range(ns):
        col = pl.ds(pl.multiple_of((info[0] ^ rel) * cw, cw), cw)
        pair_put(outs, ns, rel, rows, held[:, col].astype(BF))


def split_grad(info, left, right, ns):
    tok, dim = left.shape
    tile = 256
    shapes = pair_shapes((dim, dim // ns), ns)
    return pl.pallas_call(
        functools.partial(split_grad_kernel, ns),
        grid_spec=pltpu.PrefetchScalarGridSpec(
            num_scalar_prefetch=1,
            grid=(dim // tile,),
            in_specs=[pl.BlockSpec((tok, tile), lambda i, info: (0, i)), once((tok, dim))],
            out_specs=[once(shape) for shape in shapes],
            scratch_shapes=[pltpu.VMEM((tile, dim), F32)],
        ),
        out_shape=[jax.ShapeDtypeStruct(shape, BF) for shape in shapes],
        compiler_params=params(60),
        cost_estimate=cost(2 * tok * dim * dim, 6 * dim * dim),
        name="split_grad",
    )(info, left, right)


def joined_grad_kernel(nb, rows, np, terms, live, info, left, weight, vecs, *refs):
    others, refs = refs[:terms], refs[terms:]
    other = others[0][...].astype(F32)
    for term in others[1:]:
        other += term[...].astype(F32)
    other = other.astype(BF)
    smalls, refs = (refs[:3], refs[3:]) if live else (refs[:1], refs[1:])
    right, sides, outs = refs[0], refs[1 : 1 + np], refs[1 + np :]
    total = dg(left[...], right[...], TN)
    tile, cw = other.shape
    cols = weight.shape[1]
    first = pl.program_id(0) * (tile // rows)
    low = total.astype(BF)
    weights = weight[...].astype(F32)
    moment = jnp.sum(total * weights, axis=1, keepdims=True)
    shift = jnp.sum(jnp.concatenate([side[...] for side in sides], 1) * weights, axis=1, keepdims=True)
    moment = jnp.broadcast_to(moment, (tile, 128)).T[:1]
    shift = jnp.broadcast_to(shift, (tile, 128)).T[:1]
    gain = (moment - vecs[1:2] * shift) / vecs[0:1]
    row = lax.broadcasted_iota(jnp.int32, (16, tile), 0)
    held = jnp.zeros((16, tile), F32) if live else smalls[0][...]
    held = jnp.where(row == 0, gain, jnp.where(row == 1, shift, held))
    if live:
        turned = smalls[0][...]
        for at, source in ((4, 2), (5, 0), (6, 1), (11, 3)):
            held = jnp.where(row == at, turned[source : source + 1], held)
        held = jnp.where(row == 7 + info[0], smalls[1][...] + smalls[2][...], held)
        for part in range(2):
            pieces = []
            for side in sides:
                base = part * 3 * HD
                pieces += [side[:, base : base + HD], side[:, base + 2 * HD : base + 3 * HD]]
            bias = jnp.where(pl.program_id(0) == info[0], jnp.concatenate(pieces, 1), 0.0)
            held = jnp.where(row == 2 + part, bias, held)
    held = held.astype(BF)
    for k in range(tile // rows):
        slot = info[2 + first + k]
        high = slice(k * rows, (k + 1) * rows)
        put(outs, slot, low[high], slice(0, rows), slice(0, cols))
        put(outs, slot, other[high], slice(0, rows), slice(cols, cols + cw))
        put(outs, slot, held[:, high], slice(rows, rows + 16), slice(0, rows))


def joined_grad_call(info, left, right, sides, others, weight, vecs, shares, turned, biases, nb, live):
    count, dim = left.shape
    cols = weight.shape[1]
    cw = others[0].shape[1]
    rows = dim // nb
    tile = 256
    wide = (rows + 16, cols + cw)
    shapes = [(1, *wide)] * nb if live else [(nb, *wide)]
    flat = lambda width: pl.BlockSpec((tile, width), lambda i, info: (i, 0))
    first = lambda width: pl.BlockSpec((None, tile, width), lambda i, info: (0, i, 0))
    tall = lambda value: pl.BlockSpec((value.shape[0], tile), lambda i, info: (0, i))
    smalls = (turned, *biases) if live else (shares,)
    return pl.pallas_call(
        functools.partial(joined_grad_kernel, nb, rows, len(sides), len(others), live),
        grid_spec=pltpu.PrefetchScalarGridSpec(
            num_scalar_prefetch=1,
            grid=(dim // tile,),
            in_specs=[pl.BlockSpec((count, tile), lambda i, info: (0, i)), flat(cols), tall(vecs)]
            + [first(cw) if term.ndim == 3 else flat(cw) for term in others]
            + [tall(value) for value in smalls]
            + [once(value.shape) for value in (right, *sides)],
            out_specs=[once(shape) for shape in shapes],
        ),
        out_shape=[jax.ShapeDtypeStruct(shape, BF) for shape in shapes],
        compiler_params=params(60),
        cost_estimate=cost(2 * count * dim * cols, 2 * count * (dim + cols) + 4 * dim * dim),
        name="joined_grad",
    )(info, left, weight, vecs, *others, *smalls, right, *sides)


def turn_kernel(ns, np, cw, info, ga, gb, gc, resid, cot, vecs, full, resid_grad, branch, *refs):
    mixed_grads, sums, held = refs[: ns * np], refs[ns * np], refs[ns * np + 1]

    @pl.when(pl.program_id(0) == 0)
    def _():
        sums[...] = jnp.zeros_like(sums)

    grad = ga[...].astype(F32) + gb[...].astype(F32) + gc[...].astype(F32)
    unit, scale = norm_parts(resid[...])
    outer = cot[...].astype(F32)
    value = outer + norm_back(grad, unit, scale, vecs[5:6])
    resid_grad[...] = value
    low = value.astype(BF)
    branch[...] = low
    held[...] = dg(low, full[...], NT).astype(BF)
    pw = cw // np
    for pair in range(np):
        for rel in range(ns):
            col = pl.ds(pl.multiple_of((info[0] ^ rel) * cw + pair * pw, pw), pw)
            mixed_grads[pair * ns + rel][...] = held[:, col]
    for at, term in enumerate((grad * unit, grad, low.astype(F32), outer)):
        sums[at : at + 1] += jnp.sum(term, axis=0, keepdims=True)


def turn_call(info, terms, resid, cot, vecs, full, ns, np):
    tok, dim = resid.shape
    cw = dim // ns
    tile = min(256, tok)
    part = pl.BlockSpec((tile, dim), lambda i, info: (i, 0))
    return pl.pallas_call(
        functools.partial(turn_kernel, ns, np, cw),
        grid_spec=pltpu.PrefetchScalarGridSpec(
            num_scalar_prefetch=1,
            grid=(tok // tile,),
            in_specs=[part, part, part, part, part, once(vecs.shape), once(full.shape)],
            out_specs=[part, part]
            + [pl.BlockSpec((tile, cw // np), lambda i, info: (i, 0))] * (ns * np)
            + [pl.BlockSpec((8, dim), lambda i, info: (0, 0))],
            scratch_shapes=[pltpu.VMEM((tile, dim), BF)],
        ),
        out_shape=[
            jax.ShapeDtypeStruct((tok, dim), F32),
            jax.ShapeDtypeStruct((tok, dim), BF),
        ]
        + [jax.ShapeDtypeStruct((tok, cw // np), BF)] * (ns * np)
        + [jax.ShapeDtypeStruct((8, dim), F32)],
        compiler_params=params(60),
        cost_estimate=cost(2 * tok * dim * dim, 16 * tok * dim + 2 * dim * dim),
        name="turn",
    )(info, *terms, resid, cot, vecs, full)


def last_kernel(ns, info, weight, right, *outs):
    step = pl.program_id(0)
    low = dg(right[...], weight[...], NT).astype(BF)
    for rel in range(ns):

        @pl.when(ns - 1 - step == rel)
        def _():
            if ns == 4 and rel % 2:
                outs[2][0] = low
            else:
                outs[rel // 2 if ns == 4 else rel][...] = low


def last_call(info, right, weight, ns):
    count = right.shape[0]
    dim, cols = weight.shape
    tok = count // ns
    shapes = pair_shapes((tok, dim), ns)
    specs = [pl.BlockSpec((tok, dim), lambda i, info: (0, 0))] * ns
    if ns == 4:
        specs[2:] = [pl.BlockSpec((1, tok, dim), lambda i, info: (jnp.where(i < 2, 1, 0), 0, 0))]
    return pl.pallas_call(
        functools.partial(last_kernel, ns),
        grid_spec=pltpu.PrefetchScalarGridSpec(
            num_scalar_prefetch=1,
            grid=(ns,),
            in_specs=[
                once(weight.shape),
                pl.BlockSpec((tok, cols), lambda i, info: (info[0] ^ (ns - 1 - i), 0)),
            ],
            out_specs=specs,
        ),
        out_shape=[jax.ShapeDtypeStruct(shape, BF) for shape in shapes],
        compiler_params=params(60),
        cost_estimate=cost(2 * count * dim * cols, 2 * count * (2 * dim + cols)),
        name="last",
    )(info, weight, right)


def end_kernel(ga, gb, gc, x, resid_grad, vecs, out):
    grad = ga[...].astype(F32) + gb[...].astype(F32) + gc[...].astype(F32)
    unit, scale = norm_parts(x[...].astype(F32))
    out[...] = resid_grad[...] + norm_back(grad, unit, scale, vecs[0:1])


def end_call(terms, x, resid_grad, vecs):
    tok, dim = x.shape
    tile = min(128, tok)
    part = pl.BlockSpec((tile, dim), lambda i: (i, 0))
    head = pl.BlockSpec((None, tile, dim), lambda i: (0, i, 0))
    return pl.pallas_call(
        end_kernel,
        grid=(tok // tile,),
        in_specs=[head if term.ndim == 3 else part for term in terms]
        + [part, part, pl.BlockSpec(vecs.shape, lambda i: (0, 0))],
        out_specs=part,
        out_shape=jax.ShapeDtypeStruct((tok, dim), F32),
        compiler_params=params(40),
        cost_estimate=cost(20 * tok * dim, 14 * tok * dim),
        name="end",
    )(*terms, x, resid_grad, vecs)


def add_pairs_kernel(count, *refs):
    for at in range(count):
        left, right, out = refs[at], refs[count + at], refs[2 * count + at]
        out[...] = (left[...].astype(F32) + right[...].astype(F32)).astype(BF)


def add_pairs(lefts, rights):
    count = len(lefts)
    return pl.pallas_call(
        functools.partial(add_pairs_kernel, count),
        in_specs=[pl.BlockSpec(memory_space=pltpu.VMEM)] * (2 * count),
        out_specs=[pl.BlockSpec(memory_space=pltpu.VMEM)] * count,
        out_shape=[jax.ShapeDtypeStruct(left.shape, BF) for left in lefts],
        compiler_params=params(20),
        cost_estimate=cost(1, 1),
        name="add_pairs",
    )(*lefts, *rights)


def joined_out_kernel(ns, cols, info, *refs):
    parts, joined, outw, smalls = refs[:ns], refs[ns], refs[ns + 1], refs[ns + 2 :]
    rows = joined.shape[0]
    cw = parts[0].shape[1] - cols
    total = None
    for rel in range(ns):
        part = parts[rel]
        joined[:, pl.ds(pl.multiple_of((info[0] ^ rel) * cols, cols), cols)] = part[:rows, :cols].astype(F32)
        outw[:, pl.ds(pl.multiple_of((info[0] ^ rel) * cw, cw), cw)] = part[:rows, cols:].astype(F32)
        term = part[rows:, :rows].astype(F32)
        total = term if total is None else total + term
    at = 0
    for small in smalls:
        for row in range(small.shape[0]):
            small[row : row + 1] = total[at + row : at + row + 1]
        at += small.shape[0]


def joined_out(info, parts, cols):
    ns = len(parts)
    high, wide = parts[0].shape
    rows = high - 16
    shapes = [(rows, ns * cols), (rows, ns * (wide - cols))]
    shapes += [(count, rows) for count in (1, 1, 2, 1, 1, 1, 4, 1)]
    return pl.pallas_call(
        functools.partial(joined_out_kernel, ns, cols),
        grid_spec=pltpu.PrefetchScalarGridSpec(
            num_scalar_prefetch=1,
            grid=(1,),
            in_specs=[once(part.shape) for part in parts],
            out_specs=[once(shape) for shape in shapes],
        ),
        out_shape=[jax.ShapeDtypeStruct(shape, F32) for shape in shapes],
        compiler_params=params(60),
        cost_estimate=cost(0, 6 * ns * rows * wide),
        name="joined_out",
    )(info, *parts)


def feed_out_kernel(ns, nb, rows, units, info, *refs):
    parts, expand, shrink = refs[:ns], refs[ns], refs[ns + 1]
    for rel in range(ns):
        seat = info[0] ^ rel
        shrink[pl.ds(pl.multiple_of(seat * units, units), units)] = parts[rel][rows:].astype(F32)
        for k in range(nb):
            col = pl.ds(pl.multiple_of((k * ns + seat) * units, units), units)
            expand[:, col] = parts[rel][:rows, k * units : (k + 1) * units].astype(F32)


def feed_out(info, parts, nb, rows):
    ns = len(parts)
    high, dim = parts[0].shape
    units = high - rows
    shapes = [(rows, ns * units * nb), (ns * units, dim)]
    return pl.pallas_call(
        functools.partial(feed_out_kernel, ns, nb, rows, units),
        grid_spec=pltpu.PrefetchScalarGridSpec(
            num_scalar_prefetch=1,
            grid=(1,),
            in_specs=[once(part.shape) for part in parts],
            out_specs=[once(shape) for shape in shapes],
        ),
        out_shape=[jax.ShapeDtypeStruct(shape, F32) for shape in shapes],
        compiler_params=params(60),
        cost_estimate=cost(0, 6 * ns * high * dim),
        name="feed_out",
    )(info, *parts)


def body(
    layer_input,
    lengths,
    first_gain,
    first_shift,
    joined_weight,
    joined_bias,
    output_weight,
    output_bias,
    second_gain,
    second_shift,
    expand_weight,
    expand_bias,
    shrink_weight,
    shrink_bias,
    out_grad,
):
    ns = lax.axis_size("seq")
    nb = lax.axis_size("batch")
    si = lax.axis_index("seq")
    bi = lax.axis_index("batch")
    tok = layer_input.shape[1]
    dim = layer_input.shape[2]
    heads = H // ns
    np = heads // 2
    cols = 3 * HD * heads
    cw = HD * heads
    rows = dim // nb
    ff = expand_weight.shape[1] // ns
    units = ff // nb
    x = layer_input[0]
    cot = out_grad[0]
    live = ns == 4 and nb == 8
    ring = Ring(nb, bi, live)
    info = jnp.concatenate([jnp.stack([si, lengths[0]]), ring.table()]).astype(jnp.int32)
    head_ids = si * heads + jnp.arange(heads, dtype=jnp.int32) + 1
    slopes = 2.0 ** (-8.0 * head_ids.astype(F32) / H)

    smalls = (first_gain, first_shift, joined_bias, output_bias, second_gain, second_shift, expand_bias, shrink_bias)
    smalls = [small.reshape(-1, rows) for small in smalls]
    seat = si.reshape(1).astype(jnp.int32)
    one = first_pack(seat, joined_weight, output_weight, smalls, cols, cw)
    jbias = None

    def step(held, t):
        if t < ring.half:
            held[t] = ring.back(held[t - 1])
        held[nb - t] = ring.ahead(held[(nb - t + 1) % nb])

    if live:
        cot, one = tie(cot, one)
        ones = {0: one}
        step(ones, 1)
        half = tok // 2
        near = lax.ppermute(x, "seq", pairs(ns, 1))
        far_a = lax.ppermute(x[:half], "seq", pairs(ns, 2))
        expand_weight, shrink_weight, _ = tie(expand_weight, shrink_weight, one)
        two = second_pack(seat, expand_weight, shrink_weight, nb, ns)
        ones[1], ones[7], two, near, cot, x = tie(ones[1], ones[7], two, near, cot, x)
        step(ones, 2)
        far_b = lax.ppermute(x[half:], "seq", pairs(ns, 2))
        cots = {0: cot, 1: lax.ppermute(cot, "seq", pairs(ns, 1))}
        ones[2], ones[6], cots[1], far_a, cot = tie(ones[2], ones[6], cots[1], far_a, cot)
        step(ones, 3)
        far_c = lax.ppermute(far_a, "seq", pairs(ns, 1))
        ones[3], ones[5], far_b, far_c, cot = tie(ones[3], ones[5], far_b, far_c, cot)
        step(ones, 4)
        far_d = lax.ppermute(far_b, "seq", pairs(ns, 1))
        cots[2] = lax.ppermute(cot, "seq", pairs(ns, 2))
        xs = [x, near, far_a, far_b, far_c, far_d]
        ones[4], two = tie(ones[4], two)
        twos = {0: two}
        step(twos, 1)
        one_parts = [ones[slot][None] for slot in range(nb)]
    else:
        xs = gather_rel(x, "seq", ns)
        xs = [xs[rel] for rel in range(ns)]
        cots = gather_rel(cot, "seq", ns)
        one_parts = [lax.all_gather(one, "batch")]
        low = one_parts[0][:, rows + 2 : rows + 4, :rows].astype(F32).reshape(2 * dim)
        low = lax.dynamic_slice(low, (si * 2 * cw,), (2 * cw,)).reshape(heads, 2, HD)
        jbias = jnp.stack([low[:, 0], jnp.zeros_like(low[:, 0]), low[:, 1]], 1).reshape(1, cols)

    normed, joined, joined_full, outw_own, vecs = first_call(
        info, jbias, xs, one_parts, cols, live, ns
    )
    if live:
        joined, twos[1], twos[7] = tie(joined, twos[1], twos[7])
        step(twos, 2)
    if live:
        ebias = vecs
    else:
        ebias = vecs[7:11].reshape(4, nb, rows).transpose(1, 0, 2).reshape(nb, ns, units)
        ebias = lax.dynamic_slice(ebias, (0, si, 0), (nb, 1, units)).reshape(1, ff)
    outw_all = gather_rel(outw_own, "seq", ns)
    attended = None
    for pair in range(np):
        attended = attend(joined, info, slopes, pair, attended)
        if live and pair == 0:
            out, joined, twos[2], twos[6], outw_all[1], outw_all[2], cots[2] = tie(
                attended[0], joined, twos[2], twos[6], outw_all[1], outw_all[2], cots[2]
            )
            attended = (out, attended[1])
            step(twos, 3)
            outw_all[3] = lax.ppermute(outw_all[2], "seq", pairs(ns, 1))
    mixed, log_sums = attended
    if live:
        mixed, twos[3], twos[5], outw_all[3], cots[2] = tie(mixed, twos[3], twos[5], outw_all[3], cots[2])
        step(twos, 4)
        cots[3] = lax.ppermute(cots[2], "seq", pairs(ns, 1))
    merged_parts = []
    for rel in range(ns):
        block = lax.dynamic_slice(mixed, ((si ^ rel) * tok, 0), (tok, cw))
        merged_parts.append(lax.ppermute(block, "seq", pairs(ns, rel)) if rel else block)
    if live:
        cots[3], twos[4], *merged_parts = tie(cots[3], twos[4], *merged_parts)
    merged, resid, second, outw_full = middle_call(
        info, x, vecs, merged_parts, [outw_all[rel] for rel in range(ns)]
    )
    out_parts = {}
    back_parts = {}
    activs = []
    pre_grads = []
    bias_sums = []
    if live:
        seconds = {0: second, 2: lax.ppermute(second, "seq", pairs(ns, 2)), 1: lax.ppermute(second, "seq", pairs(ns, 1))}
        two_parts = [twos[slot][None] for slot in range(nb)]
    else:
        seconds = gather_rel(second, "seq", ns)
        expand_part = expand_weight.reshape(rows, nb, ns, units)
        expand_part = lax.dynamic_slice(expand_part, (0, 0, si, 0), (rows, nb, 1, units)).reshape(rows, ff)
        shrink_part = lax.dynamic_slice(shrink_weight, (si * units, 0), (units, dim))
        two_parts = [lax.all_gather(expand_part, "batch"), lax.all_gather(shrink_part, "batch")]
    for rel in range(0, ns, 2):
        activ, pre_grad, oa, ob, ba, bb, bgrad = feed_call(
            info, seconds[rel], seconds[rel + 1], cots[rel], cots[rel + 1], ebias, two_parts, rows, units, nb, live
        )
        if live and rel == 0:
            activ, ob, bb, seconds[2] = tie(activ, ob, bb, seconds[2])
            seconds[3] = lax.ppermute(seconds[2], "seq", pairs(ns, 1))
            seconds[2], seconds[3] = tie(seconds[2], seconds[3])
            near_back = lax.ppermute(bb, "seq", pairs(ns, 1))
            near_out = lax.ppermute(ob, "seq", pairs(ns, 1))
        activs.append(activ)
        pre_grads.append(pre_grad)
        bias_sums.append(bgrad)
        out_parts.update({rel: oa, rel + 1: ob})
        back_parts.update({rel: ba, rel + 1: bb})
    if live:
        back_parts[3], near_back, near_out = tie(back_parts[3], near_back, near_out)
        far_back = lax.ppermute(back_parts[3], "seq", pairs(ns, 1))
        far_back, out_far = tie(far_back, out_parts[3])
        (back_b,) = add_pairs((back_parts[2],), (far_back,))
        back_b = lax.ppermute(back_b, "seq", pairs(ns, 2))
        far_out = lax.ppermute(out_far, "seq", pairs(ns, 1))
    else:
        back_terms = (*scatter_rel(back_parts, "seq", ns, last=False), jnp.zeros((tok, dim), BF))
        out_a, out_b = scatter_rel(out_parts, "seq", ns, last=False)
    feed_stack = feed_grad_call(
        info,
        activs,
        [cots[rel] for rel in range(ns)],
        [seconds[rel] for rel in range(ns)],
        pre_grads,
        nb,
        live,
    )

    class Scatter:
        def __init__(self, parts):
            self.parts = [part[0] for part in parts]
            self.t = 0
            self.ahead = self.parts[ring.half]
            self.back = self.parts[ring.half + 1]

        def send(self):
            self.t += 1
            self.got_ahead = ring.ahead(self.ahead)
            self.got_back = ring.back(self.back) if self.t > 1 else None

        def take(self, *others):
            both = self.t > 1
            got = (self.got_ahead, self.got_back) if both else (self.got_ahead,)
            tied = tie(*got, *others)
            got, others = tied[: len(got)], tied[len(got) :]
            if self.t == ring.half:
                total = self.parts[0].astype(F32) + got[0].astype(F32) + got[1].astype(F32)
                return (total.astype(BF), *others)
            mine = self.parts[ring.half - self.t]
            if both:
                self.ahead, self.back = add_pairs((mine, self.parts[nb - ring.half + self.t]), got)
            else:
                (self.ahead,) = add_pairs((mine,), got)
            return others

    if live:
        feed_ring = Scatter(feed_stack)
        feed_ring.send()
        (out_b,) = add_pairs((out_parts[2],), (far_out,))
        back_b, out_b, _ = tie(back_b, out_b, feed_stack[0])
        back_terms = (back_parts[0], near_back, back_b)
    resid_grad, branch, *mixed_grads, turn_sums = turn_call(
        info, back_terms, resid, cot, vecs, outw_full, ns, 1
    )
    outw_parts = split_grad(info, merged, branch, ns)
    sides = []

    grads = [
        lax.ppermute(block, "seq", pairs(ns, rel)) if rel else block for rel, block in enumerate(mixed_grads)
    ]
    if live:
        grads[0], *outw_parts = tie(grads[0], *outw_parts)
        grads = feed_ring.take(*grads)
        *grads, feed_ring.ahead, outw_near, out_b = tie(*grads, feed_ring.ahead, outw_parts[2], out_b)
        out_b = lax.ppermute(out_b, "seq", pairs(ns, 2))
        feed_ring.send()
        outw_near = lax.ppermute(outw_near, "seq", pairs(ns, 1))
    joined_grad = None
    for pair in range(np):
        joined_grad, side = attend_back(joined, grads, mixed, log_sums, info, slopes, pair, joined_grad)
        sides.append(side)
        if live and pair == 0:
            joined_grad, outw_near = feed_ring.take(joined_grad, outw_near)
            outw_far = add16(outw_parts[1], outw_near[1])
            joined_grad, joined, feed_ring.ahead, feed_ring.back, outw_far = tie(
                joined_grad, joined, feed_ring.ahead, feed_ring.back, outw_far
            )
            feed_ring.send()
            outw_far = lax.ppermute(outw_far, "seq", pairs(ns, 2))
        elif live:
            joined_grad, outw_far, out_b = feed_ring.take(joined_grad, outw_far, out_b)

    if live:
        shares = None
        outw_share = (outw_parts[0], outw_near, outw_far)
        joined_grad, feed_ring.ahead, feed_ring.back = tie(joined_grad, feed_ring.ahead, feed_ring.back)
        feed_ring.send()
    else:
        spread_bias = lax.dynamic_update_slice(
            jnp.zeros((nb, ns, units), F32), sum(bias_sums).reshape(nb, 1, units), (0, si, 0)
        )
        spread_bias = spread_bias.reshape(nb, 4, rows).transpose(1, 0, 2).reshape(4, dim)
        side = jnp.concatenate(sides, 1).reshape(heads, 3, HD)
        side = jnp.stack([side[:, 0], side[:, 2]], 1).reshape(2 * cw)
        side = lax.dynamic_update_slice(jnp.zeros((2 * dim,), F32), side, (si * 2 * cw,))
        side = side.reshape(nb, 2, rows).transpose(1, 0, 2).reshape(2, dim)
        none = jnp.zeros((2, dim), F32)
        shares = [none, side, turn_sums[2:3], turn_sums[0:2], spread_bias, turn_sums[3:4], none, none]
        shares = jnp.concatenate(shares, 0)
        outw_share = (scatter_rel(dict(enumerate(outw_parts)), "seq", ns),)
    joined_stack = joined_grad_call(
        info, normed, joined_grad, sides, outw_share, joined_full, vecs, shares, turn_sums, bias_sums, nb, live
    )
    if live:
        feed_share, *joined_stack = feed_ring.take(*joined_stack)
        feed_share, *joined_stack = tie(feed_share, *joined_stack)
        feed_parts = {0: feed_share, 2: lax.ppermute(feed_share, "seq", pairs(ns, 2))}
        joined_ring = Scatter(joined_stack)
        joined_ring.send()
        joined_grad, _ = tie(joined_grad, joined_stack[0])
    normed_parts = last_call(info, joined_grad, joined_full, ns)

    def ordered(block):
        parts = gather_rel(block, "seq", ns)
        return [parts[rel] for rel in range(ns)]

    if live:
        sent, feed_parts[2] = joined_ring.take(normed_parts[2], feed_parts[2])
        joined_ring.ahead, sent = tie(joined_ring.ahead, sent)
        joined_ring.send()
        got = lax.ppermute(sent, "seq", pairs(ns, 1))
        far = add16(normed_parts[1], got[1])
        (far,) = joined_ring.take(far)
        joined_ring.ahead, joined_ring.back, far = tie(joined_ring.ahead, joined_ring.back, far)
        joined_ring.send()
        norm_b = lax.ppermute(far, "seq", pairs(ns, 2))
        out_b, out_parts[0], _ = tie(out_b, out_parts[0], far)
        out_terms = out_parts[0].astype(F32) + near_out.astype(F32) + out_b.astype(F32)
        layer_output = (resid + out_terms + vecs[11:12]).astype(BF)
        layer_output, feed_parts[0], feed_parts[2] = joined_ring.take(layer_output, feed_parts[0], feed_parts[2])
        joined_ring.ahead, joined_ring.back, feed_parts[0], feed_parts[2] = tie(
            joined_ring.ahead, joined_ring.back, feed_parts[0], feed_parts[2]
        )
        joined_ring.send()
        feed_parts[1] = lax.ppermute(feed_parts[0], "seq", pairs(ns, 1))
        feed_parts[3] = lax.ppermute(feed_parts[2], "seq", pairs(ns, 1))
        joined_share, norm_b, feed_parts[1], feed_parts[3] = joined_ring.take(norm_b, feed_parts[1], feed_parts[3])
        joined_share, norm_b, feed_parts[1] = tie(joined_share, norm_b, feed_parts[1])
        joined_parts = {0: joined_share, 2: lax.ppermute(joined_share, "seq", pairs(ns, 2))}
        joined_parts[1] = lax.ppermute(joined_share, "seq", pairs(ns, 1))
        expand_grad, shrink_grad = feed_out(info, [feed_parts[rel] for rel in range(ns)], nb, rows)
        input_grad = end_call((normed_parts[0], got, norm_b), x, resid_grad, vecs)
        joined_parts[2], joined_parts[1], input_grad, expand_grad, shrink_grad = tie(
            joined_parts[2], joined_parts[1], input_grad, expand_grad, shrink_grad
        )
        joined_parts[3] = lax.ppermute(joined_parts[2], "seq", pairs(ns, 1))
        joined_parts = [joined_parts[rel] for rel in range(ns)]
    else:
        layer_output = (resid + out_a.astype(F32) + out_b.astype(F32) + vecs[11:12]).astype(BF)
        norm_terms = scatter_rel(dict(enumerate(normed_parts)), "seq", ns, last=False)
        input_grad = end_call((*norm_terms, jnp.zeros((tok, dim), BF)), x, resid_grad, vecs)
        joined_share = lax.psum_scatter(joined_stack[0], "batch", scatter_dimension=0)
        expand_share = lax.psum_scatter(feed_stack[0], "batch", scatter_dimension=0)
        shrink_share = lax.psum_scatter(feed_stack[1], "batch", scatter_dimension=0)
        seats = jnp.arange(ns, dtype=jnp.int32) ^ si
        shrink_grad = jnp.take(jnp.stack(ordered(shrink_share)), seats, axis=0).astype(F32).reshape(ns * units, dim)
        expand_grad = jnp.take(jnp.stack(ordered(expand_share)), seats, axis=0).astype(F32)
        expand_grad = expand_grad.reshape(ns, rows, nb, units).transpose(1, 2, 0, 3).reshape(rows, ns * ff)
        joined_parts = ordered(joined_share)
    joined_wgrad, outw_grad, *small = joined_out(info, joined_parts, cols)
    small = [value.reshape(-1) for value in small]
    return (
        layer_output[None],
        input_grad[None],
        small[0],
        small[1],
        joined_wgrad,
        small[2],
        outw_grad,
        small[3],
        small[4],
        small[5],
        expand_grad,
        small[6],
        shrink_grad,
        small[7],
    )


def solution(mesh):
    row = P("batch")
    mat = P("batch", None)
    act = P("batch", "seq", None)
    return jax.shard_map(
        body,
        mesh=mesh,
        in_specs=(act, row, row, row, mat, row, mat, row, row, row, mat, row, mat, row, act),
        out_specs=(act, act, row, row, mat, row, mat, row, row, row, mat, row, mat, row),
        check_vma=False,
    )
```

```python
import functools

import jax
import jax.numpy as jnp
from jax import lax
from jax.experimental import pallas as pl
from jax.experimental.pallas import tpu as pltpu
from jax.sharding import PartitionSpec as P

H = 16
HD = 64
EPSILON = 1e-05
F32 = jnp.float32
BF = jnp.bfloat16
NT = (((1,), (1,)), ((), ()))
NN = (((1,), (0,)), ((), ()))
TN = (((0,), (0,)), ((), ()))
MIB = 2**20
SHRINK = 1000


def dg(left, right, dims):
    return lax.dot_general(left, right, dims, preferred_element_type=F32)


def params(limit=56):
    return pltpu.CompilerParams(vmem_limit_bytes=limit * MIB)


def cost(flops, moved, exps=0):
    return pl.CostEstimate(flops=flops // SHRINK, bytes_accessed=moved // SHRINK, transcendentals=exps // SHRINK)


def norm_parts(values):
    mean = jnp.mean(values, axis=-1, keepdims=True)
    centered = values - mean
    scale = lax.rsqrt(jnp.mean(centered * centered, axis=-1, keepdims=True) + EPSILON)
    return centered * scale, scale


def norm_back(grad, unit, scale, gain):
    scaled = grad * gain
    return scale * (
        scaled
        - jnp.mean(scaled, axis=-1, keepdims=True)
        - unit * jnp.mean(scaled * unit, axis=-1, keepdims=True)
    )


def pairs(size, bit):
    return [(i, i ^ bit) for i in range(size)]


def bits_low_last(size):
    bits = []
    bit = 2
    while bit < size:
        bits.append(bit)
        bit *= 2
    if size > 1:
        bits.append(1)
    return bits


def add16(left, right):
    return (left.astype(F32) + right.astype(F32)).astype(BF)


def gather_rel(block, axis, size):
    out = {0: block}
    for bit in bits_low_last(size):
        for rel in list(out):
            out[rel | bit] = lax.ppermute(out[rel], axis, pairs(size, bit))
    return out


def scatter_rel(parts, axis, size, last=True):
    parts = dict(parts)
    order = bits_low_last(size)[::-1]
    for bit in order:
        for rel in sorted(parts, reverse=True):
            if rel & bit:
                other = lax.ppermute(parts.pop(rel), axis, pairs(size, bit))
                if bit == order[-1] and not last:
                    return parts[0], other
                parts[rel ^ bit] = add16(parts[rel ^ bit], other)
    return parts[0]


def tie(*values):
    return lax.optimization_barrier(values)


class Ring:
    def __init__(self, size, index, live):
        self.size = size
        self.live = live
        order = list(range(0, size, 2)) + list(range(size - 1, 0, -2))
        self.forward = [(order[i], order[(i + 1) % size]) for i in range(size)]
        self.backward = [(b, a) for a, b in self.forward]
        count = jnp.arange(size, dtype=jnp.int32)
        place = lambda k: jnp.where(k % 2 == 0, k // 2, size - (k + 1) // 2)
        if self.live:
            self.slots = (place(count) - place(index) + size) % size
            seat = (place(index) + count) % size
            self.owners = jnp.where(seat < size // 2, 2 * seat, 2 * (size - seat) - 1)
        else:
            self.slots = count
            self.owners = count
        self.half = size // 2

    def table(self):
        return jnp.concatenate([self.slots, self.owners])

    def ahead(self, value):
        return lax.ppermute(value, "batch", self.forward)

    def back(self, value):
        return lax.ppermute(value, "batch", self.backward)


def owner_at(info, live, nb, slot):
    return info[2 + nb + slot] if live else slot


def put(outs, slot, value, rows, cols):
    if len(outs) == 1:
        outs[0][slot, rows, cols] = value
        return
    for at, out in enumerate(outs):

        @pl.when(slot == at)
        def _():
            out[0, rows, cols] = value


def blocks_of(refs):
    out = []
    for ref in refs:
        out += [(ref, at) for at in range(ref.shape[0])]
    return out


def once(shape):
    return pl.BlockSpec(shape, lambda i, *_: (0,) * len(shape), pipeline_mode=pl.Buffered(1))


def first_pack_kernel(info, joined, outw, *refs):
    smalls, out = refs[:-1], refs[-1]
    rows, cols = joined.shape
    out[:rows, :cols] = joined[...]
    out[:rows, cols:] = outw[...]
    pieces = [small[...].astype(F32) for small in smalls]
    count = sum(piece.shape[0] for piece in pieces)
    pieces.append(jnp.zeros((16 - count, rows), F32))
    out[rows:, :rows] = jnp.concatenate(pieces, 0).astype(BF)
    out[rows:, rows:] = jnp.zeros((16, out.shape[1] - rows), BF)


def first_pack(info, joined, outw, smalls, cols, cw):
    rows = joined.shape[0]
    shape = (rows + 16, cols + cw)
    return pl.pallas_call(
        first_pack_kernel,
        grid_spec=pltpu.PrefetchScalarGridSpec(
            num_scalar_prefetch=1,
            grid=(1,),
            in_specs=[
                pl.BlockSpec((rows, cols), lambda i, info: (0, info[0])),
                pl.BlockSpec((rows, cw), lambda i, info: (0, info[0])),
            ]
            + [once(small.shape) for small in smalls],
            out_specs=pl.BlockSpec(shape, lambda i, info: (0, 0)),
        ),
        out_shape=jax.ShapeDtypeStruct(shape, BF),
        compiler_params=params(60),
        name="first_pack",
    )(info, joined, outw, *smalls)


def second_pack_kernel(nb, ns, units, info, expand, shrink, out):
    rows = expand.shape[0]
    for k in range(nb):
        col = pl.ds(pl.multiple_of((k * ns + info[0]) * units, units), units)
        out[:rows, k * units : (k + 1) * units] = expand[:, col]
    out[rows:] = shrink[...]


def second_pack(info, expand, shrink, nb, ns):
    rows, wide = expand.shape
    dim = shrink.shape[1]
    units = shrink.shape[0] // ns
    return pl.pallas_call(
        functools.partial(second_pack_kernel, nb, ns, units),
        grid_spec=pltpu.PrefetchScalarGridSpec(
            num_scalar_prefetch=1,
            grid=(1,),
            in_specs=[
                pl.BlockSpec((rows, wide), lambda i, info: (0, 0)),
                pl.BlockSpec((units, dim), lambda i, info: (info[0], 0)),
            ],
            out_specs=pl.BlockSpec((rows + units, dim), lambda i, info: (0, 0)),
        ),
        out_shape=jax.ShapeDtypeStruct((rows + units, dim), BF),
        compiler_params=params(60),
        name="second_pack",
    )(info, expand, shrink)


def first_kernel(starts, nb, rows, cols, live, info, *refs):
    jbias_in, refs = (None, refs) if live else (refs[0], refs[1:])
    count = len(starts) - 1
    xs, weights = refs[:count], refs[count:-6]
    normed, joined, full, outw, vecs, jbias = refs[-6:]
    step = pl.program_id(0)

    @pl.when(step == 0)
    def _():
        for slot, (ref, at) in enumerate(blocks_of(weights)):
            high = owner_at(info, live, nb, slot) * rows
            high = pl.multiple_of(high, rows) if live else high
            full[pl.ds(high, rows)] = ref[at, :rows, :cols]
            outw[pl.ds(high, rows)] = ref[at, :rows, cols:]
            vecs[:, pl.ds(high, rows)] = ref[at, rows:, :rows].astype(F32)
        if live:
            heads = cols // (3 * HD)
            for head in range(heads):
                at = info[0] * heads + head
                col = pl.ds(pl.multiple_of(lax.div(at, 2) * rows, rows), rows)
                row = vecs[0:8, col][2 + head % 2 : 3 + head % 2]
                pieces = [row[:, :HD], jnp.zeros((1, HD), F32), row[:, HD:]]
                jbias[:, head * 3 * HD : (head + 1) * 3 * HD] = jnp.concatenate(pieces, 1)
        else:
            jbias[...] = jbias_in[...]

    for at in range(count):

        @pl.when((step >= starts[at]) & (step < starts[at + 1]))
        def _():
            unit, _ = norm_parts(xs[at][...].astype(F32))
            value = (unit * vecs[0:1] + vecs[1:2]).astype(BF)
            normed[...] = value
            joined[...] = (dg(value, full[...], NN) + jbias[...]).astype(BF)


def first_call(info, jbias, xs, weights, cols, live, ns):
    dim = xs[0].shape[1]
    tok = sum(piece.shape[0] for piece in xs) // ns
    nb = sum(weight.shape[0] for weight in weights)
    rows = dim // nb
    cw = weights[0].shape[2] - cols
    tile = min(256, tok)
    nt = tok // tile
    starts = [0]
    for piece in xs:
        starts.append(starts[-1] + piece.shape[0] // tile)
    extra = [] if live else [jbias]
    place = lambda i, info: ((info[0] ^ lax.div(i, nt)) * nt + lax.rem(i, nt), 0)

    def source(at):
        last = starts[at + 1] - starts[at] - 1
        return pl.BlockSpec((tile, dim), lambda i, info: (jnp.clip(i - starts[at], 0, last), 0))

    return pl.pallas_call(
        functools.partial(first_kernel, starts, nb, rows, cols, live),
        grid_spec=pltpu.PrefetchScalarGridSpec(
            num_scalar_prefetch=1,
            grid=(ns * nt,),
            in_specs=[once(value.shape) for value in extra]
            + [source(at) for at in range(len(xs))]
            + [once(weight.shape) for weight in weights],
            out_specs=[
                pl.BlockSpec((tile, dim), place),
                pl.BlockSpec((tile, cols), place),
                once((dim, cols)),
                once((dim, cw)),
                once((16, dim)),
            ],
            scratch_shapes=[pltpu.VMEM((1, cols), F32)],
        ),
        out_shape=[
            jax.ShapeDtypeStruct((ns * tok, dim), BF),
            jax.ShapeDtypeStruct((ns * tok, cols), BF),
            jax.ShapeDtypeStruct((dim, cols), BF),
            jax.ShapeDtypeStruct((dim, cw), BF),
            jax.ShapeDtypeStruct((16, dim), F32),
        ],
        compiler_params=params(60),
        cost_estimate=cost(2 * ns * tok * dim * cols, 2 * ns * tok * (2 * dim + cols)),
        name="first",
    )(info, *extra, *xs, *weights)


def three(value):
    high = value.astype(BF)
    rest = value - high.astype(F32)
    mid = rest.astype(BF)
    return high, mid, (rest - mid.astype(F32)).astype(BF)


def spread(lane, base, columns):
    for at, column in columns:
        base = jnp.where(lane == at, column.astype(F32), base)
    return base.astype(BF)


def key_extra(count, slope, length):
    lane = lax.broadcasted_iota(jnp.int32, (count, HD), 1)
    pos = lax.broadcasted_iota(jnp.int32, (count, HD), 0)
    high, mid, low = three(slope * pos.astype(F32))
    dead = jnp.where(pos < length, 0.0, -1e30)
    return spread(lane, jnp.where(lane < 7, 1.0, 0.0), [(0, high), (1, mid), (2, low), (3, dead)])


def attend_kernel(count, size, pair, info, slopes, joined, mixed, sums, keys):
    lane = lax.broadcasted_iota(jnp.int32, (size, HD), 1)
    ones = jnp.where(lane < 4, 1.0, 0.0).astype(BF)
    for hh in range(2):
        base = 3 * HD * hh
        extra = key_extra(count, slopes[2 * pair + hh], info[1])
        keys[hh] = jnp.concatenate([joined[:, base + HD : base + 2 * HD], extra], 1)
    query_at = lax.broadcasted_iota(jnp.int32, (size, size), 0)
    key_at = lax.broadcasted_iota(jnp.int32, (size, size), 1)
    for block in range(count // size):
        low = block * size
        high = low + size
        outs = []
        logs = []
        for hh in range(2):
            base = 3 * HD * hh
            query = (joined[low:high, base : base + HD].astype(F32) * 0.125).astype(BF)
            query = jnp.concatenate([query, ones], 1)
            near = jnp.where(key_at <= query_at, dg(query, keys[hh, low:high], NT), -1e30)
            top = jnp.max(near, axis=1, keepdims=True)
            if block:
                far = dg(query, keys[hh, 0:low], NT)
                top = jnp.maximum(top, jnp.max(far, axis=1, keepdims=True))
            near = jnp.exp(near - top)
            total = jnp.sum(near, axis=1, keepdims=True)
            acc = dg(near.astype(BF), joined[low:high, base + 2 * HD : base + 3 * HD], NN)
            if block:
                far = jnp.exp(far - top)
                total += jnp.sum(far, axis=1, keepdims=True)
                acc += dg(far.astype(BF), joined[0:low, base + 2 * HD : base + 3 * HD], NN)
            outs.append(acc / total)
            logs.append(jnp.broadcast_to(top + jnp.log(total), (size, HD)))
        mixed[low:high] = jnp.concatenate(outs, 1).astype(BF)
        sums[low:high] = jnp.concatenate(logs, 1)


def attend(joined, info, slopes, pair, held):
    count, width = joined.shape
    groups = width // (6 * HD)
    smem = pl.BlockSpec(memory_space=pltpu.SMEM)
    narrow = pl.BlockSpec((count, 2 * HD), lambda i: (0, pair))
    area = count * count
    extra = [] if held is None else list(held)

    def kernel(*refs):
        attend_kernel(count, min(512, count), pair, *refs[:3], *refs[3 + len(extra) :])

    return pl.pallas_call(
        kernel,
        grid=(1,),
        in_specs=[smem, smem, pl.BlockSpec((count, 6 * HD), lambda i: (0, pair))]
        + [pl.BlockSpec(memory_space=pl.ANY)] * len(extra),
        out_specs=[narrow, narrow],
        out_shape=[
            jax.ShapeDtypeStruct((count, groups * 2 * HD), BF),
            jax.ShapeDtypeStruct((count, groups * 2 * HD), F32),
        ],
        input_output_aliases={3: 0, 4: 1} if extra else {},
        scratch_shapes=[pltpu.VMEM((2, count, 2 * HD), BF)],
        compiler_params=params(60),
        cost_estimate=cost(area * 1024, 20 * count * HD, area),
        name="attend",
    )(info, slopes, joined, *extra)


def attend_back_kernel(count, size, ns, pair, info, slopes, joined, mixed, sums, *refs):
    pieces_in = refs[:ns]
    out, sides, keys, queries, values, grads, query_grad = refs[ns:]
    tok = count // ns
    lane = lax.broadcasted_iota(jnp.int32, (count, HD), 1)
    near_lane = lax.broadcasted_iota(jnp.int32, (tok, HD), 1)
    for hh in range(2):
        base = 3 * HD * hh
        half = slice(hh * HD, (hh + 1) * HD)
        extra = key_extra(count, slopes[2 * pair + hh], info[1])
        keys[hh] = jnp.concatenate([joined[:, base + HD : base + 2 * HD], extra], 1)
        query = (joined[:, base : base + HD].astype(F32) * 0.125).astype(BF)
        high, mid, low = three(-sums[:, half])
        extra = spread(lane, jnp.where(lane < 4, 1.0, 0.0), [(4, high), (5, mid), (6, low)])
        queries[hh] = jnp.concatenate([query, extra], 1)
        ones = jnp.where(lane < 3, 1.0, 0.0).astype(BF)
        values[hh] = jnp.concatenate([joined[:, base + 2 * HD : base + 3 * HD], ones], 1)
        for rel in range(ns):
            at = pl.ds(pl.multiple_of((info[0] ^ rel) * tok, tok), tok)
            part = pieces_in[rel][:, half]
            inner = jnp.sum(part.astype(F32) * mixed[at, half].astype(F32), axis=1, keepdims=True)
            high, mid, low = three(jnp.broadcast_to(-inner, (tok, HD)))
            extra = spread(near_lane, jnp.zeros((tok, HD), F32), [(0, high), (1, mid), (2, low)])
            grads[hh, at] = jnp.concatenate([part, extra], 1)
    key_at = lax.broadcasted_iota(jnp.int32, (size, size), 0)
    query_at = lax.broadcasted_iota(jnp.int32, (size, size), 1)
    blocks = count // size
    for j in range(blocks):
        ks = slice(j * size, (j + 1) * size)
        pieces = []
        for hh in range(2):
            key_sum = None
            for i in range(j, blocks):
                qs = slice(i * size, (i + 1) * size)
                probs = jnp.exp(dg(keys[hh, ks], queries[hh, qs], NT))
                if i == j:
                    probs = jnp.where(key_at <= query_at, probs, 0.0)
                slope = (probs * dg(values[hh, ks], grads[hh, qs], NT)).astype(BF)
                value_part = dg(probs.astype(BF), grads[hh, qs], NN)
                key_part = dg(slope, queries[hh, qs], NN)
                query_part = dg(keys[hh, ks], slope, TN)
                value_sum = value_part if key_sum is None else value_sum + value_part
                key_sum = key_part if key_sum is None else key_sum + key_part
                query_grad[hh, :, qs] = query_part if j == 0 else query_grad[hh, :, qs] + query_part
            pieces += [jnp.zeros((size, HD), F32), key_sum[:, :HD], value_sum[:, :HD]]
        out[ks] = jnp.concatenate(pieces, 1).astype(BF)
    for hh in range(2):
        base = 3 * HD * hh
        out[:, base : base + HD] = (query_grad[hh].T[:, :HD] * 0.125).astype(BF)
    sides[...] = jnp.sum(out[...].astype(F32), axis=0, keepdims=True)


def attend_back(joined, grads, mixed, sums, info, slopes, pair, held):
    count, width = joined.shape
    ns = len(grads)
    smem = pl.BlockSpec(memory_space=pltpu.SMEM)
    wide = pl.BlockSpec((count, 6 * HD), lambda i: (0, pair))
    narrow = pl.BlockSpec((count, 2 * HD), lambda i: (0, pair))
    piece = pl.BlockSpec((count // ns, 2 * HD), lambda i: (0, pair))
    area = count * count
    extra = [] if held is None else [held]

    def kernel(*refs):
        inputs, rest = refs[: 5 + ns], refs[5 + ns + len(extra) :]
        attend_back_kernel(count, min(512, count), ns, pair, *inputs, *rest)

    return pl.pallas_call(
        kernel,
        grid=(1,),
        in_specs=[smem, smem, wide, narrow, narrow]
        + [piece] * ns
        + [pl.BlockSpec(memory_space=pl.ANY)] * len(extra),
        out_specs=[wide, pl.BlockSpec((1, 6 * HD), lambda i: (0, 0))],
        out_shape=[jax.ShapeDtypeStruct((count, width), BF), jax.ShapeDtypeStruct((1, 6 * HD), F32)],
        input_output_aliases={5 + ns: 0} if extra else {},
        scratch_shapes=[pltpu.VMEM((2, count, 2 * HD), BF)] * 4 + [pltpu.VMEM((2, 2 * HD, count), F32)],
        compiler_params=params(60),
        cost_estimate=cost(area * 2560, 40 * count * HD, area),
        name="attend_back",
    )(info, slopes, joined, mixed, sums, *grads, *extra)


def middle_kernel(ns, np, info, x, vecs, *refs):
    mixed, weights = refs[: ns * np], refs[ns * np : ns * np + ns]
    merged, resid, second, full = refs[ns * np + ns :]
    cw = weights[0].shape[1]
    pw = cw // np

    @pl.when(pl.program_id(0) == 0)
    def _():
        for rel in range(ns):
            full[:, pl.ds(pl.multiple_of((info[0] ^ rel) * cw, cw), cw)] = weights[rel][...]

    for pair in range(np):
        for rel in range(ns):
            col = pl.ds(pl.multiple_of((info[0] ^ rel) * cw + pair * pw, pw), pw)
            merged[:, col] = mixed[pair * ns + rel][...]
    value = x[...].astype(F32) + dg(merged[...], full[...], NN) + vecs[4:5]
    resid[...] = value
    unit, _ = norm_parts(value)
    second[...] = (unit * vecs[5:6] + vecs[6:7]).astype(BF)


def middle_call(info, x, vecs, mixed, weights):
    tok, dim = x.shape
    ns = len(weights)
    np = len(mixed) // ns
    tile = min(256, tok)
    part = lambda width: pl.BlockSpec((tile, width), lambda i, info: (i, 0))
    return pl.pallas_call(
        functools.partial(middle_kernel, ns, np),
        grid_spec=pltpu.PrefetchScalarGridSpec(
            num_scalar_prefetch=1,
            grid=(tok // tile,),
            in_specs=[part(dim), once(vecs.shape)]
            + [part(block.shape[1]) for block in mixed]
            + [once(weight.shape) for weight in weights],
            out_specs=[part(dim), part(dim), part(dim), once((dim, dim))],
        ),
        out_shape=[
            jax.ShapeDtypeStruct((tok, dim), BF),
            jax.ShapeDtypeStruct((tok, dim), F32),
            jax.ShapeDtypeStruct((tok, dim), BF),
            jax.ShapeDtypeStruct((dim, dim), BF),
        ],
        compiler_params=params(60),
        cost_estimate=cost(2 * tok * dim * dim, 12 * tok * dim + 4 * dim * dim),
        name="middle",
    )(info, x, vecs, *mixed, *weights)


def feed_kernel(nt, nb, rows, units, live, info, sa, sb, ca, cb, ebias, *refs):
    weights = refs[:-9]
    activ, pre_grad, oa, ob, ba, bb, bgrad, wide, tall = refs[-9:]
    step = pl.program_id(0)
    bias = ebias[...]
    if live:
        row = lax.broadcasted_iota(jnp.int32, bias.shape, 0)
        bias = jnp.sum(jnp.where(row == 7 + info[0], bias, 0.0), axis=0, keepdims=True)

    @pl.when(step == 0)
    def _():
        blocks = blocks_of(weights)
        for slot in range(nb):
            owner = owner_at(info, live, nb, slot)
            high = pl.multiple_of(owner * rows, rows) if live else owner * rows
            deep = pl.multiple_of(owner * units, units) if live else owner * units
            if len(blocks) == nb:
                ref, at = blocks[slot]
                wide[pl.ds(high, rows)] = ref[at, :rows]
                tall[pl.ds(deep, units)] = ref[at, rows:]
            else:
                wide[pl.ds(high, rows)] = weights[0][slot]
                tall[pl.ds(deep, units)] = weights[1][slot]
        bgrad[...] = jnp.zeros_like(bgrad)

    def work(second, cot, out, back):
        pre = dg(second[...], wide[...], NN) + bias
        square = pre * pre
        bend = jnp.tanh(0.7978845608028654 * pre * (1.0 + 0.044715 * square))
        half = 0.5 + 0.5 * bend
        act = (pre * half).astype(BF)
        activ[...] = act
        out[...] = dg(act, tall[...], NN).astype(BF)
        steep = half + pre * (0.5 - 0.5 * bend * bend) * (0.7978845608028654 + 0.10703222440890037 * square)
        grad = (dg(cot[...], tall[...], NT) * steep).astype(BF)
        pre_grad[...] = grad
        bgrad[...] += jnp.sum(grad.astype(F32), axis=0, keepdims=True)
        back[...] = dg(grad, wide[...], NT).astype(BF)

    @pl.when(step < nt)
    def _():
        work(sa, ca, oa, ba)

    @pl.when(step >= nt)
    def _():
        work(sb, cb, ob, bb)


def feed_call(info, sa, sb, ca, cb, ebias, weights, rows, units, nb, live):
    tok, dim = sa.shape
    ff = ebias.shape[1]
    tile = min(256, tok)
    nt = tok // tile
    left = pl.BlockSpec((tile, dim), lambda i, info: (jnp.minimum(i, nt - 1), 0))
    right = pl.BlockSpec((tile, dim), lambda i, info: (jnp.maximum(i - nt, 0), 0))
    flat = pl.BlockSpec((tile, ff), lambda i, info: (i, 0))
    shape = jax.ShapeDtypeStruct((tok, dim), BF)
    return pl.pallas_call(
        functools.partial(feed_kernel, nt, nb, rows, units, live),
        grid_spec=pltpu.PrefetchScalarGridSpec(
            num_scalar_prefetch=1,
            grid=(2 * nt,),
            in_specs=[left, right, left, right, once(ebias.shape)] + [once(weight.shape) for weight in weights],
            out_specs=[flat, flat, left, right, left, right, pl.BlockSpec((1, ff), lambda i, info: (0, 0))],
            scratch_shapes=[pltpu.VMEM((dim, ff), BF), pltpu.VMEM((ff, dim), BF)],
        ),
        out_shape=[jax.ShapeDtypeStruct((2 * tok, ff), BF)] * 2
        + [shape] * 4
        + [jax.ShapeDtypeStruct((1, ff), F32)],
        compiler_params=params(60),
        cost_estimate=cost(16 * tok * dim * ff, 16 * tok * dim + 8 * dim * ff, 2 * tok * ff),
        name="feed",
    )(info, sa, sb, ca, cb, ebias, *weights)


def feed_grad_kernel(ns, nb, rows, units, steps, info, *refs):
    half = ns // 2
    activs, cots, seconds, grads = refs[:half], refs[half : half + ns], refs[half + ns : half + 2 * ns], refs[half + 2 * ns : 2 * half + 2 * ns]
    outs = refs[2 * half + 2 * ns :]
    step = pl.program_id(0)

    def total(wides, thins, wide_left):
        out = None
        for rel in range(ns):
            thin = thins[rel]
            tok = thin.shape[0]
            wide = wides[rel // 2][(rel % 2) * tok : (rel % 2 + 1) * tok]
            term = dg(wide, thin[...], TN) if wide_left else dg(thin[...], wide, TN)
            out = term if out is None else out + term
        return out.astype(BF)

    def store(value, high, count, at, low):
        for k in range(value.shape[0] // count):
            slot = info[2 + at * (value.shape[0] // count) + k]
            piece = value[k * count : (k + 1) * count]
            if len(outs) == nb:
                for mine, out in enumerate(outs):

                    @pl.when(slot == mine)
                    def _():
                        out[0, low : low + count] = piece

            else:
                outs[0 if high else 1][slot] = piece

    @pl.when(step < steps)
    def _():
        store(total(activs, cots, True), False, units, step, rows)

    @pl.when(step >= steps)
    def _():
        store(total(grads, seconds, False), True, rows, step - steps, 0)


def feed_grad_call(info, activs, cots, seconds, grads, nb, live):
    ns = len(cots)
    dim = cots[0].shape[1]
    ff = activs[0].shape[1]
    rows, units = dim // nb, ff // nb
    tile = 512
    steps = ff // tile
    tok = ns * cots[0].shape[0]
    left = lambda a: pl.BlockSpec((a.shape[0], tile), lambda i, info: (0, jnp.minimum(i, steps - 1)))
    right = lambda a: pl.BlockSpec((a.shape[0], tile), lambda i, info: (0, jnp.maximum(i - steps, 0)))
    fixed = lambda a: once(a.shape)
    shapes = [(1, rows + units, dim)] * nb if live else [(nb, rows, ff), (nb, units, dim)]
    return pl.pallas_call(
        functools.partial(feed_grad_kernel, ns, nb, rows, units, steps),
        grid_spec=pltpu.PrefetchScalarGridSpec(
            num_scalar_prefetch=1,
            grid=(steps + dim // tile,),
            in_specs=[left(a) for a in activs]
            + [fixed(a) for a in cots]
            + [right(a) for a in seconds]
            + [fixed(a) for a in grads],
            out_specs=[once(shape) for shape in shapes],
        ),
        out_shape=[jax.ShapeDtypeStruct(shape, BF) for shape in shapes],
        compiler_params=params(60),
        cost_estimate=cost(4 * tok * dim * ff, 4 * tok * (dim + ff) + 4 * dim * ff),
        name="feed_grad",
    )(info, *activs, *cots, *seconds, *grads)


def pair_shapes(shape, ns):
    return [shape, shape, (2, *shape)] if ns == 4 else [shape] * ns


def pair_put(outs, ns, rel, rows, value):
    if ns == 4 and rel % 2:
        outs[2][rel // 2, rows] = value
    elif ns == 4:
        outs[rel // 2][rows] = value
    else:
        outs[rel][rows] = value


def split_grad_kernel(ns, info, left, right, *refs):
    outs, held = refs[:-1], refs[-1]
    held[...] = dg(left[...], right[...], TN)
    tile = held.shape[0]
    cw = held.shape[1] // ns
    rows = pl.ds(pl.multiple_of(pl.program_id(0) * tile, tile), tile)
    for rel in range(ns):
        col = pl.ds(pl.multiple_of((info[0] ^ rel) * cw, cw), cw)
        pair_put(outs, ns, rel, rows, held[:, col].astype(BF))


def split_grad(info, left, right, ns):
    tok, dim = left.shape
    tile = 256
    shapes = pair_shapes((dim, dim // ns), ns)
    return pl.pallas_call(
        functools.partial(split_grad_kernel, ns),
        grid_spec=pltpu.PrefetchScalarGridSpec(
            num_scalar_prefetch=1,
            grid=(dim // tile,),
            in_specs=[pl.BlockSpec((tok, tile), lambda i, info: (0, i)), once((tok, dim))],
            out_specs=[once(shape) for shape in shapes],
            scratch_shapes=[pltpu.VMEM((tile, dim), F32)],
        ),
        out_shape=[jax.ShapeDtypeStruct(shape, BF) for shape in shapes],
        compiler_params=params(60),
        cost_estimate=cost(2 * tok * dim * dim, 6 * dim * dim),
        name="split_grad",
    )(info, left, right)


def joined_grad_kernel(nb, rows, np, terms, live, info, left, weight, vecs, *refs):
    others, refs = refs[:terms], refs[terms:]
    other = others[0][...].astype(F32)
    for term in others[1:]:
        other += term[...].astype(F32)
    other = other.astype(BF)
    smalls, refs = (refs[:3], refs[3:]) if live else (refs[:1], refs[1:])
    right, sides, outs = refs[0], refs[1 : 1 + np], refs[1 + np :]
    total = dg(left[...], right[...], TN)
    tile, cw = other.shape
    cols = weight.shape[1]
    first = pl.program_id(0) * (tile // rows)
    low = total.astype(BF)
    weights = weight[...].astype(F32)
    moment = jnp.sum(total * weights, axis=1, keepdims=True)
    shift = jnp.sum(jnp.concatenate([side[...] for side in sides], 1) * weights, axis=1, keepdims=True)
    moment = jnp.broadcast_to(moment, (tile, 128)).T[:1]
    shift = jnp.broadcast_to(shift, (tile, 128)).T[:1]
    gain = (moment - vecs[1:2] * shift) / vecs[0:1]
    row = lax.broadcasted_iota(jnp.int32, (16, tile), 0)
    held = jnp.zeros((16, tile), F32) if live else smalls[0][...]
    held = jnp.where(row == 0, gain, jnp.where(row == 1, shift, held))
    if live:
        turned = smalls[0][...]
        for at, source in ((4, 2), (5, 0), (6, 1), (11, 3)):
            held = jnp.where(row == at, turned[source : source + 1], held)
        held = jnp.where(row == 7 + info[0], smalls[1][...] + smalls[2][...], held)
        for part in range(2):
            pieces = []
            for side in sides:
                base = part * 3 * HD
                pieces += [side[:, base : base + HD], side[:, base + 2 * HD : base + 3 * HD]]
            bias = jnp.where(pl.program_id(0) == info[0], jnp.concatenate(pieces, 1), 0.0)
            held = jnp.where(row == 2 + part, bias, held)
    held = held.astype(BF)
    for k in range(tile // rows):
        slot = info[2 + first + k]
        high = slice(k * rows, (k + 1) * rows)
        put(outs, slot, low[high], slice(0, rows), slice(0, cols))
        put(outs, slot, other[high], slice(0, rows), slice(cols, cols + cw))
        put(outs, slot, held[:, high], slice(rows, rows + 16), slice(0, rows))


def joined_grad_call(info, left, right, sides, others, weight, vecs, shares, turned, biases, nb, live):
    count, dim = left.shape
    cols = weight.shape[1]
    cw = others[0].shape[1]
    rows = dim // nb
    tile = 256
    wide = (rows + 16, cols + cw)
    shapes = [(1, *wide)] * nb if live else [(nb, *wide)]
    flat = lambda width: pl.BlockSpec((tile, width), lambda i, info: (i, 0))
    first = lambda width: pl.BlockSpec((None, tile, width), lambda i, info: (0, i, 0))
    tall = lambda value: pl.BlockSpec((value.shape[0], tile), lambda i, info: (0, i))
    smalls = (turned, *biases) if live else (shares,)
    return pl.pallas_call(
        functools.partial(joined_grad_kernel, nb, rows, len(sides), len(others), live),
        grid_spec=pltpu.PrefetchScalarGridSpec(
            num_scalar_prefetch=1,
            grid=(dim // tile,),
            in_specs=[pl.BlockSpec((count, tile), lambda i, info: (0, i)), flat(cols), tall(vecs)]
            + [first(cw) if term.ndim == 3 else flat(cw) for term in others]
            + [tall(value) for value in smalls]
            + [once(value.shape) for value in (right, *sides)],
            out_specs=[once(shape) for shape in shapes],
        ),
        out_shape=[jax.ShapeDtypeStruct(shape, BF) for shape in shapes],
        compiler_params=params(60),
        cost_estimate=cost(2 * count * dim * cols, 2 * count * (dim + cols) + 4 * dim * dim),
        name="joined_grad",
    )(info, left, weight, vecs, *others, *smalls, right, *sides)


def turn_kernel(ns, np, cw, info, ga, gb, gc, resid, cot, vecs, full, resid_grad, branch, *refs):
    mixed_grads, sums, held = refs[: ns * np], refs[ns * np], refs[ns * np + 1]

    @pl.when(pl.program_id(0) == 0)
    def _():
        sums[...] = jnp.zeros_like(sums)

    grad = ga[...].astype(F32) + gb[...].astype(F32) + gc[...].astype(F32)
    unit, scale = norm_parts(resid[...])
    outer = cot[...].astype(F32)
    value = outer + norm_back(grad, unit, scale, vecs[5:6])
    resid_grad[...] = value
    low = value.astype(BF)
    branch[...] = low
    held[...] = dg(low, full[...], NT).astype(BF)
    pw = cw // np
    for pair in range(np):
        for rel in range(ns):
            col = pl.ds(pl.multiple_of((info[0] ^ rel) * cw + pair * pw, pw), pw)
            mixed_grads[pair * ns + rel][...] = held[:, col]
    for at, term in enumerate((grad * unit, grad, low.astype(F32), outer)):
        sums[at : at + 1] += jnp.sum(term, axis=0, keepdims=True)


def turn_call(info, terms, resid, cot, vecs, full, ns, np):
    tok, dim = resid.shape
    cw = dim // ns
    tile = min(256, tok)
    part = pl.BlockSpec((tile, dim), lambda i, info: (i, 0))
    return pl.pallas_call(
        functools.partial(turn_kernel, ns, np, cw),
        grid_spec=pltpu.PrefetchScalarGridSpec(
            num_scalar_prefetch=1,
            grid=(tok // tile,),
            in_specs=[part, part, part, part, part, once(vecs.shape), once(full.shape)],
            out_specs=[part, part]
            + [pl.BlockSpec((tile, cw // np), lambda i, info: (i, 0))] * (ns * np)
            + [pl.BlockSpec((8, dim), lambda i, info: (0, 0))],
            scratch_shapes=[pltpu.VMEM((tile, dim), BF)],
        ),
        out_shape=[
            jax.ShapeDtypeStruct((tok, dim), F32),
            jax.ShapeDtypeStruct((tok, dim), BF),
        ]
        + [jax.ShapeDtypeStruct((tok, cw // np), BF)] * (ns * np)
        + [jax.ShapeDtypeStruct((8, dim), F32)],
        compiler_params=params(60),
        cost_estimate=cost(2 * tok * dim * dim, 16 * tok * dim + 2 * dim * dim),
        name="turn",
    )(info, *terms, resid, cot, vecs, full)


def last_kernel(ns, info, weight, right, *outs):
    step = pl.program_id(0)
    low = dg(right[...], weight[...], NT).astype(BF)
    for rel in range(ns):

        @pl.when(ns - 1 - step == rel)
        def _():
            if ns == 4 and rel % 2:
                outs[2][0] = low
            else:
                outs[rel // 2 if ns == 4 else rel][...] = low


def last_call(info, right, weight, ns):
    count = right.shape[0]
    dim, cols = weight.shape
    tok = count // ns
    shapes = pair_shapes((tok, dim), ns)
    specs = [pl.BlockSpec((tok, dim), lambda i, info: (0, 0))] * ns
    if ns == 4:
        specs[2:] = [pl.BlockSpec((1, tok, dim), lambda i, info: (jnp.where(i < 2, 1, 0), 0, 0))]
    return pl.pallas_call(
        functools.partial(last_kernel, ns),
        grid_spec=pltpu.PrefetchScalarGridSpec(
            num_scalar_prefetch=1,
            grid=(ns,),
            in_specs=[
                once(weight.shape),
                pl.BlockSpec((tok, cols), lambda i, info: (info[0] ^ (ns - 1 - i), 0)),
            ],
            out_specs=specs,
        ),
        out_shape=[jax.ShapeDtypeStruct(shape, BF) for shape in shapes],
        compiler_params=params(60),
        cost_estimate=cost(2 * count * dim * cols, 2 * count * (2 * dim + cols)),
        name="last",
    )(info, weight, right)


def end_kernel(ga, gb, gc, x, resid_grad, vecs, out):
    grad = ga[...].astype(F32) + gb[...].astype(F32) + gc[...].astype(F32)
    unit, scale = norm_parts(x[...].astype(F32))
    out[...] = resid_grad[...] + norm_back(grad, unit, scale, vecs[0:1])


def end_call(terms, x, resid_grad, vecs):
    tok, dim = x.shape
    tile = min(128, tok)
    part = pl.BlockSpec((tile, dim), lambda i: (i, 0))
    head = pl.BlockSpec((None, tile, dim), lambda i: (0, i, 0))
    return pl.pallas_call(
        end_kernel,
        grid=(tok // tile,),
        in_specs=[head if term.ndim == 3 else part for term in terms]
        + [part, part, pl.BlockSpec(vecs.shape, lambda i: (0, 0))],
        out_specs=part,
        out_shape=jax.ShapeDtypeStruct((tok, dim), F32),
        compiler_params=params(40),
        cost_estimate=cost(20 * tok * dim, 14 * tok * dim),
        name="end",
    )(*terms, x, resid_grad, vecs)


def add_pairs_kernel(count, *refs):
    for at in range(count):
        left, right, out = refs[at], refs[count + at], refs[2 * count + at]
        out[...] = (left[...].astype(F32) + right[...].astype(F32)).astype(BF)


def add_pairs(lefts, rights):
    count = len(lefts)
    return pl.pallas_call(
        functools.partial(add_pairs_kernel, count),
        in_specs=[pl.BlockSpec(memory_space=pltpu.VMEM)] * (2 * count),
        out_specs=[pl.BlockSpec(memory_space=pltpu.VMEM)] * count,
        out_shape=[jax.ShapeDtypeStruct(left.shape, BF) for left in lefts],
        compiler_params=params(20),
        cost_estimate=cost(1, 1),
        name="add_pairs",
    )(*lefts, *rights)


def joined_out_kernel(ns, cols, info, *refs):
    parts, joined, outw, smalls = refs[:ns], refs[ns], refs[ns + 1], refs[ns + 2 :]
    rows = joined.shape[0]
    cw = parts[0].shape[1] - cols
    total = None
    for rel in range(ns):
        part = parts[rel]
        joined[:, pl.ds(pl.multiple_of((info[0] ^ rel) * cols, cols), cols)] = part[:rows, :cols].astype(F32)
        outw[:, pl.ds(pl.multiple_of((info[0] ^ rel) * cw, cw), cw)] = part[:rows, cols:].astype(F32)
        term = part[rows:, :rows].astype(F32)
        total = term if total is None else total + term
    at = 0
    for small in smalls:
        for row in range(small.shape[0]):
            small[row : row + 1] = total[at + row : at + row + 1]
        at += small.shape[0]


def joined_out(info, parts, cols):
    ns = len(parts)
    high, wide = parts[0].shape
    rows = high - 16
    shapes = [(rows, ns * cols), (rows, ns * (wide - cols))]
    shapes += [(count, rows) for count in (1, 1, 2, 1, 1, 1, 4, 1)]
    return pl.pallas_call(
        functools.partial(joined_out_kernel, ns, cols),
        grid_spec=pltpu.PrefetchScalarGridSpec(
            num_scalar_prefetch=1,
            grid=(1,),
            in_specs=[once(part.shape) for part in parts],
            out_specs=[once(shape) for shape in shapes],
        ),
        out_shape=[jax.ShapeDtypeStruct(shape, F32) for shape in shapes],
        compiler_params=params(60),
        cost_estimate=cost(0, 6 * ns * rows * wide),
        name="joined_out",
    )(info, *parts)


def feed_out_kernel(ns, nb, rows, units, info, *refs):
    parts, expand, shrink = refs[:ns], refs[ns], refs[ns + 1]
    for rel in range(ns):
        seat = info[0] ^ rel
        shrink[pl.ds(pl.multiple_of(seat * units, units), units)] = parts[rel][rows:].astype(F32)
        for k in range(nb):
            col = pl.ds(pl.multiple_of((k * ns + seat) * units, units), units)
            expand[:, col] = parts[rel][:rows, k * units : (k + 1) * units].astype(F32)


def feed_out(info, parts, nb, rows):
    ns = len(parts)
    high, dim = parts[0].shape
    units = high - rows
    shapes = [(rows, ns * units * nb), (ns * units, dim)]
    return pl.pallas_call(
        functools.partial(feed_out_kernel, ns, nb, rows, units),
        grid_spec=pltpu.PrefetchScalarGridSpec(
            num_scalar_prefetch=1,
            grid=(1,),
            in_specs=[once(part.shape) for part in parts],
            out_specs=[once(shape) for shape in shapes],
        ),
        out_shape=[jax.ShapeDtypeStruct(shape, F32) for shape in shapes],
        compiler_params=params(60),
        cost_estimate=cost(0, 6 * ns * high * dim),
        name="feed_out",
    )(info, *parts)


def body(
    layer_input,
    lengths,
    first_gain,
    first_shift,
    joined_weight,
    joined_bias,
    output_weight,
    output_bias,
    second_gain,
    second_shift,
    expand_weight,
    expand_bias,
    shrink_weight,
    shrink_bias,
    out_grad,
):
    ns = lax.axis_size("seq")
    nb = lax.axis_size("batch")
    si = lax.axis_index("seq")
    bi = lax.axis_index("batch")
    tok = layer_input.shape[1]
    dim = layer_input.shape[2]
    heads = H // ns
    np = heads // 2
    cols = 3 * HD * heads
    cw = HD * heads
    rows = dim // nb
    ff = expand_weight.shape[1] // ns
    units = ff // nb
    x = layer_input[0]
    cot = out_grad[0]
    live = ns == 4 and nb == 8
    ring = Ring(nb, bi, live)
    info = jnp.concatenate([jnp.stack([si, lengths[0]]), ring.table()]).astype(jnp.int32)
    head_ids = si * heads + jnp.arange(heads, dtype=jnp.int32) + 1
    slopes = 2.0 ** (-8.0 * head_ids.astype(F32) / H)

    smalls = (first_gain, first_shift, joined_bias, output_bias, second_gain, second_shift, expand_bias, shrink_bias)
    smalls = [small.reshape(-1, rows) for small in smalls]
    seat = si.reshape(1).astype(jnp.int32)
    one = first_pack(seat, joined_weight, output_weight, smalls, cols, cw)
    jbias = None

    def step(held, t):
        if t < ring.half:
            held[t] = ring.back(held[t - 1])
        held[nb - t] = ring.ahead(held[(nb - t + 1) % nb])

    if live:
        cot, one = tie(cot, one)
        ones = {0: one}
        step(ones, 1)
        half = tok // 2
        near = lax.ppermute(x, "seq", pairs(ns, 1))
        far_a = lax.ppermute(x[:half], "seq", pairs(ns, 2))
        expand_weight, shrink_weight, _ = tie(expand_weight, shrink_weight, one)
        two = second_pack(seat, expand_weight, shrink_weight, nb, ns)
        ones[1], ones[7], two, near, cot, x = tie(ones[1], ones[7], two, near, cot, x)
        step(ones, 2)
        far_b = lax.ppermute(x[half:], "seq", pairs(ns, 2))
        cots = {0: cot, 1: lax.ppermute(cot, "seq", pairs(ns, 1))}
        ones[2], ones[6], cots[1], far_a, cot = tie(ones[2], ones[6], cots[1], far_a, cot)
        step(ones, 3)
        far_c = lax.ppermute(far_a, "seq", pairs(ns, 1))
        ones[3], ones[5], far_b, far_c, cot = tie(ones[3], ones[5], far_b, far_c, cot)
        step(ones, 4)
        far_d = lax.ppermute(far_b, "seq", pairs(ns, 1))
        cots[2] = lax.ppermute(cot, "seq", pairs(ns, 2))
        xs = [x, near, far_a, far_b, far_c, far_d]
        ones[4], two = tie(ones[4], two)
        twos = {0: two}
        step(twos, 1)
        one_parts = [ones[slot][None] for slot in range(nb)]
    else:
        xs = gather_rel(x, "seq", ns)
        xs = [xs[rel] for rel in range(ns)]
        cots = gather_rel(cot, "seq", ns)
        one_parts = [lax.all_gather(one, "batch")]
        low = one_parts[0][:, rows + 2 : rows + 4, :rows].astype(F32).reshape(2 * dim)
        low = lax.dynamic_slice(low, (si * 2 * cw,), (2 * cw,)).reshape(heads, 2, HD)
        jbias = jnp.stack([low[:, 0], jnp.zeros_like(low[:, 0]), low[:, 1]], 1).reshape(1, cols)

    normed, joined, joined_full, outw_own, vecs = first_call(
        info, jbias, xs, one_parts, cols, live, ns
    )
    if live:
        joined, twos[1], twos[7] = tie(joined, twos[1], twos[7])
        step(twos, 2)
    if live:
        ebias = vecs
    else:
        ebias = vecs[7:11].reshape(4, nb, rows).transpose(1, 0, 2).reshape(nb, ns, units)
        ebias = lax.dynamic_slice(ebias, (0, si, 0), (nb, 1, units)).reshape(1, ff)
    outw_all = gather_rel(outw_own, "seq", ns)
    attended = None
    for pair in range(np):
        attended = attend(joined, info, slopes, pair, attended)
        if live and pair == 0:
            out, joined, twos[2], twos[6], outw_all[1], outw_all[2], cots[2] = tie(
                attended[0], joined, twos[2], twos[6], outw_all[1], outw_all[2], cots[2]
            )
            attended = (out, attended[1])
            step(twos, 3)
            outw_all[3] = lax.ppermute(outw_all[2], "seq", pairs(ns, 1))
    mixed, log_sums = attended
    if live:
        mixed, twos[3], twos[5], outw_all[3], cots[2] = tie(mixed, twos[3], twos[5], outw_all[3], cots[2])
        step(twos, 4)
        cots[3] = lax.ppermute(cots[2], "seq", pairs(ns, 1))
    merged_parts = []
    for rel in range(ns):
        block = lax.dynamic_slice(mixed, ((si ^ rel) * tok, 0), (tok, cw))
        merged_parts.append(lax.ppermute(block, "seq", pairs(ns, rel)) if rel else block)
    if live:
        cots[3], twos[4], *merged_parts = tie(cots[3], twos[4], *merged_parts)
    merged, resid, second, outw_full = middle_call(
        info, x, vecs, merged_parts, [outw_all[rel] for rel in range(ns)]
    )
    out_parts = {}
    back_parts = {}
    activs = []
    pre_grads = []
    bias_sums = []
    if live:
        seconds = {0: second, 2: lax.ppermute(second, "seq", pairs(ns, 2)), 1: lax.ppermute(second, "seq", pairs(ns, 1))}
        two_parts = [twos[slot][None] for slot in range(nb)]
    else:
        seconds = gather_rel(second, "seq", ns)
        expand_part = expand_weight.reshape(rows, nb, ns, units)
        expand_part = lax.dynamic_slice(expand_part, (0, 0, si, 0), (rows, nb, 1, units)).reshape(rows, ff)
        shrink_part = lax.dynamic_slice(shrink_weight, (si * units, 0), (units, dim))
        two_parts = [lax.all_gather(expand_part, "batch"), lax.all_gather(shrink_part, "batch")]
    for rel in range(0, ns, 2):
        activ, pre_grad, oa, ob, ba, bb, bgrad = feed_call(
            info, seconds[rel], seconds[rel + 1], cots[rel], cots[rel + 1], ebias, two_parts, rows, units, nb, live
        )
        if live and rel == 0:
            activ, ob, bb, seconds[2] = tie(activ, ob, bb, seconds[2])
            seconds[3] = lax.ppermute(seconds[2], "seq", pairs(ns, 1))
            seconds[2], seconds[3] = tie(seconds[2], seconds[3])
            near_back = lax.ppermute(bb, "seq", pairs(ns, 1))
            near_out = lax.ppermute(ob, "seq", pairs(ns, 1))
        activs.append(activ)
        pre_grads.append(pre_grad)
        bias_sums.append(bgrad)
        out_parts.update({rel: oa, rel + 1: ob})
        back_parts.update({rel: ba, rel + 1: bb})
    if live:
        back_parts[3], near_back, near_out = tie(back_parts[3], near_back, near_out)
        far_back = lax.ppermute(back_parts[3], "seq", pairs(ns, 1))
        far_back, out_far = tie(far_back, out_parts[3])
        (back_b,) = add_pairs((back_parts[2],), (far_back,))
        back_b = lax.ppermute(back_b, "seq", pairs(ns, 2))
        far_out = lax.ppermute(out_far, "seq", pairs(ns, 1))
    else:
        back_terms = (*scatter_rel(back_parts, "seq", ns, last=False), jnp.zeros((tok, dim), BF))
        out_a, out_b = scatter_rel(out_parts, "seq", ns, last=False)
    feed_stack = feed_grad_call(
        info,
        activs,
        [cots[rel] for rel in range(ns)],
        [seconds[rel] for rel in range(ns)],
        pre_grads,
        nb,
        live,
    )

    class Scatter:
        def __init__(self, parts):
            self.parts = [part[0] for part in parts]
            self.t = 0
            self.ahead = self.parts[ring.half]
            self.back = self.parts[ring.half + 1]

        def send(self):
            self.t += 1
            self.got_ahead = ring.ahead(self.ahead)
            self.got_back = ring.back(self.back) if self.t > 1 else None

        def take(self, *others):
            both = self.t > 1
            got = (self.got_ahead, self.got_back) if both else (self.got_ahead,)
            tied = tie(*got, *others)
            got, others = tied[: len(got)], tied[len(got) :]
            if self.t == ring.half:
                total = self.parts[0].astype(F32) + got[0].astype(F32) + got[1].astype(F32)
                return (total.astype(BF), *others)
            mine = self.parts[ring.half - self.t]
            if both:
                self.ahead, self.back = add_pairs((mine, self.parts[nb - ring.half + self.t]), got)
            else:
                (self.ahead,) = add_pairs((mine,), got)
            return others

    if live:
        feed_ring = Scatter(feed_stack)
        feed_ring.send()
        (out_b,) = add_pairs((out_parts[2],), (far_out,))
        back_b, out_b, _ = tie(back_b, out_b, feed_stack[0])
        back_terms = (back_parts[0], near_back, back_b)
    resid_grad, branch, *mixed_grads, turn_sums = turn_call(
        info, back_terms, resid, cot, vecs, outw_full, ns, 1
    )
    outw_parts = split_grad(info, merged, branch, ns)
    sides = []

    grads = [
        lax.ppermute(block, "seq", pairs(ns, rel)) if rel else block for rel, block in enumerate(mixed_grads)
    ]
    if live:
        grads[0], *outw_parts = tie(grads[0], *outw_parts)
        grads = feed_ring.take(*grads)
        *grads, feed_ring.ahead, outw_near, out_b = tie(*grads, feed_ring.ahead, outw_parts[2], out_b)
        out_b = lax.ppermute(out_b, "seq", pairs(ns, 2))
        feed_ring.send()
        outw_near = lax.ppermute(outw_near, "seq", pairs(ns, 1))
    joined_grad = None
    for pair in range(np):
        joined_grad, side = attend_back(joined, grads, mixed, log_sums, info, slopes, pair, joined_grad)
        sides.append(side)
        if live and pair == 0:
            joined_grad, outw_near = feed_ring.take(joined_grad, outw_near)
            outw_far = add16(outw_parts[1], outw_near[1])
            joined_grad, joined, feed_ring.ahead, feed_ring.back, outw_far = tie(
                joined_grad, joined, feed_ring.ahead, feed_ring.back, outw_far
            )
            feed_ring.send()
            outw_far = lax.ppermute(outw_far, "seq", pairs(ns, 2))
        elif live:
            joined_grad, outw_far, out_b = feed_ring.take(joined_grad, outw_far, out_b)

    if live:
        shares = None
        outw_share = (outw_parts[0], outw_near, outw_far)
        joined_grad, feed_ring.ahead, feed_ring.back = tie(joined_grad, feed_ring.ahead, feed_ring.back)
        feed_ring.send()
    else:
        spread_bias = lax.dynamic_update_slice(
            jnp.zeros((nb, ns, units), F32), sum(bias_sums).reshape(nb, 1, units), (0, si, 0)
        )
        spread_bias = spread_bias.reshape(nb, 4, rows).transpose(1, 0, 2).reshape(4, dim)
        side = jnp.concatenate(sides, 1).reshape(heads, 3, HD)
        side = jnp.stack([side[:, 0], side[:, 2]], 1).reshape(2 * cw)
        side = lax.dynamic_update_slice(jnp.zeros((2 * dim,), F32), side, (si * 2 * cw,))
        side = side.reshape(nb, 2, rows).transpose(1, 0, 2).reshape(2, dim)
        none = jnp.zeros((2, dim), F32)
        shares = [none, side, turn_sums[2:3], turn_sums[0:2], spread_bias, turn_sums[3:4], none, none]
        shares = jnp.concatenate(shares, 0)
        outw_share = (scatter_rel(dict(enumerate(outw_parts)), "seq", ns),)
    joined_stack = joined_grad_call(
        info, normed, joined_grad, sides, outw_share, joined_full, vecs, shares, turn_sums, bias_sums, nb, live
    )
    if live:
        feed_share, *joined_stack = feed_ring.take(*joined_stack)
        feed_share, *joined_stack = tie(feed_share, *joined_stack)
        feed_parts = {0: feed_share, 2: lax.ppermute(feed_share, "seq", pairs(ns, 2))}
        joined_ring = Scatter(joined_stack)
        joined_ring.send()
        joined_grad, _ = tie(joined_grad, joined_stack[0])
    normed_parts = last_call(info, joined_grad, joined_full, ns)

    def ordered(block):
        parts = gather_rel(block, "seq", ns)
        return [parts[rel] for rel in range(ns)]

    if live:
        sent, feed_parts[2] = joined_ring.take(normed_parts[2], feed_parts[2])
        joined_ring.ahead, sent = tie(joined_ring.ahead, sent)
        joined_ring.send()
        got = lax.ppermute(sent, "seq", pairs(ns, 1))
        far = add16(normed_parts[1], got[1])
        norm_b = lax.ppermute(far, "seq", pairs(ns, 2))
        (far,) = joined_ring.take(far)
        joined_ring.ahead, joined_ring.back, far = tie(joined_ring.ahead, joined_ring.back, far)
        joined_ring.send()
        out_b, out_parts[0], _ = tie(out_b, out_parts[0], far)
        out_terms = out_parts[0].astype(F32) + near_out.astype(F32) + out_b.astype(F32)
        layer_output = (resid + out_terms + vecs[11:12]).astype(BF)
        layer_output, feed_parts[0], feed_parts[2] = joined_ring.take(layer_output, feed_parts[0], feed_parts[2])
        joined_ring.ahead, joined_ring.back, feed_parts[0], feed_parts[2] = tie(
            joined_ring.ahead, joined_ring.back, feed_parts[0], feed_parts[2]
        )
        joined_ring.send()
        feed_parts[1] = lax.ppermute(feed_parts[0], "seq", pairs(ns, 1))
        feed_parts[3] = lax.ppermute(feed_parts[2], "seq", pairs(ns, 1))
        joined_share, norm_b, feed_parts[1], feed_parts[3] = joined_ring.take(norm_b, feed_parts[1], feed_parts[3])
        joined_share, norm_b, feed_parts[1] = tie(joined_share, norm_b, feed_parts[1])
        joined_parts = {0: joined_share, 2: lax.ppermute(joined_share, "seq", pairs(ns, 2))}
        joined_parts[1] = lax.ppermute(joined_share, "seq", pairs(ns, 1))
        expand_grad, shrink_grad = feed_out(info, [feed_parts[rel] for rel in range(ns)], nb, rows)
        input_grad = end_call((normed_parts[0], got, norm_b), x, resid_grad, vecs)
        joined_parts[2], joined_parts[1], input_grad, expand_grad, shrink_grad = tie(
            joined_parts[2], joined_parts[1], input_grad, expand_grad, shrink_grad
        )
        joined_parts[3] = lax.ppermute(joined_parts[2], "seq", pairs(ns, 1))
        joined_parts = [joined_parts[rel] for rel in range(ns)]
    else:
        layer_output = (resid + out_a.astype(F32) + out_b.astype(F32) + vecs[11:12]).astype(BF)
        norm_terms = scatter_rel(dict(enumerate(normed_parts)), "seq", ns, last=False)
        input_grad = end_call((*norm_terms, jnp.zeros((tok, dim), BF)), x, resid_grad, vecs)
        joined_share = lax.psum_scatter(joined_stack[0], "batch", scatter_dimension=0)
        expand_share = lax.psum_scatter(feed_stack[0], "batch", scatter_dimension=0)
        shrink_share = lax.psum_scatter(feed_stack[1], "batch", scatter_dimension=0)
        seats = jnp.arange(ns, dtype=jnp.int32) ^ si
        shrink_grad = jnp.take(jnp.stack(ordered(shrink_share)), seats, axis=0).astype(F32).reshape(ns * units, dim)
        expand_grad = jnp.take(jnp.stack(ordered(expand_share)), seats, axis=0).astype(F32)
        expand_grad = expand_grad.reshape(ns, rows, nb, units).transpose(1, 2, 0, 3).reshape(rows, ns * ff)
        joined_parts = ordered(joined_share)
    joined_wgrad, outw_grad, *small = joined_out(info, joined_parts, cols)
    small = [value.reshape(-1) for value in small]
    return (
        layer_output[None],
        input_grad[None],
        small[0],
        small[1],
        joined_wgrad,
        small[2],
        outw_grad,
        small[3],
        small[4],
        small[5],
        expand_grad,
        small[6],
        shrink_grad,
        small[7],
    )


def solution(mesh):
    row = P("batch")
    mat = P("batch", None)
    act = P("batch", "seq", None)
    return jax.shard_map(
        body,
        mesh=mesh,
        in_specs=(act, row, row, row, mat, row, mat, row, row, row, mat, row, mat, row, act),
        out_specs=(act, act, row, row, mat, row, mat, row, row, row, mat, row, mat, row),
        check_vma=False,
    )
```

```python
import functools

import jax
import jax.numpy as jnp
from jax import lax
from jax.experimental import pallas as pl
from jax.experimental.pallas import tpu as pltpu
from jax.sharding import PartitionSpec as P

H = 16
HD = 64
EPSILON = 1e-05
F32 = jnp.float32
BF = jnp.bfloat16
NT = (((1,), (1,)), ((), ()))
NN = (((1,), (0,)), ((), ()))
TN = (((0,), (0,)), ((), ()))
MIB = 2**20
SHRINK = 1000


def dg(left, right, dims):
    return lax.dot_general(left, right, dims, preferred_element_type=F32)


def params(limit=56):
    return pltpu.CompilerParams(vmem_limit_bytes=limit * MIB)


def cost(flops, moved, exps=0):
    return pl.CostEstimate(flops=flops // SHRINK, bytes_accessed=moved // SHRINK, transcendentals=exps // SHRINK)


def norm_parts(values):
    mean = jnp.mean(values, axis=-1, keepdims=True)
    centered = values - mean
    scale = lax.rsqrt(jnp.mean(centered * centered, axis=-1, keepdims=True) + EPSILON)
    return centered * scale, scale


def norm_back(grad, unit, scale, gain):
    scaled = grad * gain
    return scale * (
        scaled
        - jnp.mean(scaled, axis=-1, keepdims=True)
        - unit * jnp.mean(scaled * unit, axis=-1, keepdims=True)
    )


def pairs(size, bit):
    return [(i, i ^ bit) for i in range(size)]


def bits_low_last(size):
    bits = []
    bit = 2
    while bit < size:
        bits.append(bit)
        bit *= 2
    if size > 1:
        bits.append(1)
    return bits


def add16(left, right):
    return (left.astype(F32) + right.astype(F32)).astype(BF)


def gather_rel(block, axis, size):
    out = {0: block}
    for bit in bits_low_last(size):
        for rel in list(out):
            out[rel | bit] = lax.ppermute(out[rel], axis, pairs(size, bit))
    return out


def scatter_rel(parts, axis, size, last=True):
    parts = dict(parts)
    order = bits_low_last(size)[::-1]
    for bit in order:
        for rel in sorted(parts, reverse=True):
            if rel & bit:
                other = lax.ppermute(parts.pop(rel), axis, pairs(size, bit))
                if bit == order[-1] and not last:
                    return parts[0], other
                parts[rel ^ bit] = add16(parts[rel ^ bit], other)
    return parts[0]


def tie(*values):
    return lax.optimization_barrier(values)


class Ring:
    def __init__(self, size, index, live):
        self.size = size
        self.live = live
        order = list(range(0, size, 2)) + list(range(size - 1, 0, -2))
        self.forward = [(order[i], order[(i + 1) % size]) for i in range(size)]
        self.backward = [(b, a) for a, b in self.forward]
        count = jnp.arange(size, dtype=jnp.int32)
        place = lambda k: jnp.where(k % 2 == 0, k // 2, size - (k + 1) // 2)
        if self.live:
            self.slots = (place(count) - place(index) + size) % size
            seat = (place(index) + count) % size
            self.owners = jnp.where(seat < size // 2, 2 * seat, 2 * (size - seat) - 1)
        else:
            self.slots = count
            self.owners = count
        self.half = size // 2

    def table(self):
        return jnp.concatenate([self.slots, self.owners])

    def ahead(self, value):
        return lax.ppermute(value, "batch", self.forward)

    def back(self, value):
        return lax.ppermute(value, "batch", self.backward)


def owner_at(info, live, nb, slot):
    return info[2 + nb + slot] if live else slot


def put(outs, slot, value, rows, cols):
    if len(outs) == 1:
        outs[0][slot, rows, cols] = value
        return
    for at, out in enumerate(outs):

        @pl.when(slot == at)
        def _():
            out[0, rows, cols] = value


def blocks_of(refs):
    out = []
    for ref in refs:
        out += [(ref, at) for at in range(ref.shape[0])]
    return out


def once(shape):
    return pl.BlockSpec(shape, lambda i, *_: (0,) * len(shape), pipeline_mode=pl.Buffered(1))


def first_pack_kernel(info, joined, outw, *refs):
    smalls, out = refs[:-1], refs[-1]
    rows, cols = joined.shape
    out[:rows, :cols] = joined[...]
    out[:rows, cols:] = outw[...]
    pieces = [small[...].astype(F32) for small in smalls]
    count = sum(piece.shape[0] for piece in pieces)
    pieces.append(jnp.zeros((16 - count, rows), F32))
    out[rows:, :rows] = jnp.concatenate(pieces, 0).astype(BF)
    out[rows:, rows:] = jnp.zeros((16, out.shape[1] - rows), BF)


def first_pack(info, joined, outw, smalls, cols, cw):
    rows = joined.shape[0]
    shape = (rows + 16, cols + cw)
    return pl.pallas_call(
        first_pack_kernel,
        grid_spec=pltpu.PrefetchScalarGridSpec(
            num_scalar_prefetch=1,
            grid=(1,),
            in_specs=[
                pl.BlockSpec((rows, cols), lambda i, info: (0, info[0])),
                pl.BlockSpec((rows, cw), lambda i, info: (0, info[0])),
            ]
            + [once(small.shape) for small in smalls],
            out_specs=pl.BlockSpec(shape, lambda i, info: (0, 0)),
        ),
        out_shape=jax.ShapeDtypeStruct(shape, BF),
        compiler_params=params(60),
        name="first_pack",
    )(info, joined, outw, *smalls)


def second_pack_kernel(nb, ns, units, info, expand, shrink, out):
    rows = expand.shape[0]
    for k in range(nb):
        col = pl.ds(pl.multiple_of((k * ns + info[0]) * units, units), units)
        out[:rows, k * units : (k + 1) * units] = expand[:, col]
    out[rows:] = shrink[...]


def second_pack(info, expand, shrink, nb, ns):
    rows, wide = expand.shape
    dim = shrink.shape[1]
    units = shrink.shape[0] // ns
    return pl.pallas_call(
        functools.partial(second_pack_kernel, nb, ns, units),
        grid_spec=pltpu.PrefetchScalarGridSpec(
            num_scalar_prefetch=1,
            grid=(1,),
            in_specs=[
                pl.BlockSpec((rows, wide), lambda i, info: (0, 0)),
                pl.BlockSpec((units, dim), lambda i, info: (info[0], 0)),
            ],
            out_specs=pl.BlockSpec((rows + units, dim), lambda i, info: (0, 0)),
        ),
        out_shape=jax.ShapeDtypeStruct((rows + units, dim), BF),
        compiler_params=params(60),
        name="second_pack",
    )(info, expand, shrink)


def first_kernel(starts, nb, rows, cols, live, info, *refs):
    jbias_in, refs = (None, refs) if live else (refs[0], refs[1:])
    count = len(starts) - 1
    xs, weights = refs[:count], refs[count:-6]
    normed, joined, full, outw, vecs, jbias = refs[-6:]
    step = pl.program_id(0)

    @pl.when(step == 0)
    def _():
        for slot, (ref, at) in enumerate(blocks_of(weights)):
            high = owner_at(info, live, nb, slot) * rows
            high = pl.multiple_of(high, rows) if live else high
            full[pl.ds(high, rows)] = ref[at, :rows, :cols]
            outw[pl.ds(high, rows)] = ref[at, :rows, cols:]
            vecs[:, pl.ds(high, rows)] = ref[at, rows:, :rows].astype(F32)
        if live:
            heads = cols // (3 * HD)
            for head in range(heads):
                at = info[0] * heads + head
                col = pl.ds(pl.multiple_of(lax.div(at, 2) * rows, rows), rows)
                row = vecs[0:8, col][2 + head % 2 : 3 + head % 2]
                pieces = [row[:, :HD], jnp.zeros((1, HD), F32), row[:, HD:]]
                jbias[:, head * 3 * HD : (head + 1) * 3 * HD] = jnp.concatenate(pieces, 1)
        else:
            jbias[...] = jbias_in[...]

    for at in range(count):

        @pl.when((step >= starts[at]) & (step < starts[at + 1]))
        def _():
            unit, _ = norm_parts(xs[at][...].astype(F32))
            value = (unit * vecs[0:1] + vecs[1:2]).astype(BF)
            normed[...] = value
            joined[...] = (dg(value, full[...], NN) + jbias[...]).astype(BF)


def first_call(info, jbias, xs, weights, cols, live, ns):
    dim = xs[0].shape[1]
    tok = sum(piece.shape[0] for piece in xs) // ns
    nb = sum(weight.shape[0] for weight in weights)
    rows = dim // nb
    cw = weights[0].shape[2] - cols
    tile = min(256, tok)
    nt = tok // tile
    starts = [0]
    for piece in xs:
        starts.append(starts[-1] + piece.shape[0] // tile)
    extra = [] if live else [jbias]
    place = lambda i, info: ((info[0] ^ lax.div(i, nt)) * nt + lax.rem(i, nt), 0)

    def source(at):
        last = starts[at + 1] - starts[at] - 1
        return pl.BlockSpec((tile, dim), lambda i, info: (jnp.clip(i - starts[at], 0, last), 0))

    return pl.pallas_call(
        functools.partial(first_kernel, starts, nb, rows, cols, live),
        grid_spec=pltpu.PrefetchScalarGridSpec(
            num_scalar_prefetch=1,
            grid=(ns * nt,),
            in_specs=[once(value.shape) for value in extra]
            + [source(at) for at in range(len(xs))]
            + [once(weight.shape) for weight in weights],
            out_specs=[
                pl.BlockSpec((tile, dim), place),
                pl.BlockSpec((tile, cols), place),
                once((dim, cols)),
                once((dim, cw)),
                once((16, dim)),
            ],
            scratch_shapes=[pltpu.VMEM((1, cols), F32)],
        ),
        out_shape=[
            jax.ShapeDtypeStruct((ns * tok, dim), BF),
            jax.ShapeDtypeStruct((ns * tok, cols), BF),
            jax.ShapeDtypeStruct((dim, cols), BF),
            jax.ShapeDtypeStruct((dim, cw), BF),
            jax.ShapeDtypeStruct((16, dim), F32),
        ],
        compiler_params=params(60),
        cost_estimate=cost(2 * ns * tok * dim * cols, 2 * ns * tok * (2 * dim + cols)),
        name="first",
    )(info, *extra, *xs, *weights)


def three(value):
    high = value.astype(BF)
    rest = value - high.astype(F32)
    mid = rest.astype(BF)
    return high, mid, (rest - mid.astype(F32)).astype(BF)


def spread(lane, base, columns):
    for at, column in columns:
        base = jnp.where(lane == at, column.astype(F32), base)
    return base.astype(BF)


def key_extra(count, slope, length):
    lane = lax.broadcasted_iota(jnp.int32, (count, HD), 1)
    pos = lax.broadcasted_iota(jnp.int32, (count, HD), 0)
    high, mid, low = three(slope * pos.astype(F32))
    dead = jnp.where(pos < length, 0.0, -1e30)
    return spread(lane, jnp.where(lane < 7, 1.0, 0.0), [(0, high), (1, mid), (2, low), (3, dead)])


def attend_kernel(count, size, pair, info, slopes, joined, mixed, sums, keys):
    lane = lax.broadcasted_iota(jnp.int32, (size, HD), 1)
    ones = jnp.where(lane < 4, 1.0, 0.0).astype(BF)
    for hh in range(2):
        base = 3 * HD * hh
        extra = key_extra(count, slopes[2 * pair + hh], info[1])
        keys[hh] = jnp.concatenate([joined[:, base + HD : base + 2 * HD], extra], 1)
    query_at = lax.broadcasted_iota(jnp.int32, (size, size), 0)
    key_at = lax.broadcasted_iota(jnp.int32, (size, size), 1)
    for block in range(count // size):
        low = block * size
        high = low + size
        outs = []
        logs = []
        for hh in range(2):
            base = 3 * HD * hh
            query = (joined[low:high, base : base + HD].astype(F32) * 0.125).astype(BF)
            query = jnp.concatenate([query, ones], 1)
            near = jnp.where(key_at <= query_at, dg(query, keys[hh, low:high], NT), -1e30)
            top = jnp.max(near, axis=1, keepdims=True)
            if block:
                far = dg(query, keys[hh, 0:low], NT)
                top = jnp.maximum(top, jnp.max(far, axis=1, keepdims=True))
            near = jnp.exp(near - top)
            total = jnp.sum(near, axis=1, keepdims=True)
            acc = dg(near.astype(BF), joined[low:high, base + 2 * HD : base + 3 * HD], NN)
            if block:
                far = jnp.exp(far - top)
                total += jnp.sum(far, axis=1, keepdims=True)
                acc += dg(far.astype(BF), joined[0:low, base + 2 * HD : base + 3 * HD], NN)
            outs.append(acc / total)
            logs.append(jnp.broadcast_to(top + jnp.log(total), (size, HD)))
        mixed[low:high] = jnp.concatenate(outs, 1).astype(BF)
        sums[low:high] = jnp.concatenate(logs, 1)


def attend(joined, info, slopes, pair, held):
    count, width = joined.shape
    groups = width // (6 * HD)
    smem = pl.BlockSpec(memory_space=pltpu.SMEM)
    narrow = pl.BlockSpec((count, 2 * HD), lambda i: (0, pair))
    area = count * count
    extra = [] if held is None else list(held)

    def kernel(*refs):
        attend_kernel(count, min(512, count), pair, *refs[:3], *refs[3 + len(extra) :])

    return pl.pallas_call(
        kernel,
        grid=(1,),
        in_specs=[smem, smem, pl.BlockSpec((count, 6 * HD), lambda i: (0, pair))]
        + [pl.BlockSpec(memory_space=pl.ANY)] * len(extra),
        out_specs=[narrow, narrow],
        out_shape=[
            jax.ShapeDtypeStruct((count, groups * 2 * HD), BF),
            jax.ShapeDtypeStruct((count, groups * 2 * HD), F32),
        ],
        input_output_aliases={3: 0, 4: 1} if extra else {},
        scratch_shapes=[pltpu.VMEM((2, count, 2 * HD), BF)],
        compiler_params=params(48),
        cost_estimate=cost(area * 1024, 20 * count * HD, area),
        name="attend",
    )(info, slopes, joined, *extra)


def attend_back_kernel(count, size, ns, pair, info, slopes, joined, mixed, sums, *refs):
    pieces_in = refs[:ns]
    out, sides, keys, queries, values, grads, query_grad = refs[ns:]
    tok = count // ns
    lane = lax.broadcasted_iota(jnp.int32, (count, HD), 1)
    near_lane = lax.broadcasted_iota(jnp.int32, (tok, HD), 1)
    for hh in range(2):
        base = 3 * HD * hh
        half = slice(hh * HD, (hh + 1) * HD)
        extra = key_extra(count, slopes[2 * pair + hh], info[1])
        keys[hh] = jnp.concatenate([joined[:, base + HD : base + 2 * HD], extra], 1)
        query = (joined[:, base : base + HD].astype(F32) * 0.125).astype(BF)
        high, mid, low = three(-sums[:, half])
        extra = spread(lane, jnp.where(lane < 4, 1.0, 0.0), [(4, high), (5, mid), (6, low)])
        queries[hh] = jnp.concatenate([query, extra], 1)
        ones = jnp.where(lane < 3, 1.0, 0.0).astype(BF)
        values[hh] = jnp.concatenate([joined[:, base + 2 * HD : base + 3 * HD], ones], 1)
        for rel in range(ns):
            at = pl.ds(pl.multiple_of((info[0] ^ rel) * tok, tok), tok)
            part = pieces_in[rel][:, half]
            inner = jnp.sum(part.astype(F32) * mixed[at, half].astype(F32), axis=1, keepdims=True)
            high, mid, low = three(jnp.broadcast_to(-inner, (tok, HD)))
            extra = spread(near_lane, jnp.zeros((tok, HD), F32), [(0, high), (1, mid), (2, low)])
            grads[hh, at] = jnp.concatenate([part, extra], 1)
    key_at = lax.broadcasted_iota(jnp.int32, (size, size), 0)
    query_at = lax.broadcasted_iota(jnp.int32, (size, size), 1)
    blocks = count // size
    for j in range(blocks):
        ks = slice(j * size, (j + 1) * size)
        pieces = []
        for hh in range(2):
            key_sum = None
            for i in range(j, blocks):
                qs = slice(i * size, (i + 1) * size)
                probs = jnp.exp(dg(keys[hh, ks], queries[hh, qs], NT))
                if i == j:
                    probs = jnp.where(key_at <= query_at, probs, 0.0)
                slope = (probs * dg(values[hh, ks], grads[hh, qs], NT)).astype(BF)
                value_part = dg(probs.astype(BF), grads[hh, qs], NN)
                key_part = dg(slope, queries[hh, qs], NN)
                query_part = dg(keys[hh, ks], slope, TN)
                value_sum = value_part if key_sum is None else value_sum + value_part
                key_sum = key_part if key_sum is None else key_sum + key_part
                query_grad[hh, :, qs] = query_part if j == 0 else query_grad[hh, :, qs] + query_part
            pieces += [jnp.zeros((size, HD), F32), key_sum[:, :HD], value_sum[:, :HD]]
        out[ks] = jnp.concatenate(pieces, 1).astype(BF)
    for hh in range(2):
        base = 3 * HD * hh
        out[:, base : base + HD] = (query_grad[hh].T[:, :HD] * 0.125).astype(BF)
    sides[...] = jnp.sum(out[...].astype(F32), axis=0, keepdims=True)


def attend_back(joined, grads, mixed, sums, info, slopes, pair, held):
    count, width = joined.shape
    ns = len(grads)
    smem = pl.BlockSpec(memory_space=pltpu.SMEM)
    wide = pl.BlockSpec((count, 6 * HD), lambda i: (0, pair))
    narrow = pl.BlockSpec((count, 2 * HD), lambda i: (0, pair))
    piece = pl.BlockSpec((count // ns, 2 * HD), lambda i: (0, pair))
    area = count * count
    extra = [] if held is None else [held]

    def kernel(*refs):
        inputs, rest = refs[: 5 + ns], refs[5 + ns + len(extra) :]
        attend_back_kernel(count, min(512, count), ns, pair, *inputs, *rest)

    return pl.pallas_call(
        kernel,
        grid=(1,),
        in_specs=[smem, smem, wide, narrow, narrow]
        + [piece] * ns
        + [pl.BlockSpec(memory_space=pl.ANY)] * len(extra),
        out_specs=[wide, pl.BlockSpec((1, 6 * HD), lambda i: (0, 0))],
        out_shape=[jax.ShapeDtypeStruct((count, width), BF), jax.ShapeDtypeStruct((1, 6 * HD), F32)],
        input_output_aliases={5 + ns: 0} if extra else {},
        scratch_shapes=[pltpu.VMEM((2, count, 2 * HD), BF)] * 4 + [pltpu.VMEM((2, 2 * HD, count), F32)],
        compiler_params=params(48),
        cost_estimate=cost(area * 2560, 40 * count * HD, area),
        name="attend_back",
    )(info, slopes, joined, mixed, sums, *grads, *extra)


def middle_kernel(ns, np, info, x, vecs, *refs):
    mixed, weights = refs[: ns * np], refs[ns * np : ns * np + ns]
    merged, resid, second, full = refs[ns * np + ns :]
    cw = weights[0].shape[1]
    pw = cw // np

    @pl.when(pl.program_id(0) == 0)
    def _():
        for rel in range(ns):
            full[:, pl.ds(pl.multiple_of((info[0] ^ rel) * cw, cw), cw)] = weights[rel][...]

    for pair in range(np):
        for rel in range(ns):
            col = pl.ds(pl.multiple_of((info[0] ^ rel) * cw + pair * pw, pw), pw)
            merged[:, col] = mixed[pair * ns + rel][...]
    value = x[...].astype(F32) + dg(merged[...], full[...], NN) + vecs[4:5]
    resid[...] = value
    unit, _ = norm_parts(value)
    second[...] = (unit * vecs[5:6] + vecs[6:7]).astype(BF)


def middle_call(info, x, vecs, mixed, weights):
    tok, dim = x.shape
    ns = len(weights)
    np = len(mixed) // ns
    tile = min(256, tok)
    part = lambda width: pl.BlockSpec((tile, width), lambda i, info: (i, 0))
    return pl.pallas_call(
        functools.partial(middle_kernel, ns, np),
        grid_spec=pltpu.PrefetchScalarGridSpec(
            num_scalar_prefetch=1,
            grid=(tok // tile,),
            in_specs=[part(dim), once(vecs.shape)]
            + [part(block.shape[1]) for block in mixed]
            + [once(weight.shape) for weight in weights],
            out_specs=[part(dim), part(dim), part(dim), once((dim, dim))],
        ),
        out_shape=[
            jax.ShapeDtypeStruct((tok, dim), BF),
            jax.ShapeDtypeStruct((tok, dim), F32),
            jax.ShapeDtypeStruct((tok, dim), BF),
            jax.ShapeDtypeStruct((dim, dim), BF),
        ],
        compiler_params=params(60),
        cost_estimate=cost(2 * tok * dim * dim, 12 * tok * dim + 4 * dim * dim),
        name="middle",
    )(info, x, vecs, *mixed, *weights)


def feed_kernel(nt, nb, rows, units, live, info, sa, sb, ca, cb, ebias, *refs):
    weights = refs[:-9]
    activ, pre_grad, oa, ob, ba, bb, bgrad, wide, tall = refs[-9:]
    step = pl.program_id(0)
    bias = ebias[...]
    if live:
        row = lax.broadcasted_iota(jnp.int32, bias.shape, 0)
        bias = jnp.sum(jnp.where(row == 7 + info[0], bias, 0.0), axis=0, keepdims=True)

    @pl.when(step == 0)
    def _():
        blocks = blocks_of(weights)
        for slot in range(nb):
            owner = owner_at(info, live, nb, slot)
            high = pl.multiple_of(owner * rows, rows) if live else owner * rows
            deep = pl.multiple_of(owner * units, units) if live else owner * units
            if len(blocks) == nb:
                ref, at = blocks[slot]
                wide[pl.ds(high, rows)] = ref[at, :rows]
                tall[pl.ds(deep, units)] = ref[at, rows:]
            else:
                wide[pl.ds(high, rows)] = weights[0][slot]
                tall[pl.ds(deep, units)] = weights[1][slot]
        bgrad[...] = jnp.zeros_like(bgrad)

    def work(second, cot, out, back):
        pre = dg(second[...], wide[...], NN) + bias
        square = pre * pre
        bend = jnp.tanh(0.7978845608028654 * pre * (1.0 + 0.044715 * square))
        half = 0.5 + 0.5 * bend
        act = (pre * half).astype(BF)
        activ[...] = act
        out[...] = dg(act, tall[...], NN).astype(BF)
        steep = half + pre * (0.5 - 0.5 * bend * bend) * (0.7978845608028654 + 0.10703222440890037 * square)
        grad = (dg(cot[...], tall[...], NT) * steep).astype(BF)
        pre_grad[...] = grad
        bgrad[...] += jnp.sum(grad.astype(F32), axis=0, keepdims=True)
        back[...] = dg(grad, wide[...], NT).astype(BF)

    @pl.when(step < nt)
    def _():
        work(sa, ca, oa, ba)

    @pl.when(step >= nt)
    def _():
        work(sb, cb, ob, bb)


def feed_call(info, sa, sb, ca, cb, ebias, weights, rows, units, nb, live):
    tok, dim = sa.shape
    ff = ebias.shape[1]
    tile = min(256, tok)
    nt = tok // tile
    left = pl.BlockSpec((tile, dim), lambda i, info: (jnp.minimum(i, nt - 1), 0))
    right = pl.BlockSpec((tile, dim), lambda i, info: (jnp.maximum(i - nt, 0), 0))
    flat = pl.BlockSpec((tile, ff), lambda i, info: (i, 0))
    shape = jax.ShapeDtypeStruct((tok, dim), BF)
    return pl.pallas_call(
        functools.partial(feed_kernel, nt, nb, rows, units, live),
        grid_spec=pltpu.PrefetchScalarGridSpec(
            num_scalar_prefetch=1,
            grid=(2 * nt,),
            in_specs=[left, right, left, right, once(ebias.shape)] + [once(weight.shape) for weight in weights],
            out_specs=[flat, flat, left, right, left, right, pl.BlockSpec((1, ff), lambda i, info: (0, 0))],
            scratch_shapes=[pltpu.VMEM((dim, ff), BF), pltpu.VMEM((ff, dim), BF)],
        ),
        out_shape=[jax.ShapeDtypeStruct((2 * tok, ff), BF)] * 2
        + [shape] * 4
        + [jax.ShapeDtypeStruct((1, ff), F32)],
        compiler_params=params(60),
        cost_estimate=cost(16 * tok * dim * ff, 16 * tok * dim + 8 * dim * ff, 2 * tok * ff),
        name="feed",
    )(info, sa, sb, ca, cb, ebias, *weights)


def feed_grad_kernel(ns, nb, rows, units, steps, info, *refs):
    half = ns // 2
    activs, cots, seconds, grads = refs[:half], refs[half : half + ns], refs[half + ns : half + 2 * ns], refs[half + 2 * ns : 2 * half + 2 * ns]
    outs = refs[2 * half + 2 * ns :]
    step = pl.program_id(0)

    def total(wides, thins, wide_left):
        out = None
        for rel in range(ns):
            thin = thins[rel]
            tok = thin.shape[0]
            wide = wides[rel // 2][(rel % 2) * tok : (rel % 2 + 1) * tok]
            term = dg(wide, thin[...], TN) if wide_left else dg(thin[...], wide, TN)
            out = term if out is None else out + term
        return out.astype(BF)

    def store(value, high, count, at, low):
        for k in range(value.shape[0] // count):
            slot = info[2 + at * (value.shape[0] // count) + k]
            piece = value[k * count : (k + 1) * count]
            if len(outs) == nb:
                for mine, out in enumerate(outs):

                    @pl.when(slot == mine)
                    def _():
                        out[0, low : low + count] = piece

            else:
                outs[0 if high else 1][slot] = piece

    @pl.when(step < steps)
    def _():
        store(total(activs, cots, True), False, units, step, rows)

    @pl.when(step >= steps)
    def _():
        store(total(grads, seconds, False), True, rows, step - steps, 0)


def feed_grad_call(info, activs, cots, seconds, grads, nb, live):
    ns = len(cots)
    dim = cots[0].shape[1]
    ff = activs[0].shape[1]
    rows, units = dim // nb, ff // nb
    tile = 512
    steps = ff // tile
    tok = ns * cots[0].shape[0]
    left = lambda a: pl.BlockSpec((a.shape[0], tile), lambda i, info: (0, jnp.minimum(i, steps - 1)))
    right = lambda a: pl.BlockSpec((a.shape[0], tile), lambda i, info: (0, jnp.maximum(i - steps, 0)))
    fixed = lambda a: once(a.shape)
    shapes = [(1, rows + units, dim)] * nb if live else [(nb, rows, ff), (nb, units, dim)]
    return pl.pallas_call(
        functools.partial(feed_grad_kernel, ns, nb, rows, units, steps),
        grid_spec=pltpu.PrefetchScalarGridSpec(
            num_scalar_prefetch=1,
            grid=(steps + dim // tile,),
            in_specs=[left(a) for a in activs]
            + [fixed(a) for a in cots]
            + [right(a) for a in seconds]
            + [fixed(a) for a in grads],
            out_specs=[once(shape) for shape in shapes],
        ),
        out_shape=[jax.ShapeDtypeStruct(shape, BF) for shape in shapes],
        compiler_params=params(60),
        cost_estimate=cost(4 * tok * dim * ff, 4 * tok * (dim + ff) + 4 * dim * ff),
        name="feed_grad",
    )(info, *activs, *cots, *seconds, *grads)


def pair_shapes(shape, ns):
    return [shape, shape, (2, *shape)] if ns == 4 else [shape] * ns


def pair_put(outs, ns, rel, rows, value):
    if ns == 4 and rel % 2:
        outs[2][rel // 2, rows] = value
    elif ns == 4:
        outs[rel // 2][rows] = value
    else:
        outs[rel][rows] = value


def split_grad_kernel(ns, info, left, right, *refs):
    outs, held = refs[:-1], refs[-1]
    held[...] = dg(left[...], right[...], TN)
    tile = held.shape[0]
    cw = held.shape[1] // ns
    rows = pl.ds(pl.multiple_of(pl.program_id(0) * tile, tile), tile)
    for rel in range(ns):
        col = pl.ds(pl.multiple_of((info[0] ^ rel) * cw, cw), cw)
        pair_put(outs, ns, rel, rows, held[:, col].astype(BF))


def split_grad(info, left, right, ns):
    tok, dim = left.shape
    tile = 256
    shapes = pair_shapes((dim, dim // ns), ns)
    return pl.pallas_call(
        functools.partial(split_grad_kernel, ns),
        grid_spec=pltpu.PrefetchScalarGridSpec(
            num_scalar_prefetch=1,
            grid=(dim // tile,),
            in_specs=[pl.BlockSpec((tok, tile), lambda i, info: (0, i)), once((tok, dim))],
            out_specs=[once(shape) for shape in shapes],
            scratch_shapes=[pltpu.VMEM((tile, dim), F32)],
        ),
        out_shape=[jax.ShapeDtypeStruct(shape, BF) for shape in shapes],
        compiler_params=params(60),
        cost_estimate=cost(2 * tok * dim * dim, 6 * dim * dim),
        name="split_grad",
    )(info, left, right)


def joined_grad_kernel(nb, rows, np, terms, live, info, left, weight, vecs, *refs):
    others, refs = refs[:terms], refs[terms:]
    other = others[0][...].astype(F32)
    for term in others[1:]:
        other += term[...].astype(F32)
    other = other.astype(BF)
    smalls, refs = (refs[:3], refs[3:]) if live else (refs[:1], refs[1:])
    right, sides, outs = refs[0], refs[1 : 1 + np], refs[1 + np :]
    total = dg(left[...], right[...], TN)
    tile, cw = other.shape
    cols = weight.shape[1]
    first = pl.program_id(0) * (tile // rows)
    low = total.astype(BF)
    weights = weight[...].astype(F32)
    moment = jnp.sum(total * weights, axis=1, keepdims=True)
    shift = jnp.sum(jnp.concatenate([side[...] for side in sides], 1) * weights, axis=1, keepdims=True)
    moment = jnp.broadcast_to(moment, (tile, 128)).T[:1]
    shift = jnp.broadcast_to(shift, (tile, 128)).T[:1]
    gain = (moment - vecs[1:2] * shift) / vecs[0:1]
    row = lax.broadcasted_iota(jnp.int32, (16, tile), 0)
    held = jnp.zeros((16, tile), F32) if live else smalls[0][...]
    held = jnp.where(row == 0, gain, jnp.where(row == 1, shift, held))
    if live:
        turned = smalls[0][...]
        for at, source in ((4, 2), (5, 0), (6, 1), (11, 3)):
            held = jnp.where(row == at, turned[source : source + 1], held)
        held = jnp.where(row == 7 + info[0], smalls[1][...] + smalls[2][...], held)
        for part in range(2):
            pieces = []
            for side in sides:
                base = part * 3 * HD
                pieces += [side[:, base : base + HD], side[:, base + 2 * HD : base + 3 * HD]]
            bias = jnp.where(pl.program_id(0) == info[0], jnp.concatenate(pieces, 1), 0.0)
            held = jnp.where(row == 2 + part, bias, held)
    held = held.astype(BF)
    for k in range(tile // rows):
        slot = info[2 + first + k]
        high = slice(k * rows, (k + 1) * rows)
        put(outs, slot, low[high], slice(0, rows), slice(0, cols))
        put(outs, slot, other[high], slice(0, rows), slice(cols, cols + cw))
        put(outs, slot, held[:, high], slice(rows, rows + 16), slice(0, rows))


def joined_grad_call(info, left, right, sides, others, weight, vecs, shares, turned, biases, nb, live):
    count, dim = left.shape
    cols = weight.shape[1]
    cw = others[0].shape[1]
    rows = dim // nb
    tile = 256
    wide = (rows + 16, cols + cw)
    shapes = [(1, *wide)] * nb if live else [(nb, *wide)]
    flat = lambda width: pl.BlockSpec((tile, width), lambda i, info: (i, 0))
    first = lambda width: pl.BlockSpec((None, tile, width), lambda i, info: (0, i, 0))
    tall = lambda value: pl.BlockSpec((value.shape[0], tile), lambda i, info: (0, i))
    smalls = (turned, *biases) if live else (shares,)
    return pl.pallas_call(
        functools.partial(joined_grad_kernel, nb, rows, len(sides), len(others), live),
        grid_spec=pltpu.PrefetchScalarGridSpec(
            num_scalar_prefetch=1,
            grid=(dim // tile,),
            in_specs=[pl.BlockSpec((count, tile), lambda i, info: (0, i)), flat(cols), tall(vecs)]
            + [first(cw) if term.ndim == 3 else flat(cw) for term in others]
            + [tall(value) for value in smalls]
            + [once(value.shape) for value in (right, *sides)],
            out_specs=[once(shape) for shape in shapes],
        ),
        out_shape=[jax.ShapeDtypeStruct(shape, BF) for shape in shapes],
        compiler_params=params(60),
        cost_estimate=cost(2 * count * dim * cols, 2 * count * (dim + cols) + 4 * dim * dim),
        name="joined_grad",
    )(info, left, weight, vecs, *others, *smalls, right, *sides)


def turn_kernel(ns, np, cw, info, ga, gb, gc, resid, cot, vecs, full, resid_grad, branch, *refs):
    mixed_grads, sums, held = refs[: ns * np], refs[ns * np], refs[ns * np + 1]

    @pl.when(pl.program_id(0) == 0)
    def _():
        sums[...] = jnp.zeros_like(sums)

    grad = ga[...].astype(F32) + gb[...].astype(F32) + gc[...].astype(F32)
    unit, scale = norm_parts(resid[...])
    outer = cot[...].astype(F32)
    value = outer + norm_back(grad, unit, scale, vecs[5:6])
    resid_grad[...] = value
    low = value.astype(BF)
    branch[...] = low
    held[...] = dg(low, full[...], NT).astype(BF)
    pw = cw // np
    for pair in range(np):
        for rel in range(ns):
            col = pl.ds(pl.multiple_of((info[0] ^ rel) * cw + pair * pw, pw), pw)
            mixed_grads[pair * ns + rel][...] = held[:, col]
    for at, term in enumerate((grad * unit, grad, low.astype(F32), outer)):
        sums[at : at + 1] += jnp.sum(term, axis=0, keepdims=True)


def turn_call(info, terms, resid, cot, vecs, full, ns, np):
    tok, dim = resid.shape
    cw = dim // ns
    tile = min(256, tok)
    part = pl.BlockSpec((tile, dim), lambda i, info: (i, 0))
    return pl.pallas_call(
        functools.partial(turn_kernel, ns, np, cw),
        grid_spec=pltpu.PrefetchScalarGridSpec(
            num_scalar_prefetch=1,
            grid=(tok // tile,),
            in_specs=[part, part, part, part, part, once(vecs.shape), once(full.shape)],
            out_specs=[part, part]
            + [pl.BlockSpec((tile, cw // np), lambda i, info: (i, 0))] * (ns * np)
            + [pl.BlockSpec((8, dim), lambda i, info: (0, 0))],
            scratch_shapes=[pltpu.VMEM((tile, dim), BF)],
        ),
        out_shape=[
            jax.ShapeDtypeStruct((tok, dim), F32),
            jax.ShapeDtypeStruct((tok, dim), BF),
        ]
        + [jax.ShapeDtypeStruct((tok, cw // np), BF)] * (ns * np)
        + [jax.ShapeDtypeStruct((8, dim), F32)],
        compiler_params=params(60),
        cost_estimate=cost(2 * tok * dim * dim, 16 * tok * dim + 2 * dim * dim),
        name="turn",
    )(info, *terms, resid, cot, vecs, full)


def last_kernel(ns, info, weight, right, *outs):
    step = pl.program_id(0)
    low = dg(right[...], weight[...], NT).astype(BF)
    for rel in range(ns):

        @pl.when(ns - 1 - step == rel)
        def _():
            if ns == 4 and rel % 2:
                outs[2][0] = low
            else:
                outs[rel // 2 if ns == 4 else rel][...] = low


def last_call(info, right, weight, ns):
    count = right.shape[0]
    dim, cols = weight.shape
    tok = count // ns
    shapes = pair_shapes((tok, dim), ns)
    specs = [pl.BlockSpec((tok, dim), lambda i, info: (0, 0))] * ns
    if ns == 4:
        specs[2:] = [pl.BlockSpec((1, tok, dim), lambda i, info: (jnp.where(i < 2, 1, 0), 0, 0))]
    return pl.pallas_call(
        functools.partial(last_kernel, ns),
        grid_spec=pltpu.PrefetchScalarGridSpec(
            num_scalar_prefetch=1,
            grid=(ns,),
            in_specs=[
                once(weight.shape),
                pl.BlockSpec((tok, cols), lambda i, info: (info[0] ^ (ns - 1 - i), 0)),
            ],
            out_specs=specs,
        ),
        out_shape=[jax.ShapeDtypeStruct(shape, BF) for shape in shapes],
        compiler_params=params(60),
        cost_estimate=cost(2 * count * dim * cols, 2 * count * (2 * dim + cols)),
        name="last",
    )(info, weight, right)


def end_kernel(ga, gb, gc, x, resid_grad, vecs, out):
    grad = ga[...].astype(F32) + gb[...].astype(F32) + gc[...].astype(F32)
    unit, scale = norm_parts(x[...].astype(F32))
    out[...] = resid_grad[...] + norm_back(grad, unit, scale, vecs[0:1])


def end_call(terms, x, resid_grad, vecs):
    tok, dim = x.shape
    tile = min(128, tok)
    part = pl.BlockSpec((tile, dim), lambda i: (i, 0))
    head = pl.BlockSpec((None, tile, dim), lambda i: (0, i, 0))
    return pl.pallas_call(
        end_kernel,
        grid=(tok // tile,),
        in_specs=[head if term.ndim == 3 else part for term in terms]
        + [part, part, pl.BlockSpec(vecs.shape, lambda i: (0, 0))],
        out_specs=part,
        out_shape=jax.ShapeDtypeStruct((tok, dim), F32),
        compiler_params=params(40),
        cost_estimate=cost(20 * tok * dim, 14 * tok * dim),
        name="end",
    )(*terms, x, resid_grad, vecs)


def add_pairs_kernel(count, *refs):
    for at in range(count):
        left, right, out = refs[at], refs[count + at], refs[2 * count + at]
        out[...] = (left[...].astype(F32) + right[...].astype(F32)).astype(BF)


def add_pairs(lefts, rights):
    count = len(lefts)
    return pl.pallas_call(
        functools.partial(add_pairs_kernel, count),
        in_specs=[pl.BlockSpec(memory_space=pltpu.VMEM)] * (2 * count),
        out_specs=[pl.BlockSpec(memory_space=pltpu.VMEM)] * count,
        out_shape=[jax.ShapeDtypeStruct(left.shape, BF) for left in lefts],
        compiler_params=params(20),
        cost_estimate=cost(1, 1),
        name="add_pairs",
    )(*lefts, *rights)


def joined_out_kernel(ns, cols, info, *refs):
    parts, joined, outw, smalls = refs[:ns], refs[ns], refs[ns + 1], refs[ns + 2 :]
    rows = joined.shape[0]
    cw = parts[0].shape[1] - cols
    total = None
    for rel in range(ns):
        part = parts[rel]
        joined[:, pl.ds(pl.multiple_of((info[0] ^ rel) * cols, cols), cols)] = part[:rows, :cols].astype(F32)
        outw[:, pl.ds(pl.multiple_of((info[0] ^ rel) * cw, cw), cw)] = part[:rows, cols:].astype(F32)
        term = part[rows:, :rows].astype(F32)
        total = term if total is None else total + term
    at = 0
    for small in smalls:
        for row in range(small.shape[0]):
            small[row : row + 1] = total[at + row : at + row + 1]
        at += small.shape[0]


def joined_out(info, parts, cols):
    ns = len(parts)
    high, wide = parts[0].shape
    rows = high - 16
    shapes = [(rows, ns * cols), (rows, ns * (wide - cols))]
    shapes += [(count, rows) for count in (1, 1, 2, 1, 1, 1, 4, 1)]
    return pl.pallas_call(
        functools.partial(joined_out_kernel, ns, cols),
        grid_spec=pltpu.PrefetchScalarGridSpec(
            num_scalar_prefetch=1,
            grid=(1,),
            in_specs=[once(part.shape) for part in parts],
            out_specs=[once(shape) for shape in shapes],
        ),
        out_shape=[jax.ShapeDtypeStruct(shape, F32) for shape in shapes],
        compiler_params=params(60),
        cost_estimate=cost(0, 6 * ns * rows * wide),
        name="joined_out",
    )(info, *parts)


def feed_out_kernel(ns, nb, rows, units, info, *refs):
    parts, expand, shrink = refs[:ns], refs[ns], refs[ns + 1]
    for rel in range(ns):
        seat = info[0] ^ rel
        shrink[pl.ds(pl.multiple_of(seat * units, units), units)] = parts[rel][rows:].astype(F32)
        for k in range(nb):
            col = pl.ds(pl.multiple_of((k * ns + seat) * units, units), units)
            expand[:, col] = parts[rel][:rows, k * units : (k + 1) * units].astype(F32)


def feed_out(info, parts, nb, rows):
    ns = len(parts)
    high, dim = parts[0].shape
    units = high - rows
    shapes = [(rows, ns * units * nb), (ns * units, dim)]
    return pl.pallas_call(
        functools.partial(feed_out_kernel, ns, nb, rows, units),
        grid_spec=pltpu.PrefetchScalarGridSpec(
            num_scalar_prefetch=1,
            grid=(1,),
            in_specs=[once(part.shape) for part in parts],
            out_specs=[once(shape) for shape in shapes],
        ),
        out_shape=[jax.ShapeDtypeStruct(shape, F32) for shape in shapes],
        compiler_params=params(60),
        cost_estimate=cost(0, 6 * ns * high * dim),
        name="feed_out",
    )(info, *parts)


def body(
    layer_input,
    lengths,
    first_gain,
    first_shift,
    joined_weight,
    joined_bias,
    output_weight,
    output_bias,
    second_gain,
    second_shift,
    expand_weight,
    expand_bias,
    shrink_weight,
    shrink_bias,
    out_grad,
):
    ns = lax.axis_size("seq")
    nb = lax.axis_size("batch")
    si = lax.axis_index("seq")
    bi = lax.axis_index("batch")
    tok = layer_input.shape[1]
    dim = layer_input.shape[2]
    heads = H // ns
    np = heads // 2
    cols = 3 * HD * heads
    cw = HD * heads
    rows = dim // nb
    ff = expand_weight.shape[1] // ns
    units = ff // nb
    x = layer_input[0]
    cot = out_grad[0]
    live = ns == 4 and nb == 8
    ring = Ring(nb, bi, live)
    info = jnp.concatenate([jnp.stack([si, lengths[0]]), ring.table()]).astype(jnp.int32)
    head_ids = si * heads + jnp.arange(heads, dtype=jnp.int32) + 1
    slopes = 2.0 ** (-8.0 * head_ids.astype(F32) / H)

    smalls = (first_gain, first_shift, joined_bias, output_bias, second_gain, second_shift, expand_bias, shrink_bias)
    smalls = [small.reshape(-1, rows) for small in smalls]
    seat = si.reshape(1).astype(jnp.int32)
    one = first_pack(seat, joined_weight, output_weight, smalls, cols, cw)
    jbias = None

    def step(held, t):
        if t < ring.half:
            held[t] = ring.back(held[t - 1])
        held[nb - t] = ring.ahead(held[(nb - t + 1) % nb])

    if live:
        cot, one = tie(cot, one)
        ones = {0: one}
        step(ones, 1)
        half = tok // 2
        near = lax.ppermute(x, "seq", pairs(ns, 1))
        far_a = lax.ppermute(x[:half], "seq", pairs(ns, 2))
        expand_weight, shrink_weight, _ = tie(expand_weight, shrink_weight, one)
        two = second_pack(seat, expand_weight, shrink_weight, nb, ns)
        ones[1], ones[7], two, near, cot, x = tie(ones[1], ones[7], two, near, cot, x)
        step(ones, 2)
        far_b = lax.ppermute(x[half:], "seq", pairs(ns, 2))
        cots = {0: cot, 1: lax.ppermute(cot, "seq", pairs(ns, 1))}
        ones[2], ones[6], cots[1], far_a, cot = tie(ones[2], ones[6], cots[1], far_a, cot)
        step(ones, 3)
        far_c = lax.ppermute(far_a, "seq", pairs(ns, 1))
        ones[3], ones[5], far_b, far_c, cot = tie(ones[3], ones[5], far_b, far_c, cot)
        step(ones, 4)
        far_d = lax.ppermute(far_b, "seq", pairs(ns, 1))
        cots[2] = lax.ppermute(cot, "seq", pairs(ns, 2))
        xs = [x, near, far_a, far_b, far_c, far_d]
        ones[4], two = tie(ones[4], two)
        twos = {0: two}
        step(twos, 1)
        one_parts = [ones[slot][None] for slot in range(nb)]
    else:
        xs = gather_rel(x, "seq", ns)
        xs = [xs[rel] for rel in range(ns)]
        cots = gather_rel(cot, "seq", ns)
        one_parts = [lax.all_gather(one, "batch")]
        low = one_parts[0][:, rows + 2 : rows + 4, :rows].astype(F32).reshape(2 * dim)
        low = lax.dynamic_slice(low, (si * 2 * cw,), (2 * cw,)).reshape(heads, 2, HD)
        jbias = jnp.stack([low[:, 0], jnp.zeros_like(low[:, 0]), low[:, 1]], 1).reshape(1, cols)

    normed, joined, joined_full, outw_own, vecs = first_call(
        info, jbias, xs, one_parts, cols, live, ns
    )
    if live:
        joined, twos[1], twos[7] = tie(joined, twos[1], twos[7])
        step(twos, 2)
    if live:
        ebias = vecs
    else:
        ebias = vecs[7:11].reshape(4, nb, rows).transpose(1, 0, 2).reshape(nb, ns, units)
        ebias = lax.dynamic_slice(ebias, (0, si, 0), (nb, 1, units)).reshape(1, ff)
    outw_all = gather_rel(outw_own, "seq", ns)
    attended = None
    for pair in range(np):
        attended = attend(joined, info, slopes, pair, attended)
        if live and pair == 0:
            out, joined, twos[2], twos[6], outw_all[1], outw_all[2], cots[2] = tie(
                attended[0], joined, twos[2], twos[6], outw_all[1], outw_all[2], cots[2]
            )
            attended = (out, attended[1])
            step(twos, 3)
            outw_all[3] = lax.ppermute(outw_all[2], "seq", pairs(ns, 1))
    mixed, log_sums = attended
    if live:
        mixed, twos[3], twos[5], outw_all[3], cots[2] = tie(mixed, twos[3], twos[5], outw_all[3], cots[2])
        step(twos, 4)
        cots[3] = lax.ppermute(cots[2], "seq", pairs(ns, 1))
    merged_parts = []
    for rel in range(ns):
        block = lax.dynamic_slice(mixed, ((si ^ rel) * tok, 0), (tok, cw))
        merged_parts.append(lax.ppermute(block, "seq", pairs(ns, rel)) if rel else block)
    if live:
        cots[3], twos[4], *merged_parts = tie(cots[3], twos[4], *merged_parts)
    merged, resid, second, outw_full = middle_call(
        info, x, vecs, merged_parts, [outw_all[rel] for rel in range(ns)]
    )
    out_parts = {}
    back_parts = {}
    activs = []
    pre_grads = []
    bias_sums = []
    if live:
        seconds = {0: second, 2: lax.ppermute(second, "seq", pairs(ns, 2)), 1: lax.ppermute(second, "seq", pairs(ns, 1))}
        two_parts = [twos[slot][None] for slot in range(nb)]
    else:
        seconds = gather_rel(second, "seq", ns)
        expand_part = expand_weight.reshape(rows, nb, ns, units)
        expand_part = lax.dynamic_slice(expand_part, (0, 0, si, 0), (rows, nb, 1, units)).reshape(rows, ff)
        shrink_part = lax.dynamic_slice(shrink_weight, (si * units, 0), (units, dim))
        two_parts = [lax.all_gather(expand_part, "batch"), lax.all_gather(shrink_part, "batch")]
    for rel in range(0, ns, 2):
        activ, pre_grad, oa, ob, ba, bb, bgrad = feed_call(
            info, seconds[rel], seconds[rel + 1], cots[rel], cots[rel + 1], ebias, two_parts, rows, units, nb, live
        )
        if live and rel == 0:
            activ, ob, bb, seconds[2] = tie(activ, ob, bb, seconds[2])
            seconds[3] = lax.ppermute(seconds[2], "seq", pairs(ns, 1))
            seconds[2], seconds[3] = tie(seconds[2], seconds[3])
            near_back = lax.ppermute(bb, "seq", pairs(ns, 1))
            near_out = lax.ppermute(ob, "seq", pairs(ns, 1))
        activs.append(activ)
        pre_grads.append(pre_grad)
        bias_sums.append(bgrad)
        out_parts.update({rel: oa, rel + 1: ob})
        back_parts.update({rel: ba, rel + 1: bb})
    if live:
        back_parts[3], near_back, near_out = tie(back_parts[3], near_back, near_out)
        far_back = lax.ppermute(back_parts[3], "seq", pairs(ns, 1))
        far_back, out_far = tie(far_back, out_parts[3])
        (back_b,) = add_pairs((back_parts[2],), (far_back,))
        back_b = lax.ppermute(back_b, "seq", pairs(ns, 2))
        far_out = lax.ppermute(out_far, "seq", pairs(ns, 1))
    else:
        back_terms = (*scatter_rel(back_parts, "seq", ns, last=False), jnp.zeros((tok, dim), BF))
        out_a, out_b = scatter_rel(out_parts, "seq", ns, last=False)
    feed_stack = feed_grad_call(
        info,
        activs,
        [cots[rel] for rel in range(ns)],
        [seconds[rel] for rel in range(ns)],
        pre_grads,
        nb,
        live,
    )

    class Scatter:
        def __init__(self, parts):
            self.parts = [part[0] for part in parts]
            self.t = 0
            self.ahead = self.parts[ring.half]
            self.back = self.parts[ring.half + 1]

        def send(self):
            self.t += 1
            self.got_ahead = ring.ahead(self.ahead)
            self.got_back = ring.back(self.back) if self.t > 1 else None

        def take(self, *others):
            both = self.t > 1
            got = (self.got_ahead, self.got_back) if both else (self.got_ahead,)
            tied = tie(*got, *others)
            got, others = tied[: len(got)], tied[len(got) :]
            if self.t == ring.half:
                total = self.parts[0].astype(F32) + got[0].astype(F32) + got[1].astype(F32)
                return (total.astype(BF), *others)
            mine = self.parts[ring.half - self.t]
            if both:
                self.ahead, self.back = add_pairs((mine, self.parts[nb - ring.half + self.t]), got)
            else:
                (self.ahead,) = add_pairs((mine,), got)
            return others

    if live:
        feed_ring = Scatter(feed_stack)
        feed_ring.send()
        (out_b,) = add_pairs((out_parts[2],), (far_out,))
        back_b, out_b, _ = tie(back_b, out_b, feed_stack[0])
        back_terms = (back_parts[0], near_back, back_b)
    resid_grad, branch, *mixed_grads, turn_sums = turn_call(
        info, back_terms, resid, cot, vecs, outw_full, ns, 1
    )
    outw_parts = split_grad(info, merged, branch, ns)
    sides = []

    grads = [
        lax.ppermute(block, "seq", pairs(ns, rel)) if rel else block for rel, block in enumerate(mixed_grads)
    ]
    if live:
        grads[0], *outw_parts = tie(grads[0], *outw_parts)
        grads = feed_ring.take(*grads)
        *grads, feed_ring.ahead, outw_near, out_b = tie(*grads, feed_ring.ahead, outw_parts[2], out_b)
        out_b = lax.ppermute(out_b, "seq", pairs(ns, 2))
        feed_ring.send()
        outw_near = lax.ppermute(outw_near, "seq", pairs(ns, 1))
    joined_grad = None
    for pair in range(np):
        joined_grad, side = attend_back(joined, grads, mixed, log_sums, info, slopes, pair, joined_grad)
        sides.append(side)
        if live and pair == 0:
            joined_grad, outw_near = feed_ring.take(joined_grad, outw_near)
            outw_far = add16(outw_parts[1], outw_near[1])
            joined_grad, joined, feed_ring.ahead, feed_ring.back, outw_far = tie(
                joined_grad, joined, feed_ring.ahead, feed_ring.back, outw_far
            )
            feed_ring.send()
            outw_far = lax.ppermute(outw_far, "seq", pairs(ns, 2))
        elif live:
            joined_grad, outw_far, out_b = feed_ring.take(joined_grad, outw_far, out_b)

    if live:
        shares = None
        outw_share = (outw_parts[0], outw_near, outw_far)
        joined_grad, feed_ring.ahead, feed_ring.back = tie(joined_grad, feed_ring.ahead, feed_ring.back)
        feed_ring.send()
    else:
        spread_bias = lax.dynamic_update_slice(
            jnp.zeros((nb, ns, units), F32), sum(bias_sums).reshape(nb, 1, units), (0, si, 0)
        )
        spread_bias = spread_bias.reshape(nb, 4, rows).transpose(1, 0, 2).reshape(4, dim)
        side = jnp.concatenate(sides, 1).reshape(heads, 3, HD)
        side = jnp.stack([side[:, 0], side[:, 2]], 1).reshape(2 * cw)
        side = lax.dynamic_update_slice(jnp.zeros((2 * dim,), F32), side, (si * 2 * cw,))
        side = side.reshape(nb, 2, rows).transpose(1, 0, 2).reshape(2, dim)
        none = jnp.zeros((2, dim), F32)
        shares = [none, side, turn_sums[2:3], turn_sums[0:2], spread_bias, turn_sums[3:4], none, none]
        shares = jnp.concatenate(shares, 0)
        outw_share = (scatter_rel(dict(enumerate(outw_parts)), "seq", ns),)
    joined_stack = joined_grad_call(
        info, normed, joined_grad, sides, outw_share, joined_full, vecs, shares, turn_sums, bias_sums, nb, live
    )
    if live:
        feed_share, *joined_stack = feed_ring.take(*joined_stack)
        feed_share, *joined_stack = tie(feed_share, *joined_stack)
        feed_parts = {0: feed_share, 2: lax.ppermute(feed_share, "seq", pairs(ns, 2))}
        joined_ring = Scatter(joined_stack)
        joined_ring.send()
        joined_grad, _ = tie(joined_grad, joined_stack[0])
    normed_parts = last_call(info, joined_grad, joined_full, ns)

    def ordered(block):
        parts = gather_rel(block, "seq", ns)
        return [parts[rel] for rel in range(ns)]

    if live:
        sent, feed_parts[2] = joined_ring.take(normed_parts[2], feed_parts[2])
        joined_ring.ahead, sent = tie(joined_ring.ahead, sent)
        joined_ring.send()
        got = lax.ppermute(sent, "seq", pairs(ns, 1))
        far = add16(normed_parts[1], got[1])
        norm_b = lax.ppermute(far, "seq", pairs(ns, 2))
        (far,) = joined_ring.take(far)
        joined_ring.ahead, joined_ring.back, far = tie(joined_ring.ahead, joined_ring.back, far)
        joined_ring.send()
        out_b, out_parts[0], _ = tie(out_b, out_parts[0], far)
        out_terms = out_parts[0].astype(F32) + near_out.astype(F32) + out_b.astype(F32)
        layer_output = (resid + out_terms + vecs[11:12]).astype(BF)
        layer_output, feed_parts[0], feed_parts[2] = joined_ring.take(layer_output, feed_parts[0], feed_parts[2])
        joined_ring.ahead, joined_ring.back, feed_parts[0], feed_parts[2] = tie(
            joined_ring.ahead, joined_ring.back, feed_parts[0], feed_parts[2]
        )
        joined_ring.send()
        feed_parts[1] = lax.ppermute(feed_parts[0], "seq", pairs(ns, 1))
        feed_parts[3] = lax.ppermute(feed_parts[2], "seq", pairs(ns, 1))
        joined_share, norm_b, feed_parts[1], feed_parts[3] = joined_ring.take(norm_b, feed_parts[1], feed_parts[3])
        joined_share, norm_b, feed_parts[1] = tie(joined_share, norm_b, feed_parts[1])
        joined_parts = {0: joined_share, 2: lax.ppermute(joined_share, "seq", pairs(ns, 2))}
        joined_parts[1] = lax.ppermute(joined_share, "seq", pairs(ns, 1))
        expand_grad, shrink_grad = feed_out(info, [feed_parts[rel] for rel in range(ns)], nb, rows)
        input_grad = end_call((normed_parts[0], got, norm_b), x, resid_grad, vecs)
        joined_parts[2], joined_parts[1], input_grad, expand_grad, shrink_grad = tie(
            joined_parts[2], joined_parts[1], input_grad, expand_grad, shrink_grad
        )
        joined_parts[3] = lax.ppermute(joined_parts[2], "seq", pairs(ns, 1))
        joined_parts = [joined_parts[rel] for rel in range(ns)]
    else:
        layer_output = (resid + out_a.astype(F32) + out_b.astype(F32) + vecs[11:12]).astype(BF)
        norm_terms = scatter_rel(dict(enumerate(normed_parts)), "seq", ns, last=False)
        input_grad = end_call((*norm_terms, jnp.zeros((tok, dim), BF)), x, resid_grad, vecs)
        joined_share = lax.psum_scatter(joined_stack[0], "batch", scatter_dimension=0)
        expand_share = lax.psum_scatter(feed_stack[0], "batch", scatter_dimension=0)
        shrink_share = lax.psum_scatter(feed_stack[1], "batch", scatter_dimension=0)
        seats = jnp.arange(ns, dtype=jnp.int32) ^ si
        shrink_grad = jnp.take(jnp.stack(ordered(shrink_share)), seats, axis=0).astype(F32).reshape(ns * units, dim)
        expand_grad = jnp.take(jnp.stack(ordered(expand_share)), seats, axis=0).astype(F32)
        expand_grad = expand_grad.reshape(ns, rows, nb, units).transpose(1, 2, 0, 3).reshape(rows, ns * ff)
        joined_parts = ordered(joined_share)
    joined_wgrad, outw_grad, *small = joined_out(info, joined_parts, cols)
    small = [value.reshape(-1) for value in small]
    return (
        layer_output[None],
        input_grad[None],
        small[0],
        small[1],
        joined_wgrad,
        small[2],
        outw_grad,
        small[3],
        small[4],
        small[5],
        expand_grad,
        small[6],
        shrink_grad,
        small[7],
    )


def solution(mesh):
    row = P("batch")
    mat = P("batch", None)
    act = P("batch", "seq", None)
    return jax.shard_map(
        body,
        mesh=mesh,
        in_specs=(act, row, row, row, mat, row, mat, row, row, row, mat, row, mat, row, act),
        out_specs=(act, act, row, row, mat, row, mat, row, row, row, mat, row, mat, row),
        check_vma=False,
    )
```
